32 devices in a mesh: section: 2 (over core), dp: 4 (over z), seq: 4 (over y, x).
Axes of the slice: x: 2, y: 2, z: 4, core: 2. Of those that a mesh axis runs over, the one named last changes fastest.
Arguments:
- inputs: bfloat16 [8, 4096, 512], P('dp', 'seq'), may hold values from -8 to 8
- mask: int32 [8, 4096], P('dp', 'seq'), may hold values from 0 to 1, as said below
- norm_gain: float32 [2, 512], P('section'), may hold values from 0.5 to 1.5
- norm_bias: float32 [2, 512], P('section'), may hold values from -3 to 3
- nu_log: float32 [2, 256], P('section'), as said below
- theta_log: float32 [2, 256], P('section'), may hold values from -4.6 to -0.7
- w_in: bfloat16 [2, 512, 512], P('section'), may hold values from -0.1875 to 0.1875
- w_out: bfloat16 [2, 512, 512], P('section'), may hold values from -0.25 to 0.25
- skip_gain: float32 [2, 512], P('section'), may hold values from -3 to 3
- w_glu: bfloat16 [2, 512, 1024], P('section'), may hold values from -0.25 to 0.25
- b_glu: float32 [2, 1024], P('section'), may hold values from -2 to 2
- cotangent: bfloat16 [8, 4096, 512], P('dp', 'seq'), may hold values from -6 to 6
Outputs:
- activations: bfloat16 [2, 8, 4096, 512], P('section', 'dp', 'seq')
- input_grads: float32 [2, 8, 4096, 512], P('section', 'dp', 'seq')
- grad_norm_gain: float32 [2, 512], P('section')
- grad_norm_bias: float32 [2, 512], P('section')
- grad_nu_log: float32 [2, 256], P('section')
- grad_theta_log: float32 [2, 256], P('section')
- grad_w_in: float32 [2, 512, 512], P('section')
- grad_w_out: float32 [2, 512, 512], P('section')
- grad_skip_gain: float32 [2, 512], P('section')
- grad_w_glu: float32 [2, 512, 1024], P('section')
- grad_b_glu: float32 [2, 1024], P('section')
The draws below stay inside these ranges and needn't reach their ends.
Inputs may be any that keep to these rules, and one draw needn't show every extreme that they name: `mask`: each sequence is 1 on a prefix of at least 1024 steps and 0 after it; in each aligned group of 1 sequence one is 1 on more than 3072 steps. exp(nu_log) lies between 0.1 / 4096 and 1 / 30.
All inputs are finite; a program needn't handle non-finite values.
Results may differ from the reference program's by a relative error of at most 0.015.
Values may be sent and summed in bfloat16 or wider, within the bound.
A program may use at most 192 MiB of HBM per device.

```python
import math
import jax
import jax.numpy as jnp
from jax import lax

D = 512
STATES = 256
BLOCK = 64
MICRO = 2
SPAN = 1024
LENGTH = 4096
SEQS_MICRO = 1
SEQS = 8
N_DP = 4


def draw_inputs(key, part):
    key = jax.random.fold_in(key, 23)
    first, second = jax.random.split(key)
    ramp = (jnp.arange(LENGTH, dtype=jnp.float32) / LENGTH)[None, :, None]
    rise = (jnp.arange(SEQS, dtype=jnp.float32) / SEQS)[:, None, None]
    offset = 0.6 * jax.random.normal(first, (1, 1, D), jnp.float32)
    noise = jax.random.normal(second, (SEQS, LENGTH, D), jnp.float32)
    across = 0.6 + 1.2 * rise
    values = offset * (1.0 + 2.0 * ramp) + noise * (0.5 + ramp) * across
    return jnp.clip(values, -8.0, 8.0).astype(jnp.bfloat16)


def draw_mask(key, part):
    key = jax.random.fold_in(key, 11)
    first = jax.random.fold_in(key, 1)
    second = jax.random.fold_in(key, 2)
    third = jax.random.fold_in(key, 3)
    lengths = jax.random.randint(first, (SEQS,), LENGTH // 4, LENGTH + 1)
    chosen = jax.random.randint(second, (SEQS // SEQS_MICRO,), 0, SEQS_MICRO)
    longest = jax.random.randint(third, (SEQS,), LENGTH - SPAN + 1, LENGTH + 1)
    position = jnp.arange(SEQS) % SEQS_MICRO
    full = position == jnp.repeat(chosen, SEQS_MICRO)
    lengths = jnp.where(full, longest, lengths)
    return (jnp.arange(LENGTH)[None, :] < lengths[:, None]).astype(jnp.int32)


def draw_nu_log(key, part):
    key = jax.random.fold_in(key, 37)
    slowest = math.log(0.1 / LENGTH)
    fastest = math.log(1.0 / 30.0)
    return jax.random.uniform(key, (2, STATES), jnp.float32, slowest, fastest)


def levels(key, dims, shards, least, high):
    factor_of = 1.0
    for dim, blocks in shards:
        steps = jax.random.uniform(jax.random.fold_in(jax.random.fold_in(key, 6), dim), (blocks,), jnp.float32, least / len(shards), high / len(shards))
        factor_of = factor_of * jnp.repeat(jnp.exp(steps), dims[dim] // blocks).reshape((-1,) + (1,) * (len(dims) - 1 - dim))
    return factor_of


def scatter_about(rng, extent, scale, bound, shards=(), kind=jnp.bfloat16):
    values = scale * jax.random.normal(rng, extent, jnp.float32)
    if shards:
        values = values * levels(rng, extent, shards, -0.22, 0.18)
    return jnp.clip(values, -bound, bound).astype(kind)


def setup_inputs(seed: int = 0) -> dict:
    seeds = jax.random.split(jax.random.key(seed), 13)
    return {
        "inputs": draw_inputs(jax.random.fold_in(seeds[12], 71), 0),
        "mask": draw_mask(jax.random.fold_in(seeds[12], 71), 0),
        "norm_gain": jnp.clip(1.0 + 0.1 * jax.random.normal(seeds[2], (2, D), jnp.float32), 0.5, 1.5),
        "norm_bias": scatter_about(seeds[3], (2, D), 0.5, 3.0, ((0, 2),), jnp.float32),
        "nu_log": draw_nu_log(jax.random.fold_in(seeds[12], 71), 0),
        "theta_log": jnp.clip(-4.6 + 3.8999999 * jax.random.uniform(seeds[5], (2, STATES), jnp.float32) ** levels(seeds[5], (2, STATES), ((0, 2),), -0.2, 0.2), -4.6, -0.7),
        "w_in": scatter_about(seeds[6], (2, D, 2 * STATES), (2 * D) ** -0.5, 0.1875, ((0, 2),)),
        "w_out": scatter_about(seeds[7], (2, 2 * STATES, D), (2 * STATES) ** -0.5, 0.25, ((0, 2),)),
        "skip_gain": scatter_about(seeds[8], (2, D), 1.0, 3.0, ((0, 2),), jnp.float32),
        "w_glu": scatter_about(seeds[9], (2, D, 2 * D), D ** -0.5, 0.25, ((0, 2),)),
        "b_glu": scatter_about(seeds[10], (2, 2 * D), 0.3, 2.0, ((0, 2),), jnp.float32),
        "cotangent": scatter_about(seeds[11], (SEQS, LENGTH, D), 1.0, 6.0, ((0, 4), (1, 4))),
    }


EPS = 1e-05
HIGH = lax.Precision.HIGHEST

@jax.custom_vjp
def low(v):
    return lax.optimization_barrier(v.astype(jnp.bfloat16)).astype(jnp.float32)

@jax.custom_vjp
def low_back(v):
    return v

def low_keep(v):
    return (low(v), None)

def low_pass(kept, grad):
    return (grad,)

def back_keep(v):
    return (v, None)

def back_low(kept, grad):
    return (low(grad),)
low.defvjp(low_keep, low_pass)
low_back.defvjp(back_keep, back_low)

def coefficients(nu_log, theta_log):
    rate = jnp.exp(nu_log)
    phase = jnp.exp(theta_log)
    magnitude = jnp.exp(-rate)
    return (magnitude * jnp.cos(phase), magnitude * jnp.sin(phase), jnp.sqrt(-jnp.expm1(-2.0 * rate)))

def recurrence(drive_re, drive_im, decay_re, decay_im, backwards):
    batch, steps, width = drive_re.shape
    blocks = steps // BLOCK
    drive = (jnp.transpose(drive_re, (1, 0, 2)).reshape(blocks, BLOCK, batch, width), jnp.transpose(drive_im, (1, 0, 2)).reshape(blocks, BLOCK, batch, width))

    def one_step(state, inputs):
        state_re, state_im = state
        next_re = decay_re * state_re - decay_im * state_im + inputs[0]
        next_im = decay_im * state_re + decay_re * state_im + inputs[1]
        return ((next_re, next_im), (next_re, next_im))

    @jax.checkpoint
    def one_block(state, inputs):
        return lax.scan(one_step, state, inputs, reverse=backwards)
    start = (jnp.zeros((batch, width), jnp.float32), jnp.zeros((batch, width), jnp.float32))
    _, (states_re, states_im) = lax.scan(one_block, start, drive, reverse=backwards)
    states_re = jnp.transpose(states_re.reshape(steps, batch, width), (1, 0, 2))
    states_im = jnp.transpose(states_im.reshape(steps, batch, width), (1, 0, 2))
    return (states_re, states_im)

def lru_block(source, live, norm_gain, norm_bias, nu_log, theta_log, w_in, w_out, skip_gain, w_glu, b_glu, backwards):
    valid = jnp.sum(live)
    average = lax.optimization_barrier(jnp.sum(live * source, axis=(0, 1))) / valid
    variance = lax.optimization_barrier(jnp.sum(live * (source - average) ** 2, axis=(0, 1))) / valid
    normed = (source - average) * lax.rsqrt(variance + EPS)
    scaled = low(live * (norm_gain * normed + norm_bias))
    projected = low_back(jnp.dot(scaled, w_in, precision=HIGH))
    decay_re, decay_im, input_scale = coefficients(nu_log, theta_log)
    states_re, states_im = recurrence(input_scale * projected[..., :STATES], input_scale * projected[..., STATES:], decay_re, decay_im, backwards)
    readout = low(jnp.concatenate([states_re, states_im], -1))
    mixed = low_back(jnp.dot(readout, w_out, precision=HIGH) + skip_gain * scaled)
    active = low(jax.nn.gelu(mixed))
    gated = low_back(jnp.dot(active, w_glu, precision=HIGH) + b_glu)
    return source + live * (gated[..., :D] * jax.nn.sigmoid(gated[..., D:]))

def pick(array, index):
    shaped = array.reshape((N_DP, MICRO, SEQS_MICRO) + array.shape[1:])
    return shaped[:, index].reshape((N_DP * SEQS_MICRO,) + array.shape[1:])

def unpick(pieces):
    shaped = [piece.reshape((N_DP, SEQS_MICRO) + piece.shape[1:]) for piece in pieces]
    joined = jnp.stack(shaped, 1)
    return joined.reshape((N_DP * MICRO * SEQS_MICRO,) + joined.shape[3:])

def reference(inputs, mask, norm_gain, norm_bias, nu_log, theta_log, w_in, w_out, skip_gain, w_glu, b_glu, cotangent):
    params = tuple((weight.astype(jnp.float32) for weight in (norm_gain, norm_bias, nu_log, theta_log, w_in, w_out, skip_gain, w_glu, b_glu)))
    hiddens, finals, source_grads, probe_grads = ([], [], [], [])
    totals = tuple((jnp.zeros_like(weight) for weight in params))
    for index in range(MICRO):
        live = pick(mask, index).astype(jnp.float32)[..., None]
        source = pick(inputs, index).astype(jnp.float32)
        probe = jnp.zeros_like(source)

        def forward(first_in, added, weights):
            first = tuple((weight[0] for weight in weights))
            second = tuple((weight[1] for weight in weights))
            hidden = lru_block(live * first_in, live, *first, False)
            handed = low_back(low(hidden)) + added
            final = lru_block(handed, live, *second, True)
            return (final, hidden)
        final, back_fn, hidden = jax.vjp(forward, source, probe, params, has_aux=True)
        grad_source, grad_probe, grad_weights = back_fn(pick(cotangent, index).astype(jnp.float32))
        hiddens.append(hidden.astype(jnp.bfloat16))
        finals.append(final.astype(jnp.bfloat16))
        source_grads.append(grad_source)
        probe_grads.append(grad_probe)
        totals = tuple((total + grad for total, grad in zip(totals, grad_weights)))
    activations = jnp.stack([unpick(hiddens), unpick(finals)], 0)
    input_grads = jnp.stack([unpick(source_grads), unpick(probe_grads)], 0)
    return (activations, input_grads, totals[0], totals[1], totals[2], totals[3], totals[4], totals[5], totals[6], totals[7], totals[8])
```

```python
import functools
import math
import types

import jax
import jax.numpy as jnp
from jax import lax
from jax.experimental import pallas as pl
from jax.experimental.pallas import tpu as pltpu
from jax.sharding import PartitionSpec as P

D = 512
STATES = 256
MICRO = 2
EPS = 1e-05
LANES = 128
ROWS = 256
SEG = 32
GLU, OUT, IN = 0, 1, 2
GRAD_ROWS = (4096, 2048, 2048)
GRAD_AT = (0, 4096, 6144)
ALL_ROWS = 8192
ROOT = math.sqrt(2.0 / math.pi)
CUBE = 0.044715

F32 = jnp.float32
BF16 = jnp.bfloat16
MESH = pl.DeviceIdType.MESH


def mm(a, b):
    return lax.dot_general(a, b, (((1,), (0,)), ((), ())), preferred_element_type=F32)


def mm_t(a, b):
    return lax.dot_general(a, b, (((1,), (1,)), ((), ())), preferred_element_type=F32)


def t_mm(a, b):
    return lax.dot_general(a, b, (((0,), (0,)), ((), ())), preferred_element_type=F32)


def complex_mul(ar, ai, br, bi):
    return ar * br - ai * bi, ar * bi + ai * br


def power(re, im, n):
    out = None
    while n:
        if n & 1:
            out = (re, im) if out is None else complex_mul(*out, re, im)
        n >>= 1
        if n:
            re, im = complex_mul(re, im, re, im)
    return out


def as_row(four):
    return jnp.concatenate([four[c : c + 1] for c in range(4)], axis=1)


def wide(tile):
    return jnp.concatenate([tile] * 4, axis=1)


def column_sum(x):
    return jnp.sum(x, axis=0, keepdims=True)


def kernel(ns, nd, per, span, names, *refs):
    r = types.SimpleNamespace(**dict(zip(names, refs)))
    tokens = per * span
    segs = tokens // SEG
    nseg = span // SEG
    tiles = tokens // ROWS
    peers = ns * nd
    s = lax.axis_index("section")
    d = lax.axis_index("dp")
    q = lax.axis_index("seq")
    other = 1 - s
    me = d * ns + q
    sibling = {"section": other}

    def seq_peer(k):
        return {"seq": lax.rem(q + k, ns)}

    def dp_peer(k):
        return {"dp": lax.rem(d + k, nd)}

    def any_peer(k):
        at = lax.rem(me + k, peers)
        return {"dp": at // ns, "seq": lax.rem(at, ns)}

    def remote(src, dst, send, recv, device):
        return pltpu.make_async_remote_copy(
            src_ref=src, dst_ref=dst, send_sem=send, recv_sem=recv, device_id=device, device_id_type=MESH
        )

    def over(low, high, body):
        lax.fori_loop(low, high, lambda k, c: (body(k), c)[1], 0)

    def row_tiles(body, init):
        def step(i, carry):
            return body(pl.ds(pl.multiple_of(i * ROWS, ROWS), ROWS), carry)

        return lax.fori_loop(0, tiles, step, init)

    barrier = pltpu.get_barrier_semaphore()

    def greet(device):
        pl.semaphore_signal(barrier, inc=1, device_id=device, device_id_type=MESH)

    greet(sibling)
    over(1, peers, lambda k: greet(any_peer(k)))
    over(1, ns, lambda k: greet({"section": other, "seq": lax.rem(q + k, ns)}))

    load_x = pltpu.make_async_copy(r.x.at[s], r.act.at[0], r.local.at[0])
    load_x.start()
    load_cot = pltpu.make_async_copy(r.cot.at[s], r.cotv, r.local.at[1])
    weights = ((r.w_in, r.win), (r.w_out, r.wout), (r.w_glu, r.wglu))
    load_w = [
        pltpu.make_async_copy(src.at[0], dst.at[s], r.local.at[2 + i]) for i, (src, dst) in enumerate(weights)
    ]
    for copy in load_w:
        copy.start()
    load_cot.start()

    rate = jnp.exp(r.nu[...])
    phase = jnp.exp(r.theta[...])
    size = jnp.exp(-rate)
    decay_re = size * jnp.cos(phase)
    decay_im = size * jnp.sin(phase)
    double = 2.0 * rate
    scale_sq = double * (
        1.0
        - double / 2.0 * (1.0 - double / 3.0 * (1.0 - double / 4.0 * (1.0 - double / 5.0 * (1.0 - double / 6.0))))
    )
    scale = jnp.sqrt(scale_sq)
    r.prm[s, 0:1, :] = r.gain[...]
    r.prm[s, 1:2, :] = r.bias[...]
    r.prm[s, 2:3, :] = r.skip[...]
    r.prm[s, 3:4, :] = r.bglu[:, :D]
    r.prm[s, 4:5, :] = r.bglu[:, D:]
    r.prm[s, 5:6, :] = jnp.concatenate([decay_re, decay_im], axis=1)
    r.prm[s, 6:7, :] = jnp.concatenate([scale, scale], axis=1)
    r.prm[s, 7:8, :] = jnp.zeros((1, D), F32)

    count = jnp.zeros((1, 1), F32)
    steps = lax.broadcasted_iota(jnp.int32, (span, LANES), 0)
    for i in range(per):
        here = jnp.sum(r.mask[pl.ds(s * per + i, 1), :], axis=1, keepdims=True)
        r.live[i * span : (i + 1) * span, :] = jnp.where(steps < here, 1.0, 0.0)
        count = count + here.astype(F32)
    count_row = jnp.broadcast_to(count, (1, LANES))
    load_x.wait()

    def mask_input(rows, total):
        x = r.act[0, rows, :].astype(F32) * wide(r.live[rows, :])
        r.act[0, rows, :] = x.astype(BF16)
        return total + column_sum(x)

    def centred(b, mean):
        def tile(rows, total):
            off = (r.act[b, rows, :].astype(F32) - mean) * wide(r.live[rows, :])
            return total + column_sum(off * off)

        return row_tiles(tile, jnp.zeros((1, D), F32))

    def put_rows(ph, upper, lower):
        for c in range(4):
            r.bnb[ph, me, c : c + 1, :] = upper[:, c * LANES : (c + 1) * LANES]
            r.bnb[ph, me, 4 + c : 5 + c, :] = lower[:, c * LANES : (c + 1) * LANES]
        r.bnb[ph, me, 8:9, :] = count_row

    def to_all(ph, k):
        block = r.bnb.at[ph, me]
        return remote(block, block, r.bn_send.at[ph, k], r.bn_recv.at[ph, k], any_peer(k))

    def send_all(ph):
        over(1, peers, lambda k: to_all(ph, k).start())

    def wait_all(ph):
        over(1, peers, lambda k: to_all(ph, k).wait_recv())

    def norm_sums(b, total):
        mean = total / jnp.maximum(wide(count_row), 1.0)
        put_rows(b, mean, centred(b, mean))

    def norm_merge(b):
        wait_all(b)
        got = r.bnb[b]
        means, spreads, counts = got[:, 0:4, :], got[:, 4:8, :], got[:, 8:9, :]
        valid = jnp.sum(counts, axis=0)
        mean = jnp.sum(counts * means, axis=0) / valid
        apart = means - mean[None]
        spread = jnp.sum(spreads + counts * apart * apart, axis=0)
        r.stat[b, 0:1, :] = as_row(mean)
        r.stat[b, 1:2, :] = as_row(lax.rsqrt(spread / valid + EPS))
        r.stat[b, 2:3, :] = wide(valid)

    norm_sums(0, row_tiles(mask_input, jnp.zeros((1, D), F32)))

    pl.semaphore_wait(barrier, peers + ns - 1)
    send_all(0)
    send_prm = remote(r.prm.at[s], r.prm.at[s], r.far_send.at[0], r.far_recv.at[0], sibling)
    send_prm.start()
    send_w = [
        remote(src.at[0], dst.at[s], r.far_send.at[1 + i], r.far_recv.at[1 + i], sibling)
        for i, (src, dst) in enumerate(weights)
    ]
    for copy in send_w:
        copy.start()

    def decay(b, sign):
        out = []
        for c in range(2):
            re = r.prm[b, 5:6, c * LANES : (c + 1) * LANES]
            im = r.prm[b, 5:6, STATES + c * LANES : STATES + (c + 1) * LANES]
            out.append((re, sign * im))
        return out

    def every(l):
        return pl.ds(l, segs, stride=SEG)

    def advance(a, state, drive):
        return (
            a[0] * state[0] - a[1] * state[1] + drive[0],
            a[1] * state[0] + a[0] * state[1] + drive[1],
        )

    place = lax.rem(lax.broadcasted_iota(jnp.int32, (segs, LANES), 0), nseg)
    owner = lax.broadcasted_iota(jnp.int32, (segs, LANES), 0) // nseg

    def moved(x, k, reverse):
        if reverse:
            return jnp.where(place < nseg - k, pltpu.roll(x, segs - k, 0), 0.0)
        return jnp.where(place >= k, pltpu.roll(x, k, 0), 0.0)

    def seg_scan(re, im, jump, reverse):
        k = 1
        while k < nseg:
            add_re, add_im = complex_mul(*jump, moved(re, k, reverse), moved(im, k, reverse))
            re, im = re + add_re, im + add_im
            jump = complex_mul(*jump, *jump)
            k *= 2
        return re, im

    def to_seq(ph, k):
        block = r.scb.at[ph, q]
        return remote(block, block, r.sc_send.at[ph, k], r.sc_recv.at[ph, k], seq_peer(k))

    def carry(ph, drive, a, reverse, between):
        def step(i, states):
            l = SEG - 1 - i if reverse else i
            return tuple(
                advance(a[c], states[c], (drive[c, every(l), :], drive[2 + c, every(l), :])) for c in range(2)
            )

        zero = jnp.zeros((segs, LANES), F32)
        ends = lax.fori_loop(0, SEG, step, ((zero, zero), (zero, zero)), unroll=4)
        jumps = [power(*a[c], SEG) for c in range(2)]
        sums = [seg_scan(*ends[c], jumps[c], reverse) for c in range(2)]
        for i in range(per):
            last = i * nseg if reverse else (i + 1) * nseg - 1
            for c in range(2):
                r.scb[ph, q, 4 * i + c : 4 * i + c + 1, :] = sums[c][0][last : last + 1]
                r.scb[ph, q, 4 * i + 2 + c : 4 * i + 3 + c, :] = sums[c][1][last : last + 1]
        over(1, ns, lambda k: to_seq(ph, k).start())
        first = jnp.where(place == (nseg - 1 if reverse else 0), 1.0, 0.0)
        reach = [seg_scan(first, zero, jumps[c], reverse) for c in range(2)]
        between()
        over(1, ns, lambda k: to_seq(ph, k).wait_recv())
        starts = []
        for c in range(2):
            far = power(*a[c], span)
            entering = []
            for i in range(per):
                re = jnp.zeros((1, LANES), F32)
                im = jnp.zeros((1, LANES), F32)
                for lap in range(ns):
                    j = ns - 1 - lap if reverse else lap
                    before = j > q if reverse else j < q
                    new_re, new_im = advance(
                        far,
                        (re, im),
                        (r.scb[ph, j, 4 * i + c : 4 * i + c + 1, :], r.scb[ph, j, 4 * i + 2 + c : 4 * i + 3 + c, :]),
                    )
                    re = jnp.where(before, new_re, re)
                    im = jnp.where(before, new_im, im)
                entering.append((re, im))
            in_re = jnp.broadcast_to(entering[0][0], (segs, LANES))
            in_im = jnp.broadcast_to(entering[0][1], (segs, LANES))
            for i in range(1, per):
                in_re = jnp.where(owner == i, entering[i][0], in_re)
                in_im = jnp.where(owner == i, entering[i][1], in_im)
            add_re, add_im = complex_mul(*reach[c], in_re, in_im)
            starts.append((moved(sums[c][0], 1, reverse) + add_re, moved(sums[c][1], 1, reverse) + add_im))
        return starts

    def fill_states(b, starts, a, reverse):
        for c in range(2):
            r.start[b, c] = starts[c][0]
            r.start[b, 2 + c] = starts[c][1]

        def step(i, states):
            l = SEG - 1 - i if reverse else i
            out = []
            for c in range(2):
                new = advance(a[c], states[c], (r.u[b, c, every(l), :], r.u[b, 2 + c, every(l), :]))
                r.st[b, c, every(l), :] = new[0]
                r.st[b, 2 + c, every(l), :] = new[1]
                out.append(new)
            return tuple(out)

        lax.fori_loop(0, SEG, step, tuple(starts), unroll=4)

    def fill_adjoint(b, starts, a, reverse):
        back = 1 if not reverse else -1
        zero = jnp.zeros((segs, LANES), F32)
        sums = []
        for c in range(2):
            scale_c = r.prm[b, 6:7, c * LANES : (c + 1) * LANES]

            def one(l, prior, carry, c=c, scale_c=scale_c):
                state, by_re, by_im, by_scale = carry
                re, im = advance(a[c], state, (r.adj[c, every(l), :], r.adj[2 + c, every(l), :]))
                r.adj[c, every(l), :] = scale_c * re
                r.adj[2 + c, every(l), :] = scale_c * im
                by_re = by_re + (re * prior[0] + im * prior[1])
                by_im = by_im + (im * prior[0] - re * prior[1])
                by_scale = by_scale + (re * r.u[b, c, every(l), :] + im * r.u[b, 2 + c, every(l), :])
                return (re, im), by_re, by_im, by_scale

            def step(i, carry, c=c, one=one):
                l = SEG - 1 - i if reverse else i
                prior = (r.st[b, c, every(l + back), :], r.st[b, 2 + c, every(l + back), :])
                return one(l, prior, carry)

            carry_c = lax.fori_loop(0, SEG - 1, step, (starts[c], zero, zero, zero), unroll=4)
            final = one(0 if reverse else SEG - 1, (r.start[b, c], r.start[b, 2 + c]), carry_c)
            sums.append([column_sum(x) for x in final[1:]])
        return [jnp.concatenate([sums[0][i], sums[1][i]], axis=1) for i in range(3)]

    def forward_in(b):
        gain, bias, scale_row = r.prm[b, 0:1, :], r.prm[b, 1:2, :], r.prm[b, 6:7, :]
        average = r.stat[b, 0:1, :]
        slope = r.stat[b, 1:2, :] * gain

        def tile(rows, carry):
            x = r.act[b, rows, :].astype(F32)
            scaled = (wide(r.live[rows, :]) * ((x - average) * slope + bias)).astype(BF16)
            r.scaled[b, rows, :] = scaled
            u = mm(scaled, r.win[b]) * scale_row
            for c in range(4):
                r.u[b, c, rows, :] = u[:, c * LANES : (c + 1) * LANES]
            return carry

        row_tiles(tile, 0)

    def forward_out(b, finish, init):
        skip = r.prm[b, 2:3, :]
        value_bias, gate_bias = r.prm[b, 3:4, :], r.prm[b, 4:5, :]

        def tile(rows, carry):
            readout = jnp.concatenate([r.st[b, c, rows, :] for c in range(4)], axis=1).astype(BF16)
            r.readout[b, rows, :] = readout
            mixed = mm(readout, r.wout[b]) + skip * r.scaled[b, rows, :].astype(F32)
            square = mixed * mixed
            t = jnp.tanh(ROOT * mixed * (1.0 + CUBE * square))
            half = 0.5 + 0.5 * t
            active = (mixed * half).astype(BF16)
            r.active[b, rows, :] = active
            r.slope[b, rows, :] = half + (0.5 * ROOT) * mixed * (1.0 - t * t) * (1.0 + (3.0 * CUBE) * square)
            gated = mm(active, r.wglu[b])
            gate = 0.5 + 0.5 * jnp.tanh(0.5 * (gated[:, D:] + gate_bias))
            product = (gated[:, :D] + value_bias) * gate
            live = wide(r.live[rows, :])
            result = (r.act[b, rows, :].astype(F32) + live * product).astype(BF16)
            r.act[b + 1, rows, :] = result
            return finish(rows, live, gate, product * (1.0 - gate), result, carry)

        return row_tiles(tile, init)

    def back_tile(b, rows, outer, gate, steep, carry):
        grad_gated = jnp.concatenate([outer * gate, outer * steep], axis=1).astype(BF16)
        r.gg[rows, :] = grad_gated
        grad_mixed = (r.slope[b, rows, :] * mm_t(grad_gated, r.wglu[b])).astype(BF16)
        r.gm[rows, :] = grad_mixed
        grad_readout = mm_t(grad_mixed, r.wout[b])
        for c in range(4):
            r.adj[c, rows, :] = grad_readout[:, c * LANES : (c + 1) * LANES]
        by_skip = column_sum(grad_mixed.astype(F32) * r.scaled[b, rows, :].astype(F32))
        return carry[0] + by_skip, carry[1] + column_sum(grad_gated.astype(F32))

    def normed(b, rows):
        return (r.act[b, rows, :].astype(F32) - r.stat[b, 0:1, :]) * r.stat[b, 1:2, :]

    def back_in(b):
        skip = r.prm[b, 2:3, :]

        def tile(rows, carry):
            grad_projected = jnp.concatenate([r.adj[c, rows, :] for c in range(4)], axis=1).astype(BF16)
            r.gp[rows, :] = grad_projected
            grad_scaled = skip * r.gm[rows, :].astype(F32) + mm_t(grad_projected, r.win[b])
            masked = wide(r.live[rows, :]) * grad_scaled
            r.masked[rows, :] = masked
            return carry[0] + column_sum(masked * normed(b, rows)), carry[1] + column_sum(masked)

        zero = jnp.zeros((1, D), F32)
        return row_tiles(tile, (zero, zero))

    def back_norm(ph, b):
        wait_all(ph)
        got = jnp.sum(r.bnb[ph], axis=0)
        gain_total, bias_total = as_row(got[0:4]), as_row(got[4:8])
        r.vec_tot[b, 0:1, :] = gain_total
        r.vec_tot[b, 1:2, :] = bias_total
        slope = r.stat[b, 1:2, :] * r.prm[b, 0:1, :]
        per_token = slope / r.stat[b, 2:3, :]
        return slope, per_token * bias_total, per_token * gain_total

    def source_grad(b, rows, upstream, live, slope, by_bias, by_gain):
        return upstream + live * (slope * r.masked[rows, :] - by_bias - normed(b, rows) * by_gain)

    def weight_grad(b, which, left, right):
        columns = GRAD_ROWS[which] // 4

        def tile(j, carry):
            cols = pl.ds(pl.multiple_of(j * 256, 256), 256)
            grad = t_mm(left, right[:, cols]).astype(BF16)
            at = pl.multiple_of(GRAD_AT[which] + j * 1024, 1024)
            r.dw[b, pl.ds(at, 512), :] = grad[:, :LANES]
            r.dw[b, pl.ds(at + 512, 512), :] = grad[:, LANES:]
            return carry

        lax.fori_loop(0, columns // 256, tile, 0)

    def chunk(b, which):
        rows = GRAD_ROWS[which] // 2
        return b * 3 + which, rows, GRAD_AT[which], GRAD_AT[which] // 2, rows // ns, GRAD_AT[which] // 2 // ns

    def to_core(b, which):
        n, rows, at, half_at, _, _ = chunk(b, which)
        src = r.dw.at[b, pl.ds(pl.multiple_of(at + other * rows, 16), rows)]
        return remote(src, r.sec.at[b, pl.ds(half_at, rows)], r.core_send.at[n], r.core_recv.at[n], sibling)

    def to_owner(b, which, k):
        n, _, _, half_at, piece, piece_at = chunk(b, which)
        src = r.half.at[b, pl.ds(pl.multiple_of(half_at + lax.rem(q + k, ns) * piece, 16), piece)]
        dst = r.rs.at[b, q, pl.ds(piece_at, piece)]
        return remote(src, dst, r.rs_send.at[n, k], r.rs_recv.at[n, k], seq_peer(k))

    def to_line(b, which, k):
        n, _, _, _, piece, piece_at = chunk(b, which)
        block = r.line.at[b, d, pl.ds(piece_at, piece)]
        return remote(block, block, r.line_send.at[n, k], r.line_recv.at[n, k], dp_peer(k))

    def grad_place(b, which, section, k):
        _, rows, at, _, piece, _ = chunk(b, which)
        return pl.ds(pl.multiple_of(at + section * rows + lax.rem(q + k, ns) * piece, 16), piece)

    def to_result(b, which, k):
        n, _, _, _, piece, piece_at = chunk(b, which)
        src = r.sum.at[b, pl.ds(piece_at, piece)]
        dst = r.grads.at[grad_place(b, which, s, 0)]
        target = {"section": b, "seq": lax.rem(q + k, ns)}
        return remote(src, dst, r.res_send.at[n, k], r.res_recv.at[n, s * ns + k], target)

    def from_result(b, which, section, k):
        n, _, _, _, piece, piece_at = chunk(b, which)
        src = r.sum.at[b, pl.ds(piece_at, piece)]
        dst = r.grads.at[grad_place(b, which, s, 0)]
        return remote(src, dst, r.res_send.at[n, k], r.res_recv.at[n, section * ns + k], sibling)

    def own_result(b, which):
        n, _, _, _, piece, piece_at = chunk(b, which)
        return pltpu.make_async_copy(
            r.sum.at[b, pl.ds(piece_at, piece)], r.grads.at[grad_place(b, which, s, 0)], r.own.at[n]
        )

    def step_core(b, which):
        to_core(b, which).start()

    def step_owner(b, which):
        _, rows, at, half_at, _, _ = chunk(b, which)
        to_core(b, which).wait_recv()
        mine = r.dw[b, pl.ds(pl.multiple_of(at + s * rows, 16), rows), :].astype(F32)
        r.half[b, half_at : half_at + rows, :] = (mine + r.sec[b, half_at : half_at + rows, :].astype(F32)).astype(BF16)
        over(1, ns, lambda k: to_owner(b, which, k).start())

    def step_line(b, which):
        _, _, _, half_at, piece, piece_at = chunk(b, which)
        over(1, ns, lambda k: to_owner(b, which, k).wait_recv())
        total = r.half[b, pl.ds(pl.multiple_of(half_at + q * piece, 16), piece), :].astype(F32)
        for k in range(1, ns):
            total = total + r.rs[b, lax.rem(q + k, ns), piece_at : piece_at + piece, :].astype(F32)
        r.line[b, d, piece_at : piece_at + piece, :] = total.astype(BF16)
        over(1, nd, lambda k: to_line(b, which, k).start())

    def step_result(b, which):
        _, _, _, _, piece, piece_at = chunk(b, which)
        over(1, nd, lambda k: to_line(b, which, k).wait_recv())
        total = r.line[b, 0, piece_at : piece_at + piece, :].astype(F32)
        for j in range(1, nd):
            total = total + r.line[b, j, piece_at : piece_at + piece, :].astype(F32)
        r.sum[b, piece_at : piece_at + piece, :] = total.astype(BF16)
        over(1, ns, lambda k: to_result(b, which, k).start())

        @pl.when(s == b)
        def _():
            own_result(b, which).start()

        @pl.when(s != b)
        def _():
            to_result(b, which, 0).start()

    def step_end(b, which):
        @pl.when(s == b)
        def _():
            own_result(b, which).wait()
            over(1, ns, lambda k: from_result(b, which, b, k).wait_recv())
            over(0, ns, lambda k: from_result(b, which, 1 - b, k).wait_recv())

        @pl.when(s != b)
        def _():
            to_result(b, which, 0).wait_send()

        to_core(b, which).wait_send()
        over(1, ns, lambda k: to_owner(b, which, k).wait_send())
        over(1, nd, lambda k: to_line(b, which, k).wait_send())
        over(1, ns, lambda k: to_result(b, which, k).wait_send())

    def vec_seq(b, k):
        block = r.vec_a.at[b, q]
        return remote(block, block, r.va_send.at[b, k], r.va_recv.at[b, k], seq_peer(k))

    def vec_dp(b, k):
        block = r.vec_b.at[b, d]
        return remote(block, block, r.vb_send.at[b, k], r.vb_recv.at[b, k], dp_peer(k))

    def vec_one(b, by_skip, by_bias, by_decay):
        zero = jnp.zeros((1, D), F32)
        r.vec_a[b, q, 0:1, :] = zero
        r.vec_a[b, q, 1:2, :] = zero
        r.vec_a[b, q, 2:3, :] = by_skip
        r.vec_a[b, q, 3:4, :] = by_bias[:, :D]
        r.vec_a[b, q, 4:5, :] = by_bias[:, D:]
        r.vec_a[b, q, 5:6, :] = jnp.concatenate([by_decay[0], by_decay[1]], axis=1)
        r.vec_a[b, q, 6:7, :] = jnp.concatenate([by_decay[2], by_decay[2]], axis=1)
        r.vec_a[b, q, 7:8, :] = zero
        over(1, ns, lambda k: vec_seq(b, k).start())

    def vec_two(b):
        over(1, ns, lambda k: vec_seq(b, k).wait_recv())
        r.vec_b[b, d] = jnp.sum(r.vec_a[b], axis=0)
        over(1, nd, lambda k: vec_dp(b, k).start())

    def vec_three(b):
        over(1, nd, lambda k: vec_dp(b, k).wait_recv())
        total = jnp.sum(r.vec_b[b], axis=0)
        r.vec_tot[b, 2:8, :] = total[2:8]

    send_prm.wait_recv()
    for i in range(3):
        load_w[i].wait()
        send_w[i].wait_recv()
    load_cot.wait()
    zero_row = jnp.zeros((1, D), F32)

    def nothing():
        pass

    norm_merge(0)
    forward_in(0)
    ahead0, ahead1 = decay(0, 1.0), decay(1, 1.0)
    starts = carry(0, r.u.at[0], ahead0, False, nothing)
    fill_states(0, starts, ahead0, False)

    def finish_one(rows, live, gate, steep, result, carry):
        r.gate[rows, :] = gate
        r.steep[rows, :] = steep
        return carry + column_sum(result.astype(F32))

    norm_sums(1, forward_out(0, finish_one, zero_row))
    send_all(1)
    norm_merge(1)
    forward_in(1)
    starts = carry(1, r.u.at[1], ahead1, True, nothing)
    fill_states(1, starts, ahead1, True)

    def finish_two(rows, live, gate, steep, result, carry):
        return back_tile(1, rows, live * r.cotv[rows, :].astype(F32), gate, steep, carry)

    wide_zero = jnp.zeros((1, 2 * D), F32)
    by_skip, by_bias = forward_out(1, finish_two, (zero_row, wide_zero))

    keep_act = pltpu.make_async_copy(r.act.at[1 + s], r.act_out.at[s], r.local.at[5])
    keep_act.start()
    give_act = remote(r.act.at[1 + other], r.act_out.at[s], r.far_send.at[4], r.far_recv.at[4], sibling)
    give_act.start()

    back0, back1 = decay(0, -1.0), decay(1, -1.0)

    def glu_and_out(b):
        weight_grad(b, GLU, r.active[b], r.gg)
        step_core(b, GLU)
        weight_grad(b, OUT, r.readout[b], r.gm)
        step_core(b, OUT)

    starts = carry(2, r.adj, back1, False, lambda: glu_and_out(1))
    by_decay = fill_adjoint(1, starts, back1, False)
    put_rows(2, *back_in(1))
    send_all(2)
    step_owner(1, GLU)
    step_owner(1, OUT)
    vec_one(1, by_skip, by_bias, by_decay)
    weight_grad(1, IN, r.scaled[1], r.gp)
    step_core(1, IN)
    slope, by_bias_total, by_gain_total = back_norm(2, 1)

    def through(rows, carry):
        live = wide(r.live[rows, :])
        upstream = r.cotv[rows, :].astype(F32)
        grad = source_grad(1, rows, upstream, live, slope, by_bias_total, by_gain_total).astype(BF16)
        r.ig[1, rows, :] = grad
        return back_tile(0, rows, live * grad.astype(F32), r.gate[rows, :], r.steep[rows, :], carry)

    by_skip, by_bias = row_tiles(through, (zero_row, wide_zero))

    def next_pieces():
        step_line(1, GLU)
        step_line(1, OUT)
        step_owner(1, IN)
        vec_two(1)
        glu_and_out(0)

    starts = carry(3, r.adj, back0, True, next_pieces)
    by_decay = fill_adjoint(0, starts, back0, True)
    put_rows(3, *back_in(0))
    send_all(3)
    weight_grad(0, IN, r.scaled[0], r.gp)
    step_core(0, IN)
    step_owner(0, GLU)
    step_owner(0, OUT)
    vec_one(0, by_skip, by_bias, by_decay)
    step_line(1, IN)
    step_result(1, GLU)
    step_result(1, OUT)
    vec_three(1)
    slope0, by_bias_total0, by_gain_total0 = back_norm(3, 0)

    def last(rows, carry):
        live = wide(r.live[rows, :])
        upstream = r.ig[1, rows, :].astype(F32)
        grad = source_grad(0, rows, upstream, live, slope0, by_bias_total0, by_gain_total0)
        r.ig[0, rows, :] = (live * grad).astype(BF16)
        return carry

    row_tiles(last, 0)
    keep_ig = pltpu.make_async_copy(r.ig.at[s], r.ig_out.at[s], r.local.at[6])
    keep_ig.start()
    give_ig = remote(r.ig.at[other], r.ig_out.at[s], r.far_send.at[5], r.far_recv.at[5], sibling)
    give_ig.start()

    step_owner(0, IN)
    step_line(0, GLU)
    step_line(0, OUT)
    step_result(1, IN)
    vec_two(0)
    step_line(0, IN)
    step_result(0, GLU)
    step_result(0, OUT)
    vec_three(0)
    give_vec = remote(r.vec_tot.at[other], r.vec_far, r.far_send.at[6], r.far_recv.at[6], sibling)
    give_vec.start()
    step_result(0, IN)
    give_vec.wait_recv()
    total = r.vec_tot[s] + r.vec_far[...]
    r.o_gain[...] = total[0:1]
    r.o_bias[...] = total[1:2]
    r.o_skip[...] = total[2:3]
    r.o_bglu[:, :D] = total[3:4]
    r.o_bglu[:, D:] = total[4:5]
    grad_re, grad_im = total[5:6, :STATES], total[5:6, STATES:]
    grad_rate = total[6:7, :STATES] * jnp.exp(-double) / scale_sq - (grad_re * decay_re + grad_im * decay_im)
    r.o_nu[...] = grad_rate * rate
    r.o_theta[...] = (grad_im * decay_re - grad_re * decay_im) * phase

    for b in (1, 0):
        for which in (GLU, OUT, IN):
            step_end(b, which)
    keep_act.wait()
    give_act.wait()
    keep_ig.wait()
    give_ig.wait()
    give_vec.wait_send()
    send_prm.wait_send()
    for copy in send_w:
        copy.wait_send()
    for ph in range(4):
        over(1, peers, lambda k, ph=ph: to_all(ph, k).wait_send())
        over(1, ns, lambda k, ph=ph: to_seq(ph, k).wait_send())
    for b in range(2):
        over(1, ns, lambda k, b=b: vec_seq(b, k).wait_send())
        over(1, nd, lambda k, b=b: vec_dp(b, k).wait_send())


def body(ns, nd, inputs, mask, gain, bias, nu, theta, w_in, w_out, skip, w_glu, b_glu, cotangent):
    per = inputs.shape[0] // MICRO
    span = inputs.shape[1]
    tokens = per * span
    segs = tokens // SEG
    dma = pltpu.SemaphoreType.DMA
    vmem = pltpu.VMEM
    names_in = ["x", "cot", "mask", "gain", "bias", "nu", "theta", "skip", "bglu", "w_in", "w_out", "w_glu"]
    any_in = {"x", "cot", "w_in", "w_out", "w_glu"}
    outs = {
        "act_out": jax.ShapeDtypeStruct((MICRO, tokens, D), BF16),
        "ig_out": jax.ShapeDtypeStruct((MICRO, tokens, D), BF16),
        "grads": jax.ShapeDtypeStruct((ALL_ROWS, LANES), BF16),
        "o_gain": jax.ShapeDtypeStruct((1, D), F32),
        "o_bias": jax.ShapeDtypeStruct((1, D), F32),
        "o_nu": jax.ShapeDtypeStruct((1, STATES), F32),
        "o_theta": jax.ShapeDtypeStruct((1, STATES), F32),
        "o_skip": jax.ShapeDtypeStruct((1, D), F32),
        "o_bglu": jax.ShapeDtypeStruct((1, 2 * D), F32),
    }
    any_out = {"act_out", "ig_out", "grads"}
    half = ALL_ROWS // 2
    scratch = {
        "act": vmem((3, tokens, D), BF16),
        "cotv": vmem((tokens, D), BF16),
        "live": vmem((tokens, LANES), F32),
        "win": vmem((2, D, D), BF16),
        "wout": vmem((2, D, D), BF16),
        "wglu": vmem((2, D, 2 * D), BF16),
        "prm": vmem((2, 8, D), F32),
        "stat": vmem((2, 8, D), F32),
        "scaled": vmem((2, tokens, D), BF16),
        "u": vmem((2, 4, tokens, LANES), F32),
        "st": vmem((2, 4, tokens, LANES), F32),
        "start": vmem((2, 4, segs, LANES), F32),
        "readout": vmem((2, tokens, D), BF16),
        "active": vmem((2, tokens, D), BF16),
        "slope": vmem((2, tokens, D), F32),
        "gate": vmem((tokens, D), F32),
        "steep": vmem((tokens, D), F32),
        "gg": vmem((tokens, 2 * D), BF16),
        "gm": vmem((tokens, D), BF16),
        "adj": vmem((4, tokens, LANES), F32),
        "gp": vmem((tokens, D), BF16),
        "masked": vmem((tokens, D), F32),
        "ig": vmem((2, tokens, D), BF16),
        "bnb": vmem((4, ns * nd, 9, LANES), F32),
        "scb": vmem((4, ns, 4 * per, LANES), F32),
        "dw": vmem((2, ALL_ROWS, LANES), BF16),
        "sec": vmem((2, half, LANES), BF16),
        "half": vmem((2, half, LANES), BF16),
        "rs": vmem((2, ns, half // ns, LANES), BF16),
        "line": vmem((2, nd, half // ns, LANES), BF16),
        "sum": vmem((2, half // ns, LANES), BF16),
        "vec_a": vmem((2, ns, 8, D), F32),
        "vec_b": vmem((2, nd, 8, D), F32),
        "vec_tot": vmem((2, 8, D), F32),
        "vec_far": vmem((8, D), F32),
        "local": dma((7,)),
        "own": dma((6,)),
        "far_send": dma((7,)),
        "far_recv": dma((7,)),
        "bn_send": dma((4, ns * nd)),
        "bn_recv": dma((4, ns * nd)),
        "sc_send": dma((4, ns)),
        "sc_recv": dma((4, ns)),
        "core_send": dma((6,)),
        "core_recv": dma((6,)),
        "rs_send": dma((6, ns)),
        "rs_recv": dma((6, ns)),
        "line_send": dma((6, nd)),
        "line_recv": dma((6, nd)),
        "res_send": dma((6, ns)),
        "res_recv": dma((6, 2 * ns)),
        "va_send": dma((2, ns)),
        "va_recv": dma((2, ns)),
        "vb_send": dma((2, nd)),
        "vb_recv": dma((2, nd)),
    }
    in_any = pl.BlockSpec(memory_space=pl.ANY)
    in_vmem = pl.BlockSpec(memory_space=pltpu.VMEM)
    names = names_in + list(outs) + list(scratch)
    act, ig, grads, d_gain, d_bias, d_nu, d_theta, d_skip, d_bglu = pl.pallas_call(
        functools.partial(kernel, ns, nd, per, span, names),
        out_shape=list(outs.values()),
        in_specs=[in_any if name in any_in else in_vmem for name in names_in],
        out_specs=[in_any if name in any_out else in_vmem for name in outs],
        scratch_shapes=list(scratch.values()),
        compiler_params=pltpu.CompilerParams(
            collective_id=0, has_side_effects=True, vmem_limit_bytes=60 * 2**20
        ),
    )(
        inputs.reshape(MICRO, tokens, D),
        cotangent.reshape(MICRO, tokens, D),
        mask,
        gain,
        bias,
        nu,
        theta,
        skip,
        b_glu,
        w_in,
        w_out,
        w_glu,
    )

    def matrix(which):
        part = grads[GRAD_AT[which] : GRAD_AT[which] + GRAD_ROWS[which]].reshape(-1, D, LANES)
        return jnp.transpose(part, (1, 0, 2)).reshape(1, D, -1).astype(F32)

    whole = (1, MICRO * per, span, D)
    return (
        act.reshape(whole),
        ig.reshape(whole).astype(F32),
        d_gain,
        d_bias,
        d_nu,
        d_theta,
        matrix(IN),
        matrix(OUT),
        d_skip,
        matrix(GLU),
        d_bglu,
    )


def solution(mesh):
    rows = P("section", None)
    cube = P("section", None, None)
    tokens = P("dp", "seq", None)
    spread = P("section", "dp", "seq", None)
    in_specs = (tokens, P("dp", "seq"), rows, rows, rows, rows, cube, cube, rows, cube, rows, tokens)
    out_specs = (spread, spread, rows, rows, rows, rows, cube, cube, rows, cube, rows)
    return jax.shard_map(
        functools.partial(body, mesh.shape["seq"], mesh.shape["dp"]),
        mesh=mesh,
        in_specs=in_specs,
        out_specs=out_specs,
        check_vma=False,
    )
```

```python
import functools
import math
import types

import jax
import jax.numpy as jnp
from jax import lax
from jax.experimental import pallas as pl
from jax.experimental.pallas import tpu as pltpu
from jax.sharding import PartitionSpec as P

D = 512
STATES = 256
MICRO = 2
EPS = 1e-05
LANES = 128
ROWS = 256
SEG = 32
EIGHT = 8
GLU, OUT, IN = 0, 1, 2
GRAD_ROWS = (4096, 2048, 2048)
GRAD_AT = (0, 4096, 6144)
ALL_ROWS = 8192
ORDERS = (("seq", "dp"), ("seq", "dp"), ("seq", "dp"), ("seq", "dp"), ("seq", "dp"), ("seq", "dp"))
PLAN = (
    "in1",
    "glu1 out1",
    "in1",
    "glu0 out0",
    "in0 glu1 out1 in1",
    "",
    "glu1 out1 in1 glu0 out0",
    "in0 glu0 out0",
    "in0 glu0 out0 in0",
)
ROOT = math.sqrt(2.0 / math.pi)
CUBE = 0.044715

F32 = jnp.float32
BF16 = jnp.bfloat16
MESH = pl.DeviceIdType.MESH


def mm(a, b):
    return lax.dot_general(a, b, (((1,), (0,)), ((), ())), preferred_element_type=F32)


def mm_t(a, b):
    return lax.dot_general(a, b, (((1,), (1,)), ((), ())), preferred_element_type=F32)


def t_mm(a, b):
    return lax.dot_general(a, b, (((0,), (0,)), ((), ())), preferred_element_type=F32)


def complex_mul(ar, ai, br, bi):
    return ar * br - ai * bi, ar * bi + ai * br


def power(re, im, n):
    out = None
    while n:
        if n & 1:
            out = (re, im) if out is None else complex_mul(*out, re, im)
        n >>= 1
        if n:
            re, im = complex_mul(re, im, re, im)
    return out


def as_row(four):
    return jnp.concatenate([four[c : c + 1] for c in range(4)], axis=1)


def wide(tile):
    return jnp.concatenate([tile] * 4, axis=1)


def column_sum(x):
    return jnp.sum(x, axis=0, keepdims=True)


def slots_of(rows, counts, spread):
    out, start = [], 0
    for level, count in enumerate(counts):
        size = rows if spread and level == len(counts) - 1 else rows // count
        out.append((start, size))
        start += count * size
        rows //= count
    return out


def slot_rows(ns, nd):
    inner = next(n for n in range(math.isqrt(ns), 0, -1) if ns % n == 0)
    sizes = {"seq": ns, "dp": nd, "in": inner, "out": ns // inner}
    bases = [0]
    for n, order in enumerate(ORDERS):
        rows = GRAD_ROWS[n % 3] // 2
        counts = [sizes[name] for name in order]
        spread = rows // math.prod(counts) % 16 != 0
        start, size = slots_of(rows, counts, spread)[-1]
        bases.append(bases[-1] + start + counts[-1] * size)
    return bases


def kernel(ns, nd, per, span, names, *refs):
    r = types.SimpleNamespace(**dict(zip(names, refs)))
    tokens = per * span
    segs = tokens // SEG
    nseg = span // SEG
    tiles = tokens // ROWS
    blocks = segs // EIGHT
    peers = ns * nd
    s = lax.axis_index("section")
    d = lax.axis_index("dp")
    q = lax.axis_index("seq")
    other = 1 - s
    me = d * ns + q
    sibling = {"section": other}

    def seq_peer(k):
        return {"seq": lax.rem(q + k, ns)}

    def dp_peer(k):
        return {"dp": lax.rem(d + k, nd)}

    def any_peer(k):
        at = lax.rem(me + k, peers)
        return {"dp": at // ns, "seq": lax.rem(at, ns)}

    def remote(src, dst, send, recv, device):
        return pltpu.make_async_remote_copy(
            src_ref=src, dst_ref=dst, send_sem=send, recv_sem=recv, device_id=device, device_id_type=MESH
        )

    def over(low, high, body):
        lax.fori_loop(low, high, lambda k, c: (body(k), c)[1], 0)

    def row_tiles(body, init):
        def step(i, carry):
            return body(pl.ds(pl.multiple_of(i * ROWS, ROWS), ROWS), carry)

        return lax.fori_loop(0, tiles, step, init)

    slot_base = slot_rows(ns, nd)

    barrier = pltpu.get_barrier_semaphore()

    def greet(device):
        pl.semaphore_signal(barrier, inc=1, device_id=device, device_id_type=MESH)

    greet(sibling)
    over(1, peers, lambda k: greet(any_peer(k)))
    over(1, ns, lambda k: greet({"section": other, **seq_peer(k)}))
    over(1, nd, lambda k: greet({"section": other, **dp_peer(k)}))

    load_x = pltpu.make_async_copy(r.x.at[s], r.act.at[0], r.local.at[0])
    load_x.start()
    load_cot = pltpu.make_async_copy(r.cot.at[s], r.cotv, r.local.at[1])
    weights = ((r.w_in, r.win), (r.w_out, r.wout), (r.w_glu, r.wglu))
    load_w = [
        pltpu.make_async_copy(src.at[0], dst.at[s], r.local.at[2 + i]) for i, (src, dst) in enumerate(weights)
    ]
    for copy in load_w:
        copy.start()
    load_cot.start()

    rate = jnp.exp(r.nu[...])
    phase = jnp.exp(r.theta[...])
    size = jnp.exp(-rate)
    decay_re = size * jnp.cos(phase)
    decay_im = size * jnp.sin(phase)
    double = 2.0 * rate
    scale_sq = double * (
        1.0
        - double / 2.0 * (1.0 - double / 3.0 * (1.0 - double / 4.0 * (1.0 - double / 5.0 * (1.0 - double / 6.0))))
    )
    scale = jnp.sqrt(scale_sq)
    r.prm[s, 0:1, :] = r.gain[...]
    r.prm[s, 1:2, :] = r.bias[...]
    r.prm[s, 2:3, :] = r.skip[...]
    r.prm[s, 3:4, :] = r.bglu[:, :D]
    r.prm[s, 4:5, :] = r.bglu[:, D:]
    r.prm[s, 5:6, :] = jnp.concatenate([decay_re, decay_im], axis=1)
    r.prm[s, 6:7, :] = jnp.concatenate([scale, scale], axis=1)
    r.prm[s, 7:8, :] = jnp.zeros((1, D), F32)

    count = jnp.zeros((1, 1), F32)
    row = lax.broadcasted_iota(jnp.int32, (tokens, LANES), 0)
    inside = lax.rem(row, ROWS)
    token = row - inside + lax.rem(inside, EIGHT) * SEG + inside // EIGHT
    step_of = lax.rem(token, span)
    sequence = token // span
    ends_at = jnp.zeros((tokens, LANES), jnp.int32)
    for i in range(per):
        here = jnp.sum(r.mask[pl.ds(s * per + i, 1), :], axis=1, keepdims=True)
        ends_at = jnp.where(sequence == i, here, ends_at)
        count = count + here.astype(F32)
    r.live[...] = jnp.where(step_of < ends_at, 1.0, 0.0)
    count_row = jnp.broadcast_to(count, (1, LANES))
    to_row = lax.broadcasted_iota(jnp.int32, (ROWS, ROWS), 0)
    from_row = lax.broadcasted_iota(jnp.int32, (ROWS, ROWS), 1)
    r.order[...] = jnp.where(from_row == lax.rem(to_row, EIGHT) * SEG + to_row // EIGHT, 1.0, 0.0).astype(BF16)
    load_x.wait()

    def mask_input(rows, total):
        x = mm(r.order[...], r.act[0, rows, :]) * wide(r.live[rows, :])
        r.act[0, rows, :] = x.astype(BF16)
        return total + column_sum(x)

    def centred(b, mean):
        def tile(rows, total):
            off = (r.act[b, rows, :].astype(F32) - mean) * wide(r.live[rows, :])
            return total + column_sum(off * off)

        return row_tiles(tile, jnp.zeros((1, D), F32))

    def put_rows(ph, upper, lower):
        for c in range(4):
            r.bnb[ph, me, c : c + 1, :] = upper[:, c * LANES : (c + 1) * LANES]
            r.bnb[ph, me, 4 + c : 5 + c, :] = lower[:, c * LANES : (c + 1) * LANES]
        r.bnb[ph, me, 8:9, :] = count_row

    def to_all(ph, k):
        block = r.bnb.at[ph, me]
        return remote(block, block, r.bn_send.at[ph, k], r.bn_recv.at[ph, k], any_peer(k))

    def send_all(ph):
        over(1, peers, lambda k: to_all(ph, k).start())

    def wait_all(ph):
        over(1, peers, lambda k: to_all(ph, k).wait_recv())

    def norm_sums(b, total):
        mean = total / jnp.maximum(wide(count_row), 1.0)
        put_rows(b, mean, centred(b, mean))

    def norm_merge(b):
        wait_all(b)
        got = r.bnb[b]
        means, spreads, counts = got[:, 0:4, :], got[:, 4:8, :], got[:, 8:9, :]
        valid = jnp.sum(counts, axis=0)
        mean = jnp.sum(counts * means, axis=0) / valid
        apart = means - mean[None]
        spread = jnp.sum(spreads + counts * apart * apart, axis=0)
        r.stat[b, 0:1, :] = as_row(mean)
        r.stat[b, 1:2, :] = as_row(lax.rsqrt(spread / valid + EPS))
        r.stat[b, 2:3, :] = wide(valid)

    norm_sums(0, row_tiles(mask_input, jnp.zeros((1, D), F32)))

    pl.semaphore_wait(barrier, peers + ns - 1 + nd - 1)
    send_all(0)
    send_prm = remote(r.prm.at[s], r.prm.at[s], r.far_send.at[0], r.far_recv.at[0], sibling)
    send_prm.start()
    send_w = [
        remote(src.at[0], dst.at[s], r.far_send.at[1 + i], r.far_recv.at[1 + i], sibling)
        for i, (src, dst) in enumerate(weights)
    ]
    for copy in send_w:
        copy.start()

    def decay(b, sign):
        out = []
        for c in range(2):
            re = r.prm[b, 5:6, c * LANES : (c + 1) * LANES]
            im = r.prm[b, 5:6, STATES + c * LANES : STATES + (c + 1) * LANES]
            out.append((re, sign * im))
        return out

    def step_rows(k, l):
        return pl.ds(pl.multiple_of(k * ROWS + l * EIGHT, EIGHT), EIGHT)

    def at_step(ref, l):
        return jnp.concatenate([ref[step_rows(k, l), :] for k in range(blocks)], axis=0)

    def put_step(ref, l, value):
        for k in range(blocks):
            ref[step_rows(k, l), :] = value[k * EIGHT : (k + 1) * EIGHT]

    def advance(a, state, drive):
        return (
            a[0] * state[0] - a[1] * state[1] + drive[0],
            a[1] * state[0] + a[0] * state[1] + drive[1],
        )

    place = lax.rem(lax.broadcasted_iota(jnp.int32, (segs, LANES), 0), nseg)
    owner = lax.broadcasted_iota(jnp.int32, (segs, LANES), 0) // nseg

    def moved(x, k, reverse):
        if reverse:
            return jnp.where(place < nseg - k, pltpu.roll(x, segs - k, 0), 0.0)
        return jnp.where(place >= k, pltpu.roll(x, k, 0), 0.0)

    def seg_scan(re, im, jump, reverse):
        k = 1
        while k < nseg:
            add_re, add_im = complex_mul(*jump, moved(re, k, reverse), moved(im, k, reverse))
            re, im = re + add_re, im + add_im
            jump = complex_mul(*jump, *jump)
            k *= 2
        return re, im

    def to_seq(ph, k):
        block = r.scb.at[ph, q]
        return remote(block, block, r.sc_send.at[ph, k], r.sc_recv.at[ph, k], seq_peer(k))

    def carry(ph, drive, a, reverse, between):
        def step(i, states):
            l = SEG - 1 - i if reverse else i
            return tuple(
                advance(a[c], states[c], (at_step(drive.at[c], l), at_step(drive.at[2 + c], l))) for c in range(2)
            )

        zero = jnp.zeros((segs, LANES), F32)
        ends = lax.fori_loop(0, SEG, step, ((zero, zero), (zero, zero)), unroll=4)
        jumps = [power(*a[c], SEG) for c in range(2)]
        sums = [seg_scan(*ends[c], jumps[c], reverse) for c in range(2)]
        for i in range(per):
            last = i * nseg if reverse else (i + 1) * nseg - 1
            for c in range(2):
                r.scb[ph, q, 4 * i + c : 4 * i + c + 1, :] = sums[c][0][last : last + 1]
                r.scb[ph, q, 4 * i + 2 + c : 4 * i + 3 + c, :] = sums[c][1][last : last + 1]
        over(1, ns, lambda k: to_seq(ph, k).start())
        first = jnp.where(place == (nseg - 1 if reverse else 0), 1.0, 0.0)
        reach = [seg_scan(first, zero, jumps[c], reverse) for c in range(2)]
        between()
        over(1, ns, lambda k: to_seq(ph, k).wait_recv())
        starts = []
        for c in range(2):
            far = power(*a[c], span)
            entering = []
            for i in range(per):
                re = jnp.zeros((1, LANES), F32)
                im = jnp.zeros((1, LANES), F32)
                for lap in range(ns):
                    j = ns - 1 - lap if reverse else lap
                    before = j > q if reverse else j < q
                    new_re, new_im = advance(
                        far,
                        (re, im),
                        (r.scb[ph, j, 4 * i + c : 4 * i + c + 1, :], r.scb[ph, j, 4 * i + 2 + c : 4 * i + 3 + c, :]),
                    )
                    re = jnp.where(before, new_re, re)
                    im = jnp.where(before, new_im, im)
                entering.append((re, im))
            in_re = jnp.broadcast_to(entering[0][0], (segs, LANES))
            in_im = jnp.broadcast_to(entering[0][1], (segs, LANES))
            for i in range(1, per):
                in_re = jnp.where(owner == i, entering[i][0], in_re)
                in_im = jnp.where(owner == i, entering[i][1], in_im)
            add_re, add_im = complex_mul(*reach[c], in_re, in_im)
            starts.append((moved(sums[c][0], 1, reverse) + add_re, moved(sums[c][1], 1, reverse) + add_im))
        return starts

    def fill_states(b, starts, a, reverse):
        for c in range(2):
            r.start[b, c] = starts[c][0]
            r.start[b, 2 + c] = starts[c][1]

        def step(i, states):
            l = SEG - 1 - i if reverse else i
            out = []
            for c in range(2):
                new = advance(a[c], states[c], (at_step(r.u.at[b, c], l), at_step(r.u.at[b, 2 + c], l)))
                put_step(r.st.at[b, c], l, new[0])
                put_step(r.st.at[b, 2 + c], l, new[1])
                out.append(new)
            return tuple(out)

        lax.fori_loop(0, SEG, step, tuple(starts), unroll=4)

    def fill_adjoint(b, starts, a, reverse):
        back = 1 if not reverse else -1
        zero = jnp.zeros((segs, LANES), F32)
        sums = []
        for c in range(2):
            scale_c = r.prm[b, 6:7, c * LANES : (c + 1) * LANES]

            def one(l, prior, carry, c=c, scale_c=scale_c):
                state, by_re, by_im, by_scale = carry
                re, im = advance(a[c], state, (at_step(r.adj.at[c], l), at_step(r.adj.at[2 + c], l)))
                put_step(r.adj.at[c], l, scale_c * re)
                put_step(r.adj.at[2 + c], l, scale_c * im)
                by_re = by_re + (re * prior[0] + im * prior[1])
                by_im = by_im + (im * prior[0] - re * prior[1])
                by_scale = by_scale + (re * at_step(r.u.at[b, c], l) + im * at_step(r.u.at[b, 2 + c], l))
                return (re, im), by_re, by_im, by_scale

            def step(i, carry, c=c, one=one):
                l = SEG - 1 - i if reverse else i
                prior = (at_step(r.st.at[b, c], l + back), at_step(r.st.at[b, 2 + c], l + back))
                return one(l, prior, carry)

            carry_c = lax.fori_loop(0, SEG - 1, step, (starts[c], zero, zero, zero), unroll=4)
            final = one(0 if reverse else SEG - 1, (r.start[b, c], r.start[b, 2 + c]), carry_c)
            sums.append([column_sum(x) for x in final[1:]])
        return [jnp.concatenate([sums[0][i], sums[1][i]], axis=1) for i in range(3)]

    def forward_in(b):
        gain, bias, scale_row = r.prm[b, 0:1, :], r.prm[b, 1:2, :], r.prm[b, 6:7, :]
        average = r.stat[b, 0:1, :]
        slope = r.stat[b, 1:2, :] * gain

        def tile(rows, carry):
            x = r.act[b, rows, :].astype(F32)
            scaled = (wide(r.live[rows, :]) * ((x - average) * slope + bias)).astype(BF16)
            r.scaled[b, rows, :] = scaled
            u = mm(scaled, r.win[b]) * scale_row
            for c in range(4):
                r.u[b, c, rows, :] = u[:, c * LANES : (c + 1) * LANES]
            return carry

        row_tiles(tile, 0)

    def forward_out(b, finish, init):
        skip = r.prm[b, 2:3, :]
        value_bias, gate_bias = r.prm[b, 3:4, :], r.prm[b, 4:5, :]

        def tile(rows, carry):
            readout = jnp.concatenate([r.st[b, c, rows, :] for c in range(4)], axis=1).astype(BF16)
            r.readout[b, rows, :] = readout
            mixed = mm(readout, r.wout[b]) + skip * r.scaled[b, rows, :].astype(F32)
            square = mixed * mixed
            t = jnp.tanh(ROOT * mixed * (1.0 + CUBE * square))
            half = 0.5 + 0.5 * t
            active = (mixed * half).astype(BF16)
            r.active[b, rows, :] = active
            r.slope[b, rows, :] = half + (0.5 * ROOT) * mixed * (1.0 - t * t) * (1.0 + (3.0 * CUBE) * square)
            gated = mm(active, r.wglu[b])
            gate = 0.5 + 0.5 * jnp.tanh(0.5 * (gated[:, D:] + gate_bias))
            product = (gated[:, :D] + value_bias) * gate
            live = wide(r.live[rows, :])
            result = (r.act[b, rows, :].astype(F32) + live * product).astype(BF16)
            r.act[b + 1, rows, :] = result
            return finish(rows, live, gate, product * (1.0 - gate), result, carry)

        return row_tiles(tile, init)

    def back_tile(b, rows, outer, gate, steep, carry):
        grad_gated = jnp.concatenate([outer * gate, outer * steep], axis=1).astype(BF16)
        r.gg[rows, :] = grad_gated
        grad_mixed = (r.slope[b, rows, :] * mm_t(grad_gated, r.wglu[b])).astype(BF16)
        r.gm[rows, :] = grad_mixed
        grad_readout = mm_t(grad_mixed, r.wout[b])
        for c in range(4):
            r.adj[c, rows, :] = grad_readout[:, c * LANES : (c + 1) * LANES]
        by_skip = column_sum(grad_mixed.astype(F32) * r.scaled[b, rows, :].astype(F32))
        return carry[0] + by_skip, carry[1] + column_sum(grad_gated.astype(F32))

    def normed(b, rows):
        return (r.act[b, rows, :].astype(F32) - r.stat[b, 0:1, :]) * r.stat[b, 1:2, :]

    def back_in(b):
        skip = r.prm[b, 2:3, :]

        def tile(rows, carry):
            grad_projected = jnp.concatenate([r.adj[c, rows, :] for c in range(4)], axis=1).astype(BF16)
            r.readout[b, rows, :] = grad_projected
            grad_scaled = skip * r.gm[rows, :].astype(F32) + mm_t(grad_projected, r.win[b])
            masked = wide(r.live[rows, :]) * grad_scaled
            r.slope[b, rows, :] = masked
            return carry[0] + column_sum(masked * normed(b, rows)), carry[1] + column_sum(masked)

        zero = jnp.zeros((1, D), F32)
        return row_tiles(tile, (zero, zero))

    def back_norm(ph, b):
        wait_all(ph)
        got = jnp.sum(r.bnb[ph], axis=0)
        gain_total, bias_total = as_row(got[0:4]), as_row(got[4:8])
        r.vec_tot[b, 0:1, :] = gain_total
        r.vec_tot[b, 1:2, :] = bias_total
        slope = r.stat[b, 1:2, :] * r.prm[b, 0:1, :]
        per_token = slope / r.stat[b, 2:3, :]
        return slope, per_token * bias_total, per_token * gain_total

    def source_grad(b, rows, upstream, live, slope, by_bias, by_gain):
        return upstream + live * (slope * r.slope[b, rows, :] - by_bias - normed(b, rows) * by_gain)

    def weight_grad(b, which, left, right):
        columns = GRAD_ROWS[which] // 4

        def tile(j, carry):
            cols = pl.ds(pl.multiple_of(j * 256, 256), 256)
            grad = t_mm(left, right[:, cols]).astype(BF16)
            at = pl.multiple_of(GRAD_AT[which] + j * 1024, 1024)
            r.dw[b, pl.ds(at, 512), :] = grad[:, :LANES]
            r.dw[b, pl.ds(at + 512, 512), :] = grad[:, LANES:]
            return carry

        lax.fori_loop(0, columns // 256, tile, 0)

    inner = next(n for n in range(math.isqrt(ns), 0, -1) if ns % n == 0)
    outer = ns // inner
    q_out, q_in = q // inner, lax.rem(q, inner)
    axes = {
        "seq": (ns, q, seq_peer),
        "dp": (nd, d, dp_peer),
        "in": (inner, q_in, lambda k: {"seq": q_out * inner + lax.rem(q_in + k, inner)}),
        "out": (outer, q_out, lambda k: {"seq": lax.rem(q_out + k, outer) * inner + q_in}),
    }

    class Reduced:
        def __init__(self, b, which):
            self.b, self.n, self.at = b, b * 3 + which, GRAD_AT[which]
            self.base = self.at // 2
            self.axes = [axes[name] for name in ORDERS[self.n]]
            self.sizes, self.offsets = [GRAD_ROWS[which] // 2], [0]
            for count, index, _ in self.axes:
                self.sizes.append(self.sizes[-1] // count)
                self.offsets.append(self.offsets[-1] + index * self.sizes[-1])
            self.spread = self.sizes[-1] % 16 != 0
            self.slots = slots_of(GRAD_ROWS[which] // 2, [count for count, _, _ in self.axes], self.spread)
            self.slot_base = slot_base[self.n]
            self.steps = self.plan()

        def rows(self, offset, size):
            return pl.ds(pl.multiple_of(self.base + offset, 16), size)

        def to_core(self):
            size = self.sizes[0]
            src = r.dw.at[self.b, pl.ds(pl.multiple_of(self.at + other * size, 16), size)]
            return remote(src, r.sec.at[self.b, self.rows(0, size)], r.core_send.at[self.n], r.core_recv.at[self.n], sibling)

        def slot(self, level, index):
            start, size = self.slots[level]
            return pl.ds(pl.multiple_of(self.slot_base + start + index * size, 16), size)

        def scatter(self, level, k):
            count, index, peer = self.axes[level]
            if self.spread and level == len(self.axes) - 1:
                src = r.slots.at[self.slot(level, index)]
            else:
                size = self.sizes[level + 1]
                src = r.half.at[self.b, self.rows(self.offsets[level] + lax.rem(index + k, count) * size, size)]
            dst = r.slots.at[self.slot(level, index)]
            return remote(src, dst, r.rs_send.at[self.n, level, k], r.rs_recv.at[self.n, level, k], peer(k))

        def gather(self, level, k):
            block = r.gat.at[self.b, self.rows(self.offsets[level + 1], self.sizes[level + 1])]
            return remote(
                block, block, r.ag_send.at[self.n, level, k], r.ag_recv.at[self.n, level, k], self.axes[level][2](k)
            )

        def place(self):
            return pl.ds(pl.multiple_of(self.at + s * self.sizes[0] + self.offsets[1], 16), self.sizes[1])

        def result(self, k, section):
            src = r.gat.at[self.b, self.rows(self.offsets[1], self.sizes[1])]
            recv = r.ag_recv.at[self.n, 0, section * self.axes[0][0] + k]
            target = {"section": self.b, **self.axes[0][2](k)} if not isinstance(k, int) or k else {"section": self.b}
            return remote(src, r.grads.at[self.place()], r.ag_send.at[self.n, 0, k], recv, target)

        def own(self):
            src = r.gat.at[self.b, self.rows(self.offsets[1], self.sizes[1])]
            return pltpu.make_async_copy(src, r.grads.at[self.place()], r.own.at[self.n])

        def each(self, level, body):
            over(1, self.axes[level][0], body)

        def first(self):
            size = self.sizes[0]
            self.to_core().wait_recv()
            mine = r.dw[self.b, pl.ds(pl.multiple_of(self.at + s * size, 16), size), :].astype(F32)
            there = r.sec[self.b, self.base : self.base + size, :].astype(F32)
            r.half[self.b, self.base : self.base + size, :] = (mine + there).astype(BF16)

        def collect(self, level):
            self.each(level, lambda k: self.scatter(level, k).wait_recv())
            count, index, _ = self.axes[level]
            last = level == len(self.axes) - 1
            if self.spread and last:
                total = sum(r.slots[self.slot(level, j), :].astype(F32) for j in range(count))
                r.gat[self.b, self.rows(self.offsets[level], self.sizes[level]), :] = total.astype(BF16)
                return
            here = self.rows(self.offsets[level + 1], self.sizes[level + 1])
            total = r.half[self.b, here, :].astype(F32)
            for k in range(1, count):
                total = total + r.slots[self.slot(level, lax.rem(index + k, count)), :].astype(F32)
            (r.gat if last else r.half)[self.b, here, :] = total.astype(BF16)

        def send(self, level):
            if self.spread and level == len(self.axes) - 1:
                here = self.rows(self.offsets[level], self.sizes[level])
                r.slots[self.slot(level, self.axes[level][1]), :] = r.half[self.b, here, :]
            self.each(level, lambda k: self.scatter(level, k).start())

        def share(self, level):
            if level:
                self.each(level, lambda k: self.gather(level, k).start())
                return
            self.each(0, lambda k: self.result(k, s).start())

            @pl.when(s == self.b)
            def _():
                self.own().start()

            @pl.when(s != self.b)
            def _():
                self.result(0, s).start()

        def plan(self):
            depth = len(self.axes)
            top = depth - 2 if self.spread else depth - 1
            yield self.to_core().start()
            self.first()
            yield self.send(0)
            for level in range(1, depth):
                self.collect(level - 1)
                yield self.send(level)
            self.collect(depth - 1)
            yield self.share(top)
            for level in range(top, 0, -1):
                self.each(level, lambda k, level=level: self.gather(level, k).wait_recv())
                yield self.share(level - 1)

            @pl.when(s == self.b)
            def _():
                self.own().wait()
                self.each(0, lambda k: self.result(k, self.b).wait_recv())
                over(0, self.axes[0][0], lambda k: self.result(k, 1 - self.b).wait_recv())

            @pl.when(s != self.b)
            def _():
                self.result(0, s).wait_send()

            self.to_core().wait_send()
            for level in range(depth):
                self.each(level, lambda k, level=level: self.scatter(level, k).wait_send())
            for level in range(1, top + 1):
                self.each(level, lambda k, level=level: self.gather(level, k).wait_send())
            self.each(0, lambda k: self.result(k, s).wait_send())
            yield True

        def step(self):
            return next(self.steps, True)

    sums_of = [Reduced(b, which) for b in range(2) for which in (GLU, OUT, IN)]
    by_name = dict(zip(("glu0", "out0", "in0", "glu1", "out1", "in1"), sums_of))

    def go(names):
        for name in names.split():
            by_name[name].step()

    def vec_seq(b, k):
        block = r.vec_a.at[b, q]
        return remote(block, block, r.va_send.at[b, k], r.va_recv.at[b, k], seq_peer(k))

    def vec_dp(b, k):
        block = r.vec_b.at[b, d]
        return remote(block, block, r.vb_send.at[b, k], r.vb_recv.at[b, k], dp_peer(k))

    def vec_one(b, by_skip, by_bias, by_decay):
        zero = jnp.zeros((1, D), F32)
        r.vec_a[b, q, 0:1, :] = zero
        r.vec_a[b, q, 1:2, :] = zero
        r.vec_a[b, q, 2:3, :] = by_skip
        r.vec_a[b, q, 3:4, :] = by_bias[:, :D]
        r.vec_a[b, q, 4:5, :] = by_bias[:, D:]
        r.vec_a[b, q, 5:6, :] = jnp.concatenate([by_decay[0], by_decay[1]], axis=1)
        r.vec_a[b, q, 6:7, :] = jnp.concatenate([by_decay[2], by_decay[2]], axis=1)
        r.vec_a[b, q, 7:8, :] = zero
        over(1, ns, lambda k: vec_seq(b, k).start())

    def vec_two(b):
        over(1, ns, lambda k: vec_seq(b, k).wait_recv())
        r.vec_b[b, d] = jnp.sum(r.vec_a[b], axis=0)
        over(1, nd, lambda k: vec_dp(b, k).start())

    def vec_three(b):
        over(1, nd, lambda k: vec_dp(b, k).wait_recv())
        total = jnp.sum(r.vec_b[b], axis=0)
        r.vec_tot[b, 2:8, :] = total[2:8]

    send_prm.wait_recv()
    for i in range(3):
        load_w[i].wait()
        send_w[i].wait_recv()
    load_cot.wait()

    def order_cot(rows, carry):
        r.cotv[rows, :] = mm(r.order[...], r.cotv[rows, :]).astype(BF16)
        return carry

    row_tiles(order_cot, 0)

    def in_time(src, dst):
        def tile(rows, carry):
            dst[rows, :] = t_mm(r.order[...], src[rows, :]).astype(BF16)
            return carry

        row_tiles(tile, 0)

    zero_row = jnp.zeros((1, D), F32)

    def nothing():
        pass

    norm_merge(0)
    forward_in(0)
    ahead0, ahead1 = decay(0, 1.0), decay(1, 1.0)
    starts = carry(0, r.u.at[0], ahead0, False, nothing)
    fill_states(0, starts, ahead0, False)

    def finish_one(rows, live, gate, steep, result, carry):
        r.gate[rows, :] = gate
        r.steep[rows, :] = steep
        return carry + column_sum(result.astype(F32))

    norm_sums(1, forward_out(0, finish_one, zero_row))
    send_all(1)
    in_time(r.act.at[1], r.leave.at[0])
    norm_merge(1)
    forward_in(1)
    starts = carry(1, r.u.at[1], ahead1, True, nothing)
    fill_states(1, starts, ahead1, True)

    def finish_two(rows, live, gate, steep, result, carry):
        return back_tile(1, rows, live * r.cotv[rows, :].astype(F32), gate, steep, carry)

    wide_zero = jnp.zeros((1, 2 * D), F32)
    by_skip, by_bias = forward_out(1, finish_two, (zero_row, wide_zero))

    keep_act = pltpu.make_async_copy(r.leave.at[s], r.act_out.at[s], r.local.at[5])
    give_act = remote(r.leave.at[other], r.act_out.at[s], r.far_send.at[4], r.far_recv.at[4], sibling)

    back0, back1 = decay(0, -1.0), decay(1, -1.0)

    def glu_and_out(b):
        weight_grad(b, GLU, r.active[b], r.gg)
        go(f"glu{b}")
        weight_grad(b, OUT, r.readout[b], r.gm)
        go(f"out{b}")

    def first_pieces():
        glu_and_out(1)
        in_time(r.act.at[2], r.leave.at[1])
        keep_act.start()
        give_act.start()
        go("glu1 out1")

    starts = carry(2, r.adj, back1, False, first_pieces)
    by_decay = fill_adjoint(1, starts, back1, False)
    put_rows(2, *back_in(1))
    send_all(2)
    weight_grad(1, IN, r.scaled[1], r.readout.at[1])
    go("in1")
    vec_one(1, by_skip, by_bias, by_decay)
    go(PLAN[0])
    slope, by_bias_total, by_gain_total = back_norm(2, 1)

    def through(rows, carry):
        live = wide(r.live[rows, :])
        upstream = r.cotv[rows, :].astype(F32)
        grad = source_grad(1, rows, upstream, live, slope, by_bias_total, by_gain_total).astype(BF16)
        r.ig[rows, :] = grad
        return back_tile(0, rows, live * grad.astype(F32), r.gate[rows, :], r.steep[rows, :], carry)

    by_skip, by_bias = row_tiles(through, (zero_row, wide_zero))

    def next_pieces():
        go(PLAN[1])
        glu_and_out(0)
        go(PLAN[2])
        vec_two(1)

    starts = carry(3, r.adj, back0, True, next_pieces)
    by_decay = fill_adjoint(0, starts, back0, True)
    go(PLAN[3])
    put_rows(3, *back_in(0))
    send_all(3)
    weight_grad(0, IN, r.scaled[0], r.readout.at[0])
    go("in0")
    vec_one(0, by_skip, by_bias, by_decay)
    go(PLAN[4])
    vec_three(1)
    keep_act.wait()
    give_act.wait_send()
    in_time(r.ig, r.leave.at[1])
    go(PLAN[5])
    slope0, by_bias_total0, by_gain_total0 = back_norm(3, 0)

    def last(rows, carry):
        live = wide(r.live[rows, :])
        upstream = r.ig[rows, :].astype(F32)
        grad = source_grad(0, rows, upstream, live, slope0, by_bias_total0, by_gain_total0)
        r.leave[0, rows, :] = t_mm(r.order[...], (live * grad).astype(BF16)).astype(BF16)
        return carry

    row_tiles(last, 0)
    keep_ig = pltpu.make_async_copy(r.leave.at[s], r.ig_out.at[s], r.local.at[6])
    keep_ig.start()
    give_ig = remote(r.leave.at[other], r.ig_out.at[s], r.far_send.at[5], r.far_recv.at[5], sibling)
    give_ig.start()

    go(PLAN[6])
    vec_two(0)
    go(PLAN[7])
    vec_three(0)
    give_vec = remote(r.vec_tot.at[other], r.vec_far, r.far_send.at[6], r.far_recv.at[6], sibling)
    give_vec.start()
    go(PLAN[8])
    give_vec.wait_recv()
    total = r.vec_tot[s] + r.vec_far[...]
    r.small[0:5, :] = total[0:5]
    grad_re, grad_im = total[5:6, :STATES], total[5:6, STATES:]
    grad_rate = total[6:7, :STATES] * jnp.exp(-double) / scale_sq - (grad_re * decay_re + grad_im * decay_im)
    r.small[5:6, :STATES] = grad_rate * rate
    r.small[5:6, STATES:] = (grad_im * decay_re - grad_re * decay_im) * phase
    r.small[6:8, :] = jnp.zeros((2, D), F32)

    for one in (3, 4, 5, 0, 1, 2):
        while sums_of[one].step() is not True:
            pass
    give_act.wait_recv()
    keep_ig.wait()
    give_ig.wait()
    give_vec.wait_send()
    send_prm.wait_send()
    for copy in send_w:
        copy.wait_send()
    for ph in range(4):
        over(1, peers, lambda k, ph=ph: to_all(ph, k).wait_send())
        over(1, ns, lambda k, ph=ph: to_seq(ph, k).wait_send())
    for b in range(2):
        over(1, ns, lambda k, b=b: vec_seq(b, k).wait_send())
        over(1, nd, lambda k, b=b: vec_dp(b, k).wait_send())


def results_kernel(
    tokens, act, ig, grads, small, o_act, o_ig, o_glu, o_out, o_in, o_gain, o_bias, o_nu, o_theta, o_skip, o_bglu,
    act_v, ig_v, ig_f, grads_v, grads_f, act_sem, ig_sem, grad_sem,
):
    copy = pltpu.make_async_copy
    act_in = [copy(act.at[i], act_v.at[i], act_sem.at[i, 0]) for i in range(MICRO)]
    ig_in = [copy(ig.at[i], ig_v.at[i], ig_sem.at[i, 0]) for i in range(MICRO)]
    parts = [pl.ds(GRAD_AT[i], GRAD_ROWS[i]) for i in (GLU, OUT, IN)]
    grads_in = [copy(grads.at[parts[i]], grads_v.at[parts[i]], grad_sem.at[i, 0]) for i in (GLU, OUT, IN)]
    for one in ig_in + grads_in + act_in:
        one.start()
    o_gain[...] = small[0:1, :]
    o_bias[...] = small[1:2, :]
    o_skip[...] = small[2:3, :]
    o_bglu[:, :D] = small[3:4, :]
    o_bglu[:, D:] = small[4:5, :]
    o_nu[...] = small[5:6, :STATES]
    o_theta[...] = small[5:6, STATES:]
    out = []

    def leave(src, dst, sem):
        out.append(copy(src, dst, sem))
        out[-1].start()

    for i in range(MICRO):
        ig_in[i].wait()

        def tile(j, carry, i=i):
            rows = pl.ds(pl.multiple_of(j * 64, 64), 64)
            ig_f[i, rows, :] = ig_v[i, rows, :].astype(F32)
            return carry

        lax.fori_loop(0, tokens // 64, tile, 0)
        leave(ig_f.at[i], o_ig.at[i], ig_sem.at[i, 1])
    for i, dst in ((GLU, o_glu), (OUT, o_out), (IN, o_in)):
        grads_in[i].wait()
        for c in range(GRAD_ROWS[i] // D):
            at = GRAD_AT[i] + c * D
            cols = slice(GRAD_AT[i] // 4 + c * LANES, GRAD_AT[i] // 4 + (c + 1) * LANES)
            grads_f[:, cols] = grads_v[at : at + D, :].astype(F32)
        leave(grads_f.at[:, GRAD_AT[i] // 4 : (GRAD_AT[i] + GRAD_ROWS[i]) // 4], dst, grad_sem.at[i, 1])
    for i in range(MICRO):
        act_in[i].wait()
        leave(act_v.at[i], o_act.at[i], act_sem.at[i, 1])
    for one in out:
        one.wait()


def body(ns, nd, inputs, mask, gain, bias, nu, theta, w_in, w_out, skip, w_glu, b_glu, cotangent):
    per = inputs.shape[0] // MICRO
    span = inputs.shape[1]
    tokens = per * span
    segs = tokens // SEG
    dma = pltpu.SemaphoreType.DMA
    vmem = pltpu.VMEM
    names_in = ["x", "cot", "mask", "gain", "bias", "nu", "theta", "skip", "bglu", "w_in", "w_out", "w_glu"]
    any_in = {"x", "cot", "w_in", "w_out", "w_glu"}
    outs = {
        "act_out": jax.ShapeDtypeStruct((MICRO, tokens, D), BF16),
        "ig_out": jax.ShapeDtypeStruct((MICRO, tokens, D), BF16),
        "grads": jax.ShapeDtypeStruct((ALL_ROWS, LANES), BF16),
        "small": jax.ShapeDtypeStruct((8, D), F32),
    }
    any_out = {"act_out", "ig_out", "grads"}
    half = ALL_ROWS // 2
    scratch = {
        "act": vmem((3, tokens, D), BF16),
        "cotv": vmem((tokens, D), BF16),
        "live": vmem((tokens, LANES), F32),
        "win": vmem((2, D, D), BF16),
        "wout": vmem((2, D, D), BF16),
        "wglu": vmem((2, D, 2 * D), BF16),
        "prm": vmem((2, 8, D), F32),
        "stat": vmem((2, 8, D), F32),
        "scaled": vmem((2, tokens, D), BF16),
        "u": vmem((2, 4, tokens, LANES), F32),
        "st": vmem((2, 4, tokens, LANES), F32),
        "start": vmem((2, 4, segs, LANES), F32),
        "readout": vmem((2, tokens, D), BF16),
        "active": vmem((2, tokens, D), BF16),
        "slope": vmem((2, tokens, D), F32),
        "gate": vmem((tokens, D), F32),
        "steep": vmem((tokens, D), F32),
        "gg": vmem((tokens, 2 * D), BF16),
        "gm": vmem((tokens, D), BF16),
        "adj": vmem((4, tokens, LANES), F32),
        "ig": vmem((tokens, D), BF16),
        "leave": vmem((2, tokens, D), BF16),
        "order": vmem((ROWS, ROWS), BF16),
        "bnb": vmem((4, ns * nd, 9, LANES), F32),
        "scb": vmem((4, ns, 4 * per, LANES), F32),
        "dw": vmem((2, ALL_ROWS, LANES), BF16),
        "sec": vmem((2, half, LANES), BF16),
        "half": vmem((2, half, LANES), BF16),
        "gat": vmem((2, half, LANES), BF16),
        "slots": vmem((slot_rows(ns, nd)[-1], LANES), BF16),
        "vec_a": vmem((2, ns, 8, D), F32),
        "vec_b": vmem((2, nd, 8, D), F32),
        "vec_tot": vmem((2, 8, D), F32),
        "vec_far": vmem((8, D), F32),
        "local": dma((7,)),
        "own": dma((6,)),
        "far_send": dma((7,)),
        "far_recv": dma((7,)),
        "bn_send": dma((4, ns * nd)),
        "bn_recv": dma((4, ns * nd)),
        "sc_send": dma((4, ns)),
        "sc_recv": dma((4, ns)),
        "core_send": dma((6,)),
        "core_recv": dma((6,)),
        "rs_send": dma((6, 3, max(ns, nd))),
        "rs_recv": dma((6, 3, max(ns, nd))),
        "ag_send": dma((6, 3, max(ns, nd))),
        "ag_recv": dma((6, 3, 2 * max(ns, nd))),
        "va_send": dma((2, ns)),
        "va_recv": dma((2, ns)),
        "vb_send": dma((2, nd)),
        "vb_recv": dma((2, nd)),
    }
    in_any = pl.BlockSpec(memory_space=pl.ANY)
    in_vmem = pl.BlockSpec(memory_space=pltpu.VMEM)
    names = names_in + list(outs) + list(scratch)
    act, ig, grads, small = pl.pallas_call(
        functools.partial(kernel, ns, nd, per, span, names),
        out_shape=list(outs.values()),
        in_specs=[in_any if name in any_in else in_vmem for name in names_in],
        out_specs=[in_any if name in any_out else in_vmem for name in outs],
        scratch_shapes=list(scratch.values()),
        compiler_params=pltpu.CompilerParams(
            collective_id=0, has_side_effects=True, vmem_limit_bytes=60 * 2**20
        ),
    )(
        inputs.reshape(MICRO, tokens, D),
        cotangent.reshape(MICRO, tokens, D),
        mask,
        gain,
        bias,
        nu,
        theta,
        skip,
        b_glu,
        w_in,
        w_out,
        w_glu,
    )

    wide_out = [(1, D), (1, D), (1, STATES), (1, STATES), (1, D), (1, 2 * D)]
    big_out = [((MICRO, tokens, D), BF16), ((MICRO, tokens, D), F32)]
    big_out += [((D, GRAD_ROWS[which] // 4), F32) for which in (GLU, OUT, IN)]
    act, ig, d_glu, d_out, d_in, d_gain, d_bias, d_nu, d_theta, d_skip, d_bglu = pl.pallas_call(
        functools.partial(results_kernel, tokens),
        out_shape=[jax.ShapeDtypeStruct(*x) for x in big_out] + [jax.ShapeDtypeStruct(x, F32) for x in wide_out],
        in_specs=[in_any] * 3 + [in_vmem],
        out_specs=[in_any] * 5 + [in_vmem] * 6,
        scratch_shapes=[
            vmem((MICRO, tokens, D), BF16),
            vmem((MICRO, tokens, D), BF16),
            vmem((MICRO, tokens, D), F32),
            vmem((ALL_ROWS, LANES), BF16),
            vmem((D, ALL_ROWS // 4), F32),
            dma((2, 2)),
            dma((2, 2)),
            dma((3, 2)),
        ],
        compiler_params=pltpu.CompilerParams(vmem_limit_bytes=60 * 2**20),
    )(act, ig, grads, small)
    whole = (1, MICRO * per, span, D)
    return (
        act.reshape(whole),
        ig.reshape(whole),
        d_gain,
        d_bias,
        d_nu,
        d_theta,
        d_in[None],
        d_out[None],
        d_skip,
        d_glu[None],
        d_bglu,
    )


def solution(mesh):
    rows = P("section", None)
    cube = P("section", None, None)
    tokens = P("dp", "seq", None)
    spread = P("section", "dp", "seq", None)
    in_specs = (tokens, P("dp", "seq"), rows, rows, rows, rows, cube, cube, rows, cube, rows, tokens)
    out_specs = (spread, spread, rows, rows, rows, rows, cube, cube, rows, cube, rows)
    return jax.shard_map(
        functools.partial(body, mesh.shape["seq"], mesh.shape["dp"]),
        mesh=mesh,
        in_specs=in_specs,
        out_specs=out_specs,
        check_vma=False,
    )
```

```python
import functools
import math
import types

import jax
import jax.numpy as jnp
from jax import lax
from jax.experimental import pallas as pl
from jax.experimental.pallas import tpu as pltpu
from jax.sharding import PartitionSpec as P

D = 512
STATES = 256
MICRO = 2
EPS = 1e-05
LANES = 128
ROWS = 256
SEG = 32
EIGHT = 8
GLU, OUT, IN = 0, 1, 2
GRAD_ROWS = (4096, 2048, 2048)
GRAD_AT = (0, 4096, 6144)
ALL_ROWS = 8192
SD = ("seq", "dp")
DS = ("dp", "seq")
PARTS = (
    ((0, 2048, SD), (2048, 2048, SD),),
    ((0, 2048, SD),),
    ((0, 1024, SD), (1024, 1024, DS),),
    ((0, 4096, SD),),
    ((0, 2048, SD),),
    ((0, 1024, SD), (1024, 1024, DS),),
)
FLAT = tuple((n, *part) for n, parts in enumerate(PARTS) for part in parts)
DEPTH = max(len(part[-1]) for part in FLAT)
PLAN = {
    "carry two": (104, 103, 6),
    "filled two": (),
    "norm two": (5, 105, 6, 7, 8),
    "through": (),
    "carry one": (200, 100, 6, 5, 7),
    "filled one": (0, 8, 1, 102),
    "norm one": (3, 101, 4, 6, 2, 5, 0, 8, 7),
    "last": (201, 1, 4, 3),
    "end": (5, 0, 2, 4, 3, 1, 7, 8, 0, 2, 3, 202, 4, 1, 2),
}
ROOT = math.sqrt(2.0 / math.pi)
CUBE = 0.044715

F32 = jnp.float32
BF16 = jnp.bfloat16
MESH = pl.DeviceIdType.MESH


def mm(a, b):
    return lax.dot_general(a, b, (((1,), (0,)), ((), ())), preferred_element_type=F32)


def mm_t(a, b):
    return lax.dot_general(a, b, (((1,), (1,)), ((), ())), preferred_element_type=F32)


def t_mm(a, b):
    return lax.dot_general(a, b, (((0,), (0,)), ((), ())), preferred_element_type=F32)


def complex_mul(ar, ai, br, bi):
    return ar * br - ai * bi, ar * bi + ai * br


def power(re, im, n):
    out = None
    while n:
        if n & 1:
            out = (re, im) if out is None else complex_mul(*out, re, im)
        n >>= 1
        if n:
            re, im = complex_mul(re, im, re, im)
    return out


def as_row(four):
    return jnp.concatenate([four[c : c + 1] for c in range(4)], axis=1)


def wide(tile):
    return jnp.concatenate([tile] * 4, axis=1)


def column_sum(x):
    return jnp.sum(x, axis=0, keepdims=True)


def slots_of(rows, counts, spread):
    out, start = [], 0
    for level, count in enumerate(counts):
        size = rows if spread and level == len(counts) - 1 else rows // count
        out.append((start, size))
        start += count * size
        rows //= count
    return out


def slot_rows(ns, nd):
    inner = next(n for n in range(math.isqrt(ns), 0, -1) if ns % n == 0)
    sizes = {"seq": ns, "dp": nd, "in": inner, "out": ns // inner}
    bases = [0]
    for _, _, rows, order in FLAT:
        counts = [sizes[name] for name in order]
        spread = rows // 2 // math.prod(counts) % 16 != 0
        start, size = slots_of(rows // 2, counts, spread)[-1]
        bases.append(bases[-1] + start + counts[-1] * size)
    return bases


def kernel(ns, nd, per, span, names, *refs):
    r = types.SimpleNamespace(**dict(zip(names, refs)))
    tokens = per * span
    segs = tokens // SEG
    nseg = span // SEG
    tiles = tokens // ROWS
    blocks = segs // EIGHT
    peers = ns * nd
    s = lax.axis_index("section")
    d = lax.axis_index("dp")
    q = lax.axis_index("seq")
    other = 1 - s
    me = d * ns + q
    sibling = {"section": other}

    def seq_peer(k):
        return {"seq": lax.rem(q + k, ns)}

    def dp_peer(k):
        return {"dp": lax.rem(d + k, nd)}

    def any_peer(k):
        at = lax.rem(me + k, peers)
        return {"dp": at // ns, "seq": lax.rem(at, ns)}

    def remote(src, dst, send, recv, device):
        return pltpu.make_async_remote_copy(
            src_ref=src, dst_ref=dst, send_sem=send, recv_sem=recv, device_id=device, device_id_type=MESH
        )

    def over(low, high, body):
        lax.fori_loop(low, high, lambda k, c: (body(k), c)[1], 0)

    arriving = {}
    leaving = {}

    def begin(key, start, whole):
        start()
        arriving[key] = leaving[key] = whole

    def arrive(key):
        arriving.pop(key).wait_recv()

    def leave(key):
        leaving.pop(key).wait_send()

    def end_all():
        for key in list(arriving):
            arrive(key)
        for key in list(leaving):
            leave(key)

    def alone(key, copy):
        begin(key, copy.start, copy)

    def row_tiles(body, init):
        def step(i, carry):
            return body(pl.ds(pl.multiple_of(i * ROWS, ROWS), ROWS), carry)

        return lax.fori_loop(0, tiles, step, init, unroll=4)

    slot_base = slot_rows(ns, nd)

    barrier = pltpu.get_barrier_semaphore()

    def greet(device):
        pl.semaphore_signal(barrier, inc=1, device_id=device, device_id_type=MESH)

    greet(sibling)
    over(1, peers, lambda k: greet(any_peer(k)))
    over(1, ns, lambda k: greet({"section": other, **seq_peer(k)}))
    over(1, nd, lambda k: greet({"section": other, **dp_peer(k)}))

    load_x = pltpu.make_async_copy(r.x.at[s], r.act.at[0], r.local.at[0])
    load_x.start()
    load_cot = pltpu.make_async_copy(r.cot.at[s], r.cotv, r.local.at[1])
    weights = ((r.w_in, r.win), (r.w_out, r.wout), (r.w_glu, r.wglu))
    load_w = [
        pltpu.make_async_copy(src.at[0], dst.at[s], r.local.at[2 + i]) for i, (src, dst) in enumerate(weights)
    ]
    for copy in load_w:
        copy.start()
    load_cot.start()

    rate = jnp.exp(r.nu[...])
    phase = jnp.exp(r.theta[...])
    size = jnp.exp(-rate)
    decay_re = size * jnp.cos(phase)
    decay_im = size * jnp.sin(phase)
    double = 2.0 * rate
    scale_sq = double * (
        1.0
        - double / 2.0 * (1.0 - double / 3.0 * (1.0 - double / 4.0 * (1.0 - double / 5.0 * (1.0 - double / 6.0))))
    )
    scale = jnp.sqrt(scale_sq)
    r.prm[s, 0:1, :] = r.gain[...]
    r.prm[s, 1:2, :] = r.bias[...]
    r.prm[s, 2:3, :] = r.skip[...]
    r.prm[s, 3:4, :] = r.bglu[:, :D]
    r.prm[s, 4:5, :] = r.bglu[:, D:]
    r.prm[s, 5:6, :] = jnp.concatenate([decay_re, decay_im], axis=1)
    r.prm[s, 6:7, :] = jnp.concatenate([scale, scale], axis=1)
    r.prm[s, 7:8, :] = jnp.zeros((1, D), F32)

    count = jnp.zeros((1, 1), F32)
    row = lax.broadcasted_iota(jnp.int32, (tokens, LANES), 0)
    token = (row & -ROWS) + (row & (EIGHT - 1)) * SEG + ((row & (ROWS - 1)) >> (EIGHT.bit_length() - 1))
    live = jnp.zeros((tokens, LANES), F32)
    for i in range(per):
        here = jnp.sum(r.mask[pl.ds(s * per + i, 1), :], axis=1, keepdims=True)
        live = jnp.where((token >= i * span) & (token < i * span + here), 1.0, live)
        count = count + here.astype(F32)
    r.live[...] = live
    count_row = jnp.broadcast_to(count, (1, LANES))
    to_row = lax.broadcasted_iota(jnp.int32, (ROWS, ROWS), 0)
    from_row = lax.broadcasted_iota(jnp.int32, (ROWS, ROWS), 1)
    came_from = (to_row & (EIGHT - 1)) * SEG + (to_row >> (EIGHT.bit_length() - 1))
    r.order[...] = jnp.where(from_row == came_from, 1.0, 0.0).astype(BF16)
    load_x.wait()

    def mask_input(rows, total):
        x = mm(r.order[...], r.act[0, rows, :]) * wide(r.live[rows, :])
        r.act[0, rows, :] = x.astype(BF16)
        return total + column_sum(x)

    def centred(b, mean):
        def tile(rows, total):
            off = (r.act[b, rows, :].astype(F32) - mean) * wide(r.live[rows, :])
            return total + column_sum(off * off)

        return row_tiles(tile, jnp.zeros((1, D), F32))

    def put_rows(ph, upper, lower):
        for c in range(4):
            r.bnb[ph, me, c : c + 1, :] = upper[:, c * LANES : (c + 1) * LANES]
            r.bnb[ph, me, 4 + c : 5 + c, :] = lower[:, c * LANES : (c + 1) * LANES]
        r.bnb[ph, me, 8:9, :] = count_row

    def to_all(ph, k):
        block = r.bnb.at[ph, me]
        return remote(block, block, r.bn_send.at[ph], r.bn_recv.at[ph], any_peer(k))

    def send_all(ph):
        blocks = r.bnb.at[ph, pl.ds(0, peers - 1)]
        whole = remote(blocks, blocks, r.bn_send.at[ph], r.bn_recv.at[ph], sibling)
        begin(("all", ph), lambda: over(1, peers, lambda k: to_all(ph, k).start()), whole)

    def wait_all(ph):
        arrive(("all", ph))

    def norm_sums(b, total):
        mean = total / jnp.maximum(wide(count_row), 1.0)
        put_rows(b, mean, centred(b, mean))

    def norm_merge(b):
        wait_all(b)
        got = r.bnb[b]
        means, spreads, counts = got[:, 0:4, :], got[:, 4:8, :], got[:, 8:9, :]
        valid = jnp.sum(counts, axis=0)
        mean = jnp.sum(counts * means, axis=0) / valid
        apart = means - mean[None]
        spread = jnp.sum(spreads + counts * apart * apart, axis=0)
        r.stat[b, 0:1, :] = as_row(mean)
        r.stat[b, 1:2, :] = as_row(lax.rsqrt(spread / valid + EPS))
        r.stat[b, 2:3, :] = wide(valid)

    norm_sums(0, row_tiles(mask_input, jnp.zeros((1, D), F32)))

    pl.semaphore_wait(barrier, peers + ns - 1 + nd - 1)
    send_all(0)
    send_prm = remote(r.prm.at[s], r.prm.at[s], r.far_send.at[0], r.far_recv.at[0], sibling)
    send_w = [
        remote(src.at[0], dst.at[s], r.far_send.at[1 + i], r.far_recv.at[1 + i], sibling)
        for i, (src, dst) in enumerate(weights)
    ]

    alone("prm", send_prm)
    for i, copy in enumerate(send_w):
        alone(("w", i), copy)

    def decay(b, sign):
        out = []
        for c in range(2):
            re = r.prm[b, 5:6, c * LANES : (c + 1) * LANES]
            im = r.prm[b, 5:6, STATES + c * LANES : STATES + (c + 1) * LANES]
            out.append((re, sign * im))
        return out

    def step_rows(k, l):
        return pl.ds(pl.multiple_of(k * ROWS + l * EIGHT, EIGHT), EIGHT)

    def at_step(ref, l):
        return jnp.concatenate([ref[step_rows(k, l), :] for k in range(blocks)], axis=0)

    def put_step(ref, l, value):
        for k in range(blocks):
            ref[step_rows(k, l), :] = value[k * EIGHT : (k + 1) * EIGHT]

    def advance(a, state, drive):
        return (
            a[0] * state[0] - a[1] * state[1] + drive[0],
            a[1] * state[0] + a[0] * state[1] + drive[1],
        )

    place = lax.rem(lax.broadcasted_iota(jnp.int32, (segs, LANES), 0), nseg)
    owner = lax.broadcasted_iota(jnp.int32, (segs, LANES), 0) // nseg

    def moved(x, k, reverse):
        if reverse:
            return jnp.where(place < nseg - k, pltpu.roll(x, segs - k, 0), 0.0)
        return jnp.where(place >= k, pltpu.roll(x, k, 0), 0.0)

    def seg_scan(re, im, jump, reverse):
        k = 1
        while k < nseg:
            add_re, add_im = complex_mul(*jump, moved(re, k, reverse), moved(im, k, reverse))
            re, im = re + add_re, im + add_im
            jump = complex_mul(*jump, *jump)
            k *= 2
        return re, im

    def to_seq(ph, k):
        block = r.scb.at[ph, q]
        return remote(block, block, r.sc_send.at[ph], r.sc_recv.at[ph], seq_peer(k))

    def carry(ph, drive, a, reverse, between):
        def step(i, states):
            l = SEG - 1 - i if reverse else i
            return tuple(
                advance(a[c], states[c], (at_step(drive.at[c], l), at_step(drive.at[2 + c], l))) for c in range(2)
            )

        zero = jnp.zeros((segs, LANES), F32)
        ends = lax.fori_loop(0, SEG, step, ((zero, zero), (zero, zero)), unroll=4)
        jumps = [power(*a[c], SEG) for c in range(2)]
        sums = [seg_scan(*ends[c], jumps[c], reverse) for c in range(2)]
        for i in range(per):
            last = i * nseg if reverse else (i + 1) * nseg - 1
            for c in range(2):
                r.scb[ph, q, 4 * i + c : 4 * i + c + 1, :] = sums[c][0][last : last + 1]
                r.scb[ph, q, 4 * i + 2 + c : 4 * i + 3 + c, :] = sums[c][1][last : last + 1]
        ends_of = r.scb.at[ph, pl.ds(0, ns - 1)]
        whole = remote(ends_of, ends_of, r.sc_send.at[ph], r.sc_recv.at[ph], sibling)
        begin(("seq", ph), lambda: over(1, ns, lambda k: to_seq(ph, k).start()), whole)
        first = jnp.where(place == (nseg - 1 if reverse else 0), 1.0, 0.0)
        reach = [seg_scan(first, zero, jumps[c], reverse) for c in range(2)]
        between()
        arrive(("seq", ph))
        starts = []
        for c in range(2):
            far = power(*a[c], span)
            entering = []
            for i in range(per):
                re = jnp.zeros((1, LANES), F32)
                im = jnp.zeros((1, LANES), F32)
                for lap in range(ns):
                    j = ns - 1 - lap if reverse else lap
                    before = j > q if reverse else j < q
                    new_re, new_im = advance(
                        far,
                        (re, im),
                        (r.scb[ph, j, 4 * i + c : 4 * i + c + 1, :], r.scb[ph, j, 4 * i + 2 + c : 4 * i + 3 + c, :]),
                    )
                    re = jnp.where(before, new_re, re)
                    im = jnp.where(before, new_im, im)
                entering.append((re, im))
            in_re = jnp.broadcast_to(entering[0][0], (segs, LANES))
            in_im = jnp.broadcast_to(entering[0][1], (segs, LANES))
            for i in range(1, per):
                in_re = jnp.where(owner == i, entering[i][0], in_re)
                in_im = jnp.where(owner == i, entering[i][1], in_im)
            add_re, add_im = complex_mul(*reach[c], in_re, in_im)
            starts.append((moved(sums[c][0], 1, reverse) + add_re, moved(sums[c][1], 1, reverse) + add_im))
        return starts

    def fill_states(b, starts, a, reverse):
        for c in range(2):
            r.start[b, c] = starts[c][0]
            r.start[b, 2 + c] = starts[c][1]

        def step(i, states):
            l = SEG - 1 - i if reverse else i
            out = []
            for c in range(2):
                new = advance(a[c], states[c], (at_step(r.u.at[b, c], l), at_step(r.u.at[b, 2 + c], l)))
                put_step(r.st.at[b, c], l, new[0])
                put_step(r.st.at[b, 2 + c], l, new[1])
                out.append(new)
            return tuple(out)

        lax.fori_loop(0, SEG, step, tuple(starts), unroll=4)

    def fill_adjoint(b, starts, a, reverse):
        back = 1 if not reverse else -1
        zero = jnp.zeros((segs, LANES), F32)
        sums = []
        for c in range(2):
            scale_c = r.prm[b, 6:7, c * LANES : (c + 1) * LANES]

            def one(l, prior, carry, c=c, scale_c=scale_c):
                state, by_re, by_im, by_scale = carry
                re, im = advance(a[c], state, (at_step(r.adj.at[c], l), at_step(r.adj.at[2 + c], l)))
                put_step(r.adj.at[c], l, scale_c * re)
                put_step(r.adj.at[2 + c], l, scale_c * im)
                by_re = by_re + (re * prior[0] + im * prior[1])
                by_im = by_im + (im * prior[0] - re * prior[1])
                by_scale = by_scale + (re * at_step(r.u.at[b, c], l) + im * at_step(r.u.at[b, 2 + c], l))
                return (re, im), by_re, by_im, by_scale

            def step(i, carry, c=c, one=one):
                l = SEG - 1 - i if reverse else i
                prior = (at_step(r.st.at[b, c], l + back), at_step(r.st.at[b, 2 + c], l + back))
                return one(l, prior, carry)

            carry_c = lax.fori_loop(0, SEG - 1, step, (starts[c], zero, zero, zero), unroll=4)
            final = one(0 if reverse else SEG - 1, (r.start[b, c], r.start[b, 2 + c]), carry_c)
            sums.append([column_sum(x) for x in final[1:]])
        return [jnp.concatenate([sums[0][i], sums[1][i]], axis=1) for i in range(3)]

    def forward_in(b):
        gain, bias, scale_row = r.prm[b, 0:1, :], r.prm[b, 1:2, :], r.prm[b, 6:7, :]
        average = r.stat[b, 0:1, :]
        slope = r.stat[b, 1:2, :] * gain

        def tile(rows, carry):
            x = r.act[b, rows, :].astype(F32)
            scaled = (wide(r.live[rows, :]) * ((x - average) * slope + bias)).astype(BF16)
            r.scaled[b, rows, :] = scaled
            u = mm(scaled, r.win[b]) * scale_row
            for c in range(4):
                r.u[b, c, rows, :] = u[:, c * LANES : (c + 1) * LANES]
            return carry

        row_tiles(tile, 0)

    def forward_out(b, finish, init):
        skip = r.prm[b, 2:3, :]
        value_bias, gate_bias = r.prm[b, 3:4, :], r.prm[b, 4:5, :]

        def tile(rows, carry):
            readout = jnp.concatenate([r.st[b, c, rows, :] for c in range(4)], axis=1).astype(BF16)
            r.readout[b, rows, :] = readout
            mixed = mm(readout, r.wout[b]) + skip * r.scaled[b, rows, :].astype(F32)
            square = mixed * mixed
            t = jnp.tanh(ROOT * mixed * (1.0 + CUBE * square))
            half = 0.5 + 0.5 * t
            active = (mixed * half).astype(BF16)
            r.active[b, rows, :] = active
            r.slope[b, rows, :] = half + (0.5 * ROOT) * mixed * (1.0 - t * t) * (1.0 + (3.0 * CUBE) * square)
            gated = mm(active, r.wglu[b])
            gate = 0.5 + 0.5 * jnp.tanh(0.5 * (gated[:, D:] + gate_bias))
            product = (gated[:, :D] + value_bias) * gate
            live = wide(r.live[rows, :])
            result = (r.act[b, rows, :].astype(F32) + live * product).astype(BF16)
            r.act[b + 1, rows, :] = result
            return finish(rows, live, gate, product * (1.0 - gate), result, carry)

        return row_tiles(tile, init)

    def back_tile(b, rows, outer, gate, steep, carry):
        grad_gated = jnp.concatenate([outer * gate, outer * steep], axis=1).astype(BF16)
        r.gg[rows, :] = grad_gated
        grad_mixed = (r.slope[b, rows, :] * mm_t(grad_gated, r.wglu[b])).astype(BF16)
        r.gm[rows, :] = grad_mixed
        grad_readout = mm_t(grad_mixed, r.wout[b])
        for c in range(4):
            r.adj[c, rows, :] = grad_readout[:, c * LANES : (c + 1) * LANES]
        by_skip = column_sum(grad_mixed.astype(F32) * r.scaled[b, rows, :].astype(F32))
        return carry[0] + by_skip, carry[1] + column_sum(grad_gated.astype(F32))

    def normed(b, rows):
        return (r.act[b, rows, :].astype(F32) - r.stat[b, 0:1, :]) * r.stat[b, 1:2, :]

    projected_grads = (r.cotv, r.ig)

    def round_adjoint(b):
        def tile(rows, carry):
            adjoint = jnp.concatenate([r.adj[c, rows, :] for c in range(4)], axis=1)
            projected_grads[b][rows, :] = adjoint.astype(BF16)
            return carry

        row_tiles(tile, 0)

    def back_in(b):
        skip = r.prm[b, 2:3, :]

        def tile(rows, carry):
            grad_scaled = skip * r.gm[rows, :].astype(F32) + mm_t(projected_grads[b][rows, :], r.win[b])
            masked = wide(r.live[rows, :]) * grad_scaled
            r.slope[b, rows, :] = masked
            return carry[0] + column_sum(masked * normed(b, rows)), carry[1] + column_sum(masked)

        zero = jnp.zeros((1, D), F32)
        return row_tiles(tile, (zero, zero))

    def back_norm(ph, b):
        wait_all(ph)
        got = jnp.sum(r.bnb[ph], axis=0)
        gain_total, bias_total = as_row(got[0:4]), as_row(got[4:8])
        r.vec_tot[b, 0:1, :] = gain_total
        r.vec_tot[b, 1:2, :] = bias_total
        slope = r.stat[b, 1:2, :] * r.prm[b, 0:1, :]
        per_token = slope / r.stat[b, 2:3, :]
        return slope, per_token * bias_total, per_token * gain_total

    def source_grad(b, rows, upstream, live, slope, by_bias, by_gain):
        return upstream + live * (slope * r.slope[b, rows, :] - by_bias - normed(b, rows) * by_gain)

    def weight_grad(b, which, left, right):
        columns = GRAD_ROWS[which] // 4

        def tile(j, carry):
            cols = pl.ds(pl.multiple_of(j * 256, 256), 256)
            grad = t_mm(left, right[:, cols]).astype(BF16)
            at = pl.multiple_of(GRAD_AT[which] + j * 1024, 1024)
            r.dw[b, pl.ds(at, 512), :] = grad[:, :LANES]
            r.dw[b, pl.ds(at + 512, 512), :] = grad[:, LANES:]
            return carry

        lax.fori_loop(0, columns // 256, tile, 0, unroll=2)

    inner = next(n for n in range(math.isqrt(ns), 0, -1) if ns % n == 0)
    outer = ns // inner
    q_out, q_in = q // inner, lax.rem(q, inner)
    axes = {
        "seq": (ns, q, seq_peer),
        "dp": (nd, d, dp_peer),
        "in": (inner, q_in, lambda k: {"seq": q_out * inner + lax.rem(q_in + k, inner)}),
        "out": (outer, q_out, lambda k: {"seq": lax.rem(q_out + k, outer) * inner + q_in}),
    }

    results = []

    class Reduced:
        def __init__(self, n):
            which, start, rows, order = FLAT[n]
            self.b, self.n, self.at = which // 3, n, GRAD_AT[which % 3] + start
            self.base = self.at // 2
            self.axes = [axes[name] for name in order]
            self.sizes, self.offsets = [rows // 2], [0]
            for count, index, _ in self.axes:
                self.sizes.append(self.sizes[-1] // count)
                self.offsets.append(self.offsets[-1] + index * self.sizes[-1])
            self.spread = self.sizes[-1] % 16 != 0
            self.slots = slots_of(rows // 2, [count for count, _, _ in self.axes], self.spread)
            self.slot_base = slot_base[self.n]
            self.steps = self.plan()

        def rows(self, offset, size):
            return pl.ds(pl.multiple_of(self.base + offset, 16), size)

        def to_core(self):
            size = self.sizes[0]
            src = r.dw.at[self.b, pl.ds(pl.multiple_of(self.at + other * size, 16), size)]
            return remote(src, r.sec.at[self.b, self.rows(0, size)], r.core_send.at[self.n], r.core_recv.at[self.n], sibling)

        def slot(self, level, index):
            start, size = self.slots[level]
            return pl.ds(pl.multiple_of(self.slot_base + start + index * size, 16), size)

        def scatter(self, level, k):
            count, index, peer = self.axes[level]
            if self.spread and level == len(self.axes) - 1:
                src = r.slots.at[self.slot(level, index)]
            else:
                size = self.sizes[level + 1]
                src = r.half.at[self.b, self.rows(self.offsets[level] + lax.rem(index + k, count) * size, size)]
            dst = r.slots.at[self.slot(level, index)]
            return remote(src, dst, r.rs_send.at[self.n, level], r.rs_recv.at[self.n, level], peer(k))

        def gather(self, level, k):
            block = r.gat.at[self.b, self.rows(self.offsets[level + 1], self.sizes[level + 1])]
            return remote(block, block, r.ag_send.at[self.n, level], r.ag_recv.at[self.n, level], self.axes[level][2](k))

        def place(self):
            return pl.ds(pl.multiple_of(self.at + s * self.sizes[0] + self.offsets[1], 16), self.sizes[1])

        def result(self, device, send):
            src = r.gat.at[self.b, self.rows(self.offsets[1], self.sizes[1])]
            target = {"section": self.b, **device}
            return remote(src, r.grads.at[self.place()], send, r.ag_recv.at[self.n, 0], target)

        def results_whole(self, parts):
            rows = r.grads.at[pl.ds(0, parts * self.sizes[1])]
            return remote(rows, rows, r.ag_send.at[self.n, 0], r.ag_recv.at[self.n, 0], sibling)

        def own(self):
            src = r.gat.at[self.b, self.rows(self.offsets[1], self.sizes[1])]
            return pltpu.make_async_copy(src, r.grads.at[self.place()], r.own.at[self.n])

        def across(self):
            return self.result({}, r.own.at[self.n])

        def each(self, level, body):
            over(1, self.axes[level][0], body)

        def first(self):
            size = self.sizes[0]
            arrive((self.n, "core"))
            mine = r.dw[self.b, pl.ds(pl.multiple_of(self.at + s * size, 16), size), :].astype(F32)
            there = r.sec[self.b, self.base : self.base + size, :].astype(F32)
            r.half[self.b, self.base : self.base + size, :] = (mine + there).astype(BF16)

        def collect(self, level):
            arrive((self.n, "scatter", level))
            count, index, _ = self.axes[level]
            last = level == len(self.axes) - 1
            if self.spread and last:
                total = sum(r.slots[self.slot(level, j), :].astype(F32) for j in range(count))
                r.gat[self.b, self.rows(self.offsets[level], self.sizes[level]), :] = total.astype(BF16)
                return
            here = self.rows(self.offsets[level + 1], self.sizes[level + 1])
            total = r.half[self.b, here, :].astype(F32)
            for k in range(1, count):
                total = total + r.slots[self.slot(level, lax.rem(index + k, count)), :].astype(F32)
            (r.gat if last else r.half)[self.b, here, :] = total.astype(BF16)

        def send(self, level):
            if self.spread and level == len(self.axes) - 1:
                here = self.rows(self.offsets[level], self.sizes[level])
                r.slots[self.slot(level, self.axes[level][1]), :] = r.half[self.b, here, :]
            start, size = self.slots[level]
            rows = r.slots.at[pl.ds(self.slot_base + start, (self.axes[level][0] - 1) * size)]
            whole = remote(rows, rows, r.rs_send.at[self.n, level], r.rs_recv.at[self.n, level], sibling)
            begin((self.n, "scatter", level), lambda: self.each(level, lambda k: self.scatter(level, k).start()), whole)

        def share(self, level):
            count, _, peer = self.axes[level]
            if level:
                rows = r.gat.at[self.b, pl.ds(self.base, (count - 1) * self.sizes[level + 1])]
                whole = remote(rows, rows, r.ag_send.at[self.n, level], r.ag_recv.at[self.n, level], sibling)
                begin((self.n, "gather", level), lambda: self.each(level, lambda k: self.gather(level, k).start()), whole)
                return
            self.each(0, lambda k: self.result(peer(k), r.ag_send.at[self.n, 0]).start())

            @pl.when(s == self.b)
            def _():
                self.own().start()

            @pl.when(s != self.b)
            def _():
                self.across().start()

            results.append(self)

        def finish(self):
            count = self.axes[0][0]

            @pl.when(s == self.b)
            def _():
                self.own().wait()
                self.results_whole(2 * count - 1).wait_recv()

            @pl.when(s != self.b)
            def _():
                self.across().wait_send()

            if count > 1:
                self.results_whole(count - 1).wait_send()

        def plan(self):
            depth = len(self.axes)
            top = depth - 2 if self.spread else depth - 1
            yield alone((self.n, "core"), self.to_core())
            self.first()
            yield self.send(0)
            for level in range(1, depth):
                self.collect(level - 1)
                yield self.send(level)
            self.collect(depth - 1)
            yield self.share(top)
            for level in range(top, 0, -1):
                arrive((self.n, "gather", level))
                yield self.share(level - 1)

        def step(self):
            return next(self.steps, True)

    sums_of = [Reduced(n) for n in range(len(FLAT))]

    factors = ((r.active, (r.gg, r.gg)), (r.readout, (r.gm, r.gm)), (r.scaled, projected_grads))

    def go(gap):
        for n in PLAN[gap]:
            if n < 100:
                sums_of[n].step()
                continue
            if n >= 200:
                vec_steps[n - 200]()
                continue
            b, which = (n - 100) // 3, (n - 100) % 3
            left, right = factors[which]
            weight_grad(b, which, left[b], right[b])
            for one, part in zip(sums_of, FLAT):
                if part[0] == n - 100:
                    one.step()

    def vec_seq(b, k):
        block = r.vec_a.at[b, q]
        return remote(block, block, r.va_send.at[b], r.va_recv.at[b], seq_peer(k))

    def vec_dp(b, k):
        block = r.vec_b.at[b, d]
        return remote(block, block, r.vb_send.at[b], r.vb_recv.at[b], dp_peer(k))

    def vec_one(b, by_skip, by_bias, by_decay):
        zero = jnp.zeros((1, D), F32)
        r.vec_a[b, q, 0:1, :] = zero
        r.vec_a[b, q, 1:2, :] = zero
        r.vec_a[b, q, 2:3, :] = by_skip
        r.vec_a[b, q, 3:4, :] = by_bias[:, :D]
        r.vec_a[b, q, 4:5, :] = by_bias[:, D:]
        r.vec_a[b, q, 5:6, :] = jnp.concatenate([by_decay[0], by_decay[1]], axis=1)
        r.vec_a[b, q, 6:7, :] = jnp.concatenate([by_decay[2], by_decay[2]], axis=1)
        r.vec_a[b, q, 7:8, :] = zero
        rows = r.vec_a.at[b, pl.ds(0, ns - 1)]
        whole = remote(rows, rows, r.va_send.at[b], r.va_recv.at[b], sibling)
        begin(("vec_seq", b), lambda: over(1, ns, lambda k: vec_seq(b, k).start()), whole)

    def vec_two(b):
        arrive(("vec_seq", b))
        r.vec_b[b, d] = jnp.sum(r.vec_a[b], axis=0)
        rows = r.vec_b.at[b, pl.ds(0, nd - 1)]
        whole = remote(rows, rows, r.vb_send.at[b], r.vb_recv.at[b], sibling)
        begin(("vec_dp", b), lambda: over(1, nd, lambda k: vec_dp(b, k).start()), whole)

    def vec_three(b):
        arrive(("vec_dp", b))
        total = jnp.sum(r.vec_b[b], axis=0)
        r.vec_tot[b, 2:8, :] = total[2:8]

    def vec_last():
        vec_three(1)
        vec_three(0)
        alone("vec", remote(r.vec_tot.at[other], r.vec_far, r.far_send.at[6], r.far_recv.at[6], sibling))

    vec_steps = (lambda: vec_two(1), lambda: vec_two(0), vec_last)

    arrive("prm")
    for i in range(3):
        load_w[i].wait()
        arrive(("w", i))
    load_cot.wait()

    def order_cot(rows, carry):
        r.cotv[rows, :] = mm(r.order[...], r.cotv[rows, :]).astype(BF16)
        return carry

    row_tiles(order_cot, 0)

    def in_time(src, dst):
        def tile(rows, carry):
            dst[rows, :] = t_mm(r.order[...], src[rows, :]).astype(BF16)
            return carry

        row_tiles(tile, 0)

    zero_row = jnp.zeros((1, D), F32)

    def nothing():
        pass

    norm_merge(0)
    forward_in(0)
    ahead0, ahead1 = decay(0, 1.0), decay(1, 1.0)
    starts = carry(0, r.u.at[0], ahead0, False, nothing)
    fill_states(0, starts, ahead0, False)

    def finish_one(rows, live, gate, steep, result, carry):
        r.gate[rows, :] = gate
        r.steep[rows, :] = steep
        return carry + column_sum(result.astype(F32))

    norm_sums(1, forward_out(0, finish_one, zero_row))
    send_all(1)
    in_time(r.act.at[1], r.leave.at[0])
    norm_merge(1)
    forward_in(1)
    starts = carry(1, r.u.at[1], ahead1, True, nothing)
    fill_states(1, starts, ahead1, True)

    def finish_two(rows, live, gate, steep, result, carry):
        return back_tile(1, rows, live * r.cotv[rows, :].astype(F32), gate, steep, carry)

    wide_zero = jnp.zeros((1, 2 * D), F32)
    by_skip, by_bias = forward_out(1, finish_two, (zero_row, wide_zero))

    keep_act = pltpu.make_async_copy(r.leave.at[s], r.act_out.at[s], r.local.at[5])
    give_act = remote(r.leave.at[other], r.act_out.at[s], r.far_send.at[4], r.far_recv.at[4], sibling)

    back0, back1 = decay(0, -1.0), decay(1, -1.0)

    def first_pieces():
        go("carry two")
        in_time(r.act.at[2], r.leave.at[1])
        keep_act.start()
        alone("act", give_act)

    starts = carry(2, r.adj, back1, False, first_pieces)
    by_decay = fill_adjoint(1, starts, back1, False)
    round_adjoint(1)
    go("filled two")
    put_rows(2, *back_in(1))
    send_all(2)
    vec_one(1, by_skip, by_bias, by_decay)
    go("norm two")
    slope, by_bias_total, by_gain_total = back_norm(2, 1)

    def through(rows, carry):
        live = wide(r.live[rows, :])
        upstream = r.cotv[rows, :].astype(F32)
        grad = source_grad(1, rows, upstream, live, slope, by_bias_total, by_gain_total).astype(BF16)
        r.ig[rows, :] = grad
        return back_tile(0, rows, live * grad.astype(F32), r.gate[rows, :], r.steep[rows, :], carry)

    by_skip, by_bias = row_tiles(through, (zero_row, wide_zero))
    go("through")

    def next_pieces():
        go("carry one")

    starts = carry(3, r.adj, back0, True, next_pieces)
    by_decay = fill_adjoint(0, starts, back0, True)
    round_adjoint(0)
    go("filled one")
    put_rows(3, *back_in(0))
    send_all(3)
    vec_one(0, by_skip, by_bias, by_decay)
    go("norm one")
    keep_act.wait()
    leave("act")
    in_time(r.ig, r.leave.at[1])
    slope0, by_bias_total0, by_gain_total0 = back_norm(3, 0)

    def last(rows, carry):
        live = wide(r.live[rows, :])
        upstream = r.ig[rows, :].astype(F32)
        grad = source_grad(0, rows, upstream, live, slope0, by_bias_total0, by_gain_total0)
        r.leave[0, rows, :] = t_mm(r.order[...], (live * grad).astype(BF16)).astype(BF16)
        return carry

    row_tiles(last, 0)
    keep_ig = pltpu.make_async_copy(r.leave.at[s], r.ig_out.at[s], r.local.at[6])
    keep_ig.start()
    give_ig = remote(r.leave.at[other], r.ig_out.at[s], r.far_send.at[5], r.far_recv.at[5], sibling)
    alone("ig", give_ig)

    go("last")
    go("end")
    while not all([one.step() is True for one in sums_of]):
        pass
    arrive("vec")
    total = r.vec_tot[s] + r.vec_far[...]
    r.small[0:5, :] = total[0:5]
    grad_re, grad_im = total[5:6, :STATES], total[5:6, STATES:]
    grad_rate = total[6:7, :STATES] * jnp.exp(-double) / scale_sq - (grad_re * decay_re + grad_im * decay_im)
    r.small[5:6, :STATES] = grad_rate * rate
    r.small[5:6, STATES:] = (grad_im * decay_re - grad_re * decay_im) * phase
    r.small[6:8, :] = jnp.zeros((2, D), F32)

    keep_ig.wait()
    for one in results:
        one.finish()
    end_all()


def results_kernel(
    tokens, act, ig, grads, small, o_act, o_ig, o_glu, o_out, o_in, o_gain, o_bias, o_nu, o_theta, o_skip, o_bglu,
    act_v, ig_v, ig_f, grads_v, grads_f, act_sem, ig_sem, grad_sem,
):
    copy = pltpu.make_async_copy
    act_in = [copy(act.at[i], act_v.at[i], act_sem.at[i, 0]) for i in range(MICRO)]
    ig_in = [copy(ig.at[i], ig_v.at[i], ig_sem.at[i, 0]) for i in range(MICRO)]
    parts = [pl.ds(GRAD_AT[i], GRAD_ROWS[i]) for i in (GLU, OUT, IN)]
    grads_in = [copy(grads.at[parts[i]], grads_v.at[parts[i]], grad_sem.at[i, 0]) for i in (GLU, OUT, IN)]
    for one in ig_in + grads_in + act_in:
        one.start()
    o_gain[...] = small[0:1, :]
    o_bias[...] = small[1:2, :]
    o_skip[...] = small[2:3, :]
    o_bglu[:, :D] = small[3:4, :]
    o_bglu[:, D:] = small[4:5, :]
    o_nu[...] = small[5:6, :STATES]
    o_theta[...] = small[5:6, STATES:]
    out = []

    def leave(src, dst, sem):
        out.append(copy(src, dst, sem))
        out[-1].start()

    for i in range(MICRO):
        ig_in[i].wait()

        def tile(j, carry, i=i):
            rows = pl.ds(pl.multiple_of(j * 64, 64), 64)
            ig_f[i, rows, :] = ig_v[i, rows, :].astype(F32)
            return carry

        lax.fori_loop(0, tokens // 64, tile, 0)
        leave(ig_f.at[i], o_ig.at[i], ig_sem.at[i, 1])
    for i, dst in ((GLU, o_glu), (OUT, o_out), (IN, o_in)):
        grads_in[i].wait()
        for c in range(GRAD_ROWS[i] // D):
            at = GRAD_AT[i] + c * D
            cols = slice(GRAD_AT[i] // 4 + c * LANES, GRAD_AT[i] // 4 + (c + 1) * LANES)
            grads_f[:, cols] = grads_v[at : at + D, :].astype(F32)
        leave(grads_f.at[:, GRAD_AT[i] // 4 : (GRAD_AT[i] + GRAD_ROWS[i]) // 4], dst, grad_sem.at[i, 1])
    for i in range(MICRO):
        act_in[i].wait()
        leave(act_v.at[i], o_act.at[i], act_sem.at[i, 1])
    for one in out:
        one.wait()


def body(ns, nd, inputs, mask, gain, bias, nu, theta, w_in, w_out, skip, w_glu, b_glu, cotangent):
    per = inputs.shape[0] // MICRO
    span = inputs.shape[1]
    tokens = per * span
    segs = tokens // SEG
    dma = pltpu.SemaphoreType.DMA
    vmem = pltpu.VMEM
    names_in = ["x", "cot", "mask", "gain", "bias", "nu", "theta", "skip", "bglu", "w_in", "w_out", "w_glu"]
    any_in = {"x", "cot", "w_in", "w_out", "w_glu"}
    outs = {
        "act_out": jax.ShapeDtypeStruct((MICRO, tokens, D), BF16),
        "ig_out": jax.ShapeDtypeStruct((MICRO, tokens, D), BF16),
        "grads": jax.ShapeDtypeStruct((ALL_ROWS, LANES), BF16),
        "small": jax.ShapeDtypeStruct((8, D), F32),
    }
    any_out = {"act_out", "ig_out", "grads"}
    half = ALL_ROWS // 2
    scratch = {
        "act": vmem((3, tokens, D), BF16),
        "cotv": vmem((tokens, D), BF16),
        "live": vmem((tokens, LANES), F32),
        "win": vmem((2, D, D), BF16),
        "wout": vmem((2, D, D), BF16),
        "wglu": vmem((2, D, 2 * D), BF16),
        "prm": vmem((2, 8, D), F32),
        "stat": vmem((2, 8, D), F32),
        "scaled": vmem((2, tokens, D), BF16),
        "u": vmem((2, 4, tokens, LANES), F32),
        "st": vmem((2, 4, tokens, LANES), F32),
        "start": vmem((2, 4, segs, LANES), F32),
        "readout": vmem((2, tokens, D), BF16),
        "active": vmem((2, tokens, D), BF16),
        "slope": vmem((2, tokens, D), F32),
        "gate": vmem((tokens, D), F32),
        "steep": vmem((tokens, D), F32),
        "gg": vmem((tokens, 2 * D), BF16),
        "gm": vmem((tokens, D), BF16),
        "adj": vmem((4, tokens, LANES), F32),
        "ig": vmem((tokens, D), BF16),
        "leave": vmem((2, tokens, D), BF16),
        "order": vmem((ROWS, ROWS), BF16),
        "bnb": vmem((4, ns * nd, 9, LANES), F32),
        "scb": vmem((4, ns, 4 * per, LANES), F32),
        "dw": vmem((2, ALL_ROWS, LANES), BF16),
        "sec": vmem((2, half, LANES), BF16),
        "half": vmem((2, half, LANES), BF16),
        "gat": vmem((2, half, LANES), BF16),
        "slots": vmem((slot_rows(ns, nd)[-1], LANES), BF16),
        "vec_a": vmem((2, ns, 8, D), F32),
        "vec_b": vmem((2, nd, 8, D), F32),
        "vec_tot": vmem((2, 8, D), F32),
        "vec_far": vmem((8, D), F32),
        "local": dma((7,)),
        "own": dma((len(FLAT),)),
        "far_send": dma((7,)),
        "far_recv": dma((7,)),
        "bn_send": dma((4,)),
        "bn_recv": dma((4,)),
        "sc_send": dma((4,)),
        "sc_recv": dma((4,)),
        "core_send": dma((len(FLAT),)),
        "core_recv": dma((len(FLAT),)),
        "rs_send": dma((len(FLAT), DEPTH)),
        "rs_recv": dma((len(FLAT), DEPTH)),
        "ag_send": dma((len(FLAT), DEPTH)),
        "ag_recv": dma((len(FLAT), DEPTH)),
        "va_send": dma((2,)),
        "va_recv": dma((2,)),
        "vb_send": dma((2,)),
        "vb_recv": dma((2,)),
    }
    in_any = pl.BlockSpec(memory_space=pl.ANY)
    in_vmem = pl.BlockSpec(memory_space=pltpu.VMEM)
    names = names_in + list(outs) + list(scratch)
    act, ig, grads, small = pl.pallas_call(
        functools.partial(kernel, ns, nd, per, span, names),
        out_shape=list(outs.values()),
        in_specs=[in_any if name in any_in else in_vmem for name in names_in],
        out_specs=[in_any if name in any_out else in_vmem for name in outs],
        scratch_shapes=list(scratch.values()),
        compiler_params=pltpu.CompilerParams(
            collective_id=0, has_side_effects=True, vmem_limit_bytes=60 * 2**20
        ),
    )(
        inputs.reshape(MICRO, tokens, D),
        cotangent.reshape(MICRO, tokens, D),
        mask,
        gain,
        bias,
        nu,
        theta,
        skip,
        b_glu,
        w_in,
        w_out,
        w_glu,
    )

    wide_out = [(1, D), (1, D), (1, STATES), (1, STATES), (1, D), (1, 2 * D)]
    big_out = [((MICRO, tokens, D), BF16), ((MICRO, tokens, D), F32)]
    big_out += [((D, GRAD_ROWS[which] // 4), F32) for which in (GLU, OUT, IN)]
    act, ig, d_glu, d_out, d_in, d_gain, d_bias, d_nu, d_theta, d_skip, d_bglu = pl.pallas_call(
        functools.partial(results_kernel, tokens),
        out_shape=[jax.ShapeDtypeStruct(*x) for x in big_out] + [jax.ShapeDtypeStruct(x, F32) for x in wide_out],
        in_specs=[in_any] * 3 + [in_vmem],
        out_specs=[in_any] * 5 + [in_vmem] * 6,
        scratch_shapes=[
            vmem((MICRO, tokens, D), BF16),
            vmem((MICRO, tokens, D), BF16),
            vmem((MICRO, tokens, D), F32),
            vmem((ALL_ROWS, LANES), BF16),
            vmem((D, ALL_ROWS // 4), F32),
            dma((2, 2)),
            dma((2, 2)),
            dma((3, 2)),
        ],
        compiler_params=pltpu.CompilerParams(vmem_limit_bytes=60 * 2**20),
    )(act, ig, grads, small)
    whole = (1, MICRO * per, span, D)
    return (
        act.reshape(whole),
        ig.reshape(whole),
        d_gain,
        d_bias,
        d_nu,
        d_theta,
        d_in[None],
        d_out[None],
        d_skip,
        d_glu[None],
        d_bglu,
    )


def solution(mesh):
    rows = P("section", None)
    cube = P("section", None, None)
    tokens = P("dp", "seq", None)
    spread = P("section", "dp", "seq", None)
    in_specs = (tokens, P("dp", "seq"), rows, rows, rows, rows, cube, cube, rows, cube, rows, tokens)
    out_specs = (spread, spread, rows, rows, rows, rows, cube, cube, rows, cube, rows)
    return jax.shard_map(
        functools.partial(body, mesh.shape["seq"], mesh.shape["dp"]),
        mesh=mesh,
        in_specs=in_specs,
        out_specs=out_specs,
        check_vma=False,
    )
```

```python
import functools
import math
import types

import jax
import jax.numpy as jnp
from jax import lax
from jax.experimental import pallas as pl
from jax.experimental.pallas import tpu as pltpu
from jax.sharding import PartitionSpec as P

D = 512
STATES = 256
MICRO = 2
EPS = 1e-05
LANES = 128
ROWS = 256
SEG = 32
EIGHT = 8
GLU, OUT, IN = 0, 1, 2
GRAD_ROWS = (4096, 2048, 2048)
GRAD_AT = (0, 4096, 6144)
ALL_ROWS = 8192
SD = ("seq", "dp")
DS = ("dp", "seq")
PARTS = (
    ((0, 1536, SD), (1536, 1536, SD), (3072, 1024, DS),),
    ((0, 1024, SD), (1024, 1024, DS),),
    ((0, 2048, SD),),
    ((0, 4096, SD),),
    ((0, 2048, SD),),
    ((0, 1536, SD), (1536, 512, DS),),
)
FLAT = tuple((n, *part) for n, parts in enumerate(PARTS) for part in parts)
DEPTH = max(len(part[-1]) for part in FLAT)
PLAN = {
    "carry two": (104, 103, 7),
    "filled two": (),
    "norm two": (105, 6, 7, 8, 9),
    "through": (7,),
    "carry one": (200, 100, 6, 7, 101, 8),
    "filled one": (3, 2, 9),
    "norm one": (0, 102, 1, 8, 3, 2, 6, 5),
    "last": (8, 1, 9, 0, 6, 201),
    "end": (4, 0, 5, 4, 3, 1, 2, 0, 5, 2, 4, 1, 202, 4, 9, 3, 5),
}
ROOT = math.sqrt(2.0 / math.pi)
CUBE = 0.044715

F32 = jnp.float32
BF16 = jnp.bfloat16
MESH = pl.DeviceIdType.MESH


def mm(a, b):
    return lax.dot_general(a, b, (((1,), (0,)), ((), ())), preferred_element_type=F32)


def mm_t(a, b):
    return lax.dot_general(a, b, (((1,), (1,)), ((), ())), preferred_element_type=F32)


def t_mm(a, b):
    return lax.dot_general(a, b, (((0,), (0,)), ((), ())), preferred_element_type=F32)


def complex_mul(ar, ai, br, bi):
    return ar * br - ai * bi, ar * bi + ai * br


def power(re, im, n):
    out = None
    while n:
        if n & 1:
            out = (re, im) if out is None else complex_mul(*out, re, im)
        n >>= 1
        if n:
            re, im = complex_mul(re, im, re, im)
    return out


def as_row(four):
    return jnp.concatenate([four[c : c + 1] for c in range(4)], axis=1)


def wide(tile):
    return jnp.concatenate([tile] * 4, axis=1)


def column_sum(x):
    return jnp.sum(x, axis=0, keepdims=True)


def slots_of(rows, counts, spread):
    out, start = [], 0
    for level, count in enumerate(counts):
        size = rows if spread and level == len(counts) - 1 else rows // count
        out.append((start, size))
        start += count * size
        rows //= count
    return out


def slot_rows(ns, nd):
    inner = next(n for n in range(math.isqrt(ns), 0, -1) if ns % n == 0)
    sizes = {"seq": ns, "dp": nd, "in": inner, "out": ns // inner}
    bases = [0]
    for _, _, rows, order in FLAT:
        counts = [sizes[name] for name in order]
        spread = rows // 2 // math.prod(counts) % 16 != 0
        start, size = slots_of(rows // 2, counts, spread)[-1]
        bases.append(bases[-1] + start + counts[-1] * size)
    return bases


def kernel(ns, nd, per, span, names, *refs):
    r = types.SimpleNamespace(**dict(zip(names, refs)))
    tokens = per * span
    segs = tokens // SEG
    nseg = span // SEG
    tiles = tokens // ROWS
    blocks = segs // EIGHT
    peers = ns * nd
    s = lax.axis_index("section")
    d = lax.axis_index("dp")
    q = lax.axis_index("seq")
    other = 1 - s
    me = d * ns + q
    sibling = {"section": other}

    def seq_peer(k):
        return {"seq": lax.rem(q + k, ns)}

    def dp_peer(k):
        return {"dp": lax.rem(d + k, nd)}

    def any_peer(k):
        at = lax.rem(me + k, peers)
        return {"dp": at // ns, "seq": lax.rem(at, ns)}

    def remote(src, dst, send, recv, device):
        return pltpu.make_async_remote_copy(
            src_ref=src, dst_ref=dst, send_sem=send, recv_sem=recv, device_id=device, device_id_type=MESH
        )

    def over(low, high, body):
        lax.fori_loop(low, high, lambda k, c: (body(k), c)[1], 0)

    arriving = {}
    leaving = {}

    def begin(key, start, whole):
        start()
        arriving[key] = leaving[key] = whole

    def arrive(key):
        arriving.pop(key).wait_recv()

    def leave(key):
        leaving.pop(key).wait_send()

    def end_all():
        for key in list(arriving):
            arrive(key)
        for key in list(leaving):
            leave(key)

    def alone(key, copy):
        begin(key, copy.start, copy)

    def row_tiles(body, init):
        def step(i, carry):
            return body(pl.ds(pl.multiple_of(i * ROWS, ROWS), ROWS), carry)

        return lax.fori_loop(0, tiles, step, init, unroll=4)

    slot_base = slot_rows(ns, nd)

    def skewed(tile, sums):
        waiting, running = [pl.ds(i * ROWS, ROWS) for i in range(tiles)], []
        while waiting or running:
            if waiting:
                running.append(tile(waiting.pop(0), sums))
            running = [one for one in running if next(one, True) is not True]
        return sums

    barrier = pltpu.get_barrier_semaphore()

    def greet(device):
        pl.semaphore_signal(barrier, inc=1, device_id=device, device_id_type=MESH)

    distant = [*range(nd - 1, 0, -2), *range(nd - 2, 0, -2), 0]
    others = [(a, b) for a in distant for b in range(ns - 1, -1, -1) if a or b]

    def each_other(body):
        if len(others) > 15:
            over(1, peers, lambda k: body(any_peer(k)))
            return
        for a, b in others:
            body({"dp": lax.rem(d + a, nd), "seq": lax.rem(q + b, ns)})

    each_other(greet)
    greet(sibling)
    over(1, ns, lambda k: greet({"section": other, **seq_peer(k)}))
    over(1, nd, lambda k: greet({"section": other, **dp_peer(k)}))

    load_x = pltpu.make_async_copy(r.x.at[s], r.act.at[0], r.local.at[0])
    load_x.start()
    load_cot = pltpu.make_async_copy(r.cot.at[s], r.cotv, r.local.at[1])
    weights = ((r.w_in, r.win), (r.w_out, r.wout), (r.w_glu, r.wglu))
    load_w = [
        pltpu.make_async_copy(src.at[0], dst.at[s], r.local.at[2 + i]) for i, (src, dst) in enumerate(weights)
    ]
    for copy in load_w:
        copy.start()
    load_cot.start()

    rate = jnp.exp(r.nu[...])
    phase = jnp.exp(r.theta[...])
    size = jnp.exp(-rate)
    decay_re = size * jnp.cos(phase)
    decay_im = size * jnp.sin(phase)
    double = 2.0 * rate
    scale_sq = double * (
        1.0
        - double / 2.0 * (1.0 - double / 3.0 * (1.0 - double / 4.0 * (1.0 - double / 5.0 * (1.0 - double / 6.0))))
    )
    scale = jnp.sqrt(scale_sq)
    r.prm[s, 0:1, :] = r.gain[...]
    r.prm[s, 1:2, :] = r.bias[...]
    r.prm[s, 2:3, :] = r.skip[...]
    r.prm[s, 3:4, :] = r.bglu[:, :D]
    r.prm[s, 4:5, :] = r.bglu[:, D:]
    r.prm[s, 5:6, :] = jnp.concatenate([decay_re, decay_im], axis=1)
    r.prm[s, 6:7, :] = jnp.concatenate([scale, scale], axis=1)
    r.prm[s, 7:8, :] = jnp.zeros((1, D), F32)

    count = jnp.zeros((1, 1), F32)
    row = lax.broadcasted_iota(jnp.int32, (tokens, LANES), 0)
    token = (row & -ROWS) + (row & (EIGHT - 1)) * SEG + ((row & (ROWS - 1)) >> (EIGHT.bit_length() - 1))
    live = jnp.zeros((tokens, LANES), F32)
    for i in range(per):
        here = jnp.sum(r.mask[pl.ds(s * per + i, 1), :], axis=1, keepdims=True)
        live = jnp.where((token >= i * span) & (token < i * span + here), 1.0, live)
        count = count + here.astype(F32)
    r.live[...] = live
    count_row = jnp.broadcast_to(count, (1, LANES))
    to_row = lax.broadcasted_iota(jnp.int32, (ROWS, ROWS), 0)
    from_row = lax.broadcasted_iota(jnp.int32, (ROWS, ROWS), 1)
    came_from = (to_row & (EIGHT - 1)) * SEG + (to_row >> (EIGHT.bit_length() - 1))
    r.order[...] = jnp.where(from_row == came_from, 1.0, 0.0).astype(BF16)
    load_x.wait()

    def mask_input(rows, total):
        x = mm(r.order[...], r.act[0, rows, :]) * wide(r.live[rows, :])
        r.act[0, rows, :] = x.astype(BF16)
        return total + column_sum(x)

    def centred(b, mean):
        def tile(rows, total):
            off = (r.act[b, rows, :].astype(F32) - mean) * wide(r.live[rows, :])
            return total + column_sum(off * off)

        return row_tiles(tile, jnp.zeros((1, D), F32))

    def put_rows(ph, upper, lower):
        for c in range(4):
            r.bnb[ph, me, c : c + 1, :] = upper[:, c * LANES : (c + 1) * LANES]
            r.bnb[ph, me, 4 + c : 5 + c, :] = lower[:, c * LANES : (c + 1) * LANES]
        r.bnb[ph, me, 8:9, :] = count_row

    def to_all(ph, device):
        block = r.bnb.at[ph, me]
        return remote(block, block, r.bn_send.at[ph], r.bn_recv.at[ph], device)

    def send_all(ph):
        blocks = r.bnb.at[ph, pl.ds(0, peers - 1)]
        whole = remote(blocks, blocks, r.bn_send.at[ph], r.bn_recv.at[ph], sibling)
        begin(("all", ph), lambda: each_other(lambda device: to_all(ph, device).start()), whole)

    def wait_all(ph):
        arrive(("all", ph))

    def norm_sums(b, total):
        mean = total / jnp.maximum(wide(count_row), 1.0)
        put_rows(b, mean, centred(b, mean))

    def norm_merge(b):
        wait_all(b)
        got = r.bnb[b]
        means, spreads, counts = got[:, 0:4, :], got[:, 4:8, :], got[:, 8:9, :]
        valid = jnp.sum(counts, axis=0)
        mean = jnp.sum(counts * means, axis=0) / valid
        apart = means - mean[None]
        spread = jnp.sum(spreads + counts * apart * apart, axis=0)
        r.stat[b, 0:1, :] = as_row(mean)
        r.stat[b, 1:2, :] = as_row(lax.rsqrt(spread / valid + EPS))
        r.stat[b, 2:3, :] = wide(valid)

    norm_sums(0, row_tiles(mask_input, jnp.zeros((1, D), F32)))

    pl.semaphore_wait(barrier, peers + ns - 1 + nd - 1)
    send_all(0)
    send_prm = remote(r.prm.at[s], r.prm.at[s], r.far_send.at[0], r.far_recv.at[0], sibling)
    send_w = [
        remote(src.at[0], dst.at[s], r.far_send.at[1 + i], r.far_recv.at[1 + i], sibling)
        for i, (src, dst) in enumerate(weights)
    ]

    alone("prm", send_prm)
    for i, copy in enumerate(send_w):
        alone(("w", i), copy)

    def decay(b, sign):
        out = []
        for c in range(2):
            re = r.prm[b, 5:6, c * LANES : (c + 1) * LANES]
            im = r.prm[b, 5:6, STATES + c * LANES : STATES + (c + 1) * LANES]
            out.append((re, sign * im))
        return out

    def step_rows(k, l):
        return pl.ds(pl.multiple_of(k * ROWS + l * EIGHT, EIGHT), EIGHT)

    def at_step(ref, l):
        return jnp.concatenate([ref[step_rows(k, l), :] for k in range(blocks)], axis=0)

    def put_step(ref, l, value):
        for k in range(blocks):
            ref[step_rows(k, l), :] = value[k * EIGHT : (k + 1) * EIGHT]

    def advance(a, state, drive):
        return (
            a[0] * state[0] - a[1] * state[1] + drive[0],
            a[1] * state[0] + a[0] * state[1] + drive[1],
        )

    place = lax.rem(lax.broadcasted_iota(jnp.int32, (segs, LANES), 0), nseg)
    owner = lax.broadcasted_iota(jnp.int32, (segs, LANES), 0) // nseg

    def moved(x, k, reverse):
        if reverse:
            return jnp.where(place < nseg - k, pltpu.roll(x, segs - k, 0), 0.0)
        return jnp.where(place >= k, pltpu.roll(x, k, 0), 0.0)

    def seg_scan(re, im, jump, reverse):
        k = 1
        while k < nseg:
            add_re, add_im = complex_mul(*jump, moved(re, k, reverse), moved(im, k, reverse))
            re, im = re + add_re, im + add_im
            jump = complex_mul(*jump, *jump)
            k *= 2
        return re, im

    def to_seq(ph, k):
        block = r.scb.at[ph, q]
        return remote(block, block, r.sc_send.at[ph], r.sc_recv.at[ph], seq_peer(k))

    def carry(ph, drive, a, reverse, between):
        def step(i, states):
            l = SEG - 1 - i if reverse else i
            return tuple(
                advance(a[c], states[c], (at_step(drive.at[c], l), at_step(drive.at[2 + c], l))) for c in range(2)
            )

        zero = jnp.zeros((segs, LANES), F32)
        ends = lax.fori_loop(0, SEG, step, ((zero, zero), (zero, zero)), unroll=4)
        jumps = [power(*a[c], SEG) for c in range(2)]
        sums = [seg_scan(*ends[c], jumps[c], reverse) for c in range(2)]
        for i in range(per):
            last = i * nseg if reverse else (i + 1) * nseg - 1
            for c in range(2):
                r.scb[ph, q, 4 * i + c : 4 * i + c + 1, :] = sums[c][0][last : last + 1]
                r.scb[ph, q, 4 * i + 2 + c : 4 * i + 3 + c, :] = sums[c][1][last : last + 1]
        ends_of = r.scb.at[ph, pl.ds(0, ns - 1)]
        whole = remote(ends_of, ends_of, r.sc_send.at[ph], r.sc_recv.at[ph], sibling)
        begin(("seq", ph), lambda: over(1, ns, lambda k: to_seq(ph, k).start()), whole)
        first = jnp.where(place == (nseg - 1 if reverse else 0), 1.0, 0.0)
        reach = [seg_scan(first, zero, jumps[c], reverse) for c in range(2)]
        between()
        arrive(("seq", ph))
        starts = []
        for c in range(2):
            far = power(*a[c], span)
            entering = []
            for i in range(per):
                re = jnp.zeros((1, LANES), F32)
                im = jnp.zeros((1, LANES), F32)
                for lap in range(ns):
                    j = ns - 1 - lap if reverse else lap
                    before = j > q if reverse else j < q
                    new_re, new_im = advance(
                        far,
                        (re, im),
                        (r.scb[ph, j, 4 * i + c : 4 * i + c + 1, :], r.scb[ph, j, 4 * i + 2 + c : 4 * i + 3 + c, :]),
                    )
                    re = jnp.where(before, new_re, re)
                    im = jnp.where(before, new_im, im)
                entering.append((re, im))
            in_re = jnp.broadcast_to(entering[0][0], (segs, LANES))
            in_im = jnp.broadcast_to(entering[0][1], (segs, LANES))
            for i in range(1, per):
                in_re = jnp.where(owner == i, entering[i][0], in_re)
                in_im = jnp.where(owner == i, entering[i][1], in_im)
            add_re, add_im = complex_mul(*reach[c], in_re, in_im)
            starts.append((moved(sums[c][0], 1, reverse) + add_re, moved(sums[c][1], 1, reverse) + add_im))
        return starts

    def fill_states(b, starts, a, reverse):
        for c in range(2):
            r.start[b, c] = starts[c][0]
            r.start[b, 2 + c] = starts[c][1]

        def step(i, states):
            l = SEG - 1 - i if reverse else i
            out = []
            for c in range(2):
                new = advance(a[c], states[c], (at_step(r.u.at[b, c], l), at_step(r.u.at[b, 2 + c], l)))
                put_step(r.st.at[b, c], l, new[0])
                put_step(r.st.at[b, 2 + c], l, new[1])
                out.append(new)
            return tuple(out)

        lax.fori_loop(0, SEG, step, tuple(starts), unroll=4)

    def fill_adjoint(b, starts, a, reverse):
        back = 1 if not reverse else -1
        zero = jnp.zeros((segs, LANES), F32)
        sums = []
        for c in range(2):
            scale_c = r.prm[b, 6:7, c * LANES : (c + 1) * LANES]

            def one(l, prior, carry, c=c, scale_c=scale_c):
                state, by_re, by_im, by_scale = carry
                re, im = advance(a[c], state, (at_step(r.adj.at[c], l), at_step(r.adj.at[2 + c], l)))
                put_step(r.adj.at[c], l, scale_c * re)
                put_step(r.adj.at[2 + c], l, scale_c * im)
                by_re = by_re + (re * prior[0] + im * prior[1])
                by_im = by_im + (im * prior[0] - re * prior[1])
                by_scale = by_scale + (re * at_step(r.u.at[b, c], l) + im * at_step(r.u.at[b, 2 + c], l))
                return (re, im), by_re, by_im, by_scale

            def step(i, carry, c=c, one=one):
                l = SEG - 1 - i if reverse else i
                prior = (at_step(r.st.at[b, c], l + back), at_step(r.st.at[b, 2 + c], l + back))
                return one(l, prior, carry)

            carry_c = lax.fori_loop(0, SEG - 1, step, (starts[c], zero, zero, zero), unroll=4)
            final = one(0 if reverse else SEG - 1, (r.start[b, c], r.start[b, 2 + c]), carry_c)
            sums.append([column_sum(x) for x in final[1:]])
        return [jnp.concatenate([sums[0][i], sums[1][i]], axis=1) for i in range(3)]

    def forward_in(b):
        gain, bias, scale_row = r.prm[b, 0:1, :], r.prm[b, 1:2, :], r.prm[b, 6:7, :]
        average = r.stat[b, 0:1, :]
        slope = r.stat[b, 1:2, :] * gain

        def tile(rows, _):
            x = r.act[b, rows, :].astype(F32)
            scaled = (wide(r.live[rows, :]) * ((x - average) * slope + bias)).astype(BF16)
            r.scaled[b, rows, :] = scaled
            yield
            u = mm(scaled, r.win[b])
            yield
            u = u * scale_row
            for c in range(4):
                r.u[b, c, rows, :] = u[:, c * LANES : (c + 1) * LANES]

        skewed(tile, [])

    def forward_out(b, finish, sums):
        skip = r.prm[b, 2:3, :]
        value_bias, half_gate_bias = r.prm[b, 3:4, :], 0.5 * r.prm[b, 4:5, :]

        def tile(rows, sums):
            readout = jnp.concatenate([r.st[b, c, rows, :] for c in range(4)], axis=1).astype(BF16)
            r.readout[b, rows, :] = readout
            through = mm(readout, r.wout[b])
            yield
            mixed = through + skip * r.scaled[b, rows, :].astype(F32)
            square = mixed * mixed
            t = jnp.tanh(mixed * (ROOT + (ROOT * CUBE) * square))
            half = 0.5 + 0.5 * t
            wide_active = mixed * half
            active = wide_active.astype(BF16)
            r.active[b, rows, :] = active
            r.slope[b, rows, :] = half + wide_active * ((1.0 - t) * (ROOT + (3.0 * ROOT * CUBE) * square))
            yield
            gated = mm(active, r.wglu[b])
            yield
            gate = 0.5 + 0.5 * jnp.tanh(0.5 * gated[:, D:] + half_gate_bias)
            product = (gated[:, :D] + value_bias) * gate
            live = wide(r.live[rows, :])
            result = (r.act[b, rows, :].astype(F32) + live * product).astype(BF16)
            r.act[b + 1, rows, :] = result
            yield from finish(rows, live, gate, product * (1.0 - gate), result, sums)

        return skewed(tile, sums)

    def back_tile(b, rows, outer, gate, steep, sums):
        grad_gated = jnp.concatenate([outer * gate, outer * steep], axis=1).astype(BF16)
        r.gg[rows, :] = grad_gated
        sums[1] = sums[1] + column_sum(grad_gated.astype(F32))
        yield
        grad_active = mm_t(grad_gated, r.wglu[b])
        yield
        grad_mixed = (r.slope[b, rows, :] * grad_active).astype(BF16)
        r.gm[rows, :] = grad_mixed
        sums[0] = sums[0] + column_sum(grad_mixed.astype(F32) * r.scaled[b, rows, :].astype(F32))
        yield
        grad_readout = mm_t(grad_mixed, r.wout[b])
        yield
        for c in range(4):
            r.adj[c, rows, :] = grad_readout[:, c * LANES : (c + 1) * LANES]

    def normed(b, rows):
        return (r.act[b, rows, :].astype(F32) - r.stat[b, 0:1, :]) * r.stat[b, 1:2, :]

    projected_grads = (r.cotv, r.ig)

    def round_adjoint(b):
        def tile(rows, carry):
            adjoint = jnp.concatenate([r.adj[c, rows, :] for c in range(4)], axis=1)
            projected_grads[b][rows, :] = adjoint.astype(BF16)
            return carry

        row_tiles(tile, 0)

    def back_in(b):
        skip = r.prm[b, 2:3, :]

        def tile(rows, sums):
            into = mm_t(projected_grads[b][rows, :], r.win[b])
            yield
            masked = wide(r.live[rows, :]) * (skip * r.gm[rows, :].astype(F32) + into)
            r.slope[b, rows, :] = masked
            sums[0] = sums[0] + column_sum(masked * normed(b, rows))
            sums[1] = sums[1] + column_sum(masked)

        zero = jnp.zeros((1, D), F32)
        return skewed(tile, [zero, zero])

    def back_norm(ph, b):
        wait_all(ph)
        got = jnp.sum(r.bnb[ph], axis=0)
        gain_total, bias_total = as_row(got[0:4]), as_row(got[4:8])
        r.vec_tot[b, 0:1, :] = gain_total
        r.vec_tot[b, 1:2, :] = bias_total
        slope = r.stat[b, 1:2, :] * r.prm[b, 0:1, :]
        per_token = slope / r.stat[b, 2:3, :]
        return slope, per_token * bias_total, per_token * gain_total

    def source_grad(b, rows, upstream, live, slope, by_bias, by_gain):
        return upstream + live * (slope * r.slope[b, rows, :] - by_bias - normed(b, rows) * by_gain)

    def weight_grad(b, which, left, right):
        columns = GRAD_ROWS[which] // 4

        def tile(j, carry):
            cols = pl.ds(pl.multiple_of(j * 256, 256), 256)
            grad = t_mm(left, right[:, cols]).astype(BF16)
            at = pl.multiple_of(GRAD_AT[which] + j * 1024, 1024)
            r.dw[b, pl.ds(at, 512), :] = grad[:, :LANES]
            r.dw[b, pl.ds(at + 512, 512), :] = grad[:, LANES:]
            return carry

        lax.fori_loop(0, columns // 256, tile, 0, unroll=2)

    inner = next(n for n in range(math.isqrt(ns), 0, -1) if ns % n == 0)
    outer = ns // inner
    q_out, q_in = q // inner, lax.rem(q, inner)
    axes = {
        "seq": (ns, q, seq_peer),
        "dp": (nd, d, dp_peer),
        "in": (inner, q_in, lambda k: {"seq": q_out * inner + lax.rem(q_in + k, inner)}),
        "out": (outer, q_out, lambda k: {"seq": lax.rem(q_out + k, outer) * inner + q_in}),
    }

    results = []

    class Reduced:
        def __init__(self, n):
            which, start, rows, order = FLAT[n]
            self.b, self.n, self.at = which // 3, n, GRAD_AT[which % 3] + start
            self.base = self.at // 2
            self.axes = [axes[name] for name in order]
            self.sizes, self.offsets = [rows // 2], [0]
            for count, index, _ in self.axes:
                self.sizes.append(self.sizes[-1] // count)
                self.offsets.append(self.offsets[-1] + index * self.sizes[-1])
            self.spread = self.sizes[-1] % 16 != 0
            self.slots = slots_of(rows // 2, [count for count, _, _ in self.axes], self.spread)
            self.slot_base = slot_base[self.n]
            self.steps = self.plan()

        def rows(self, offset, size):
            return pl.ds(pl.multiple_of(self.base + offset, 16), size)

        def to_core(self):
            size = self.sizes[0]
            src = r.dw.at[self.b, pl.ds(pl.multiple_of(self.at + other * size, 16), size)]
            return remote(src, r.sec.at[self.b, self.rows(0, size)], r.core_send.at[self.n], r.core_recv.at[self.n], sibling)

        def slot(self, level, index):
            start, size = self.slots[level]
            return pl.ds(pl.multiple_of(self.slot_base + start + index * size, 16), size)

        def scatter(self, level, k):
            count, index, peer = self.axes[level]
            if self.spread and level == len(self.axes) - 1:
                src = r.slots.at[self.slot(level, index)]
            else:
                size = self.sizes[level + 1]
                src = r.half.at[self.b, self.rows(self.offsets[level] + lax.rem(index + k, count) * size, size)]
            dst = r.slots.at[self.slot(level, index)]
            return remote(src, dst, r.rs_send.at[self.n, level], r.rs_recv.at[self.n, level], peer(k))

        def gather(self, level, k):
            block = r.gat.at[self.b, self.rows(self.offsets[level + 1], self.sizes[level + 1])]
            return remote(block, block, r.ag_send.at[self.n, level], r.ag_recv.at[self.n, level], self.axes[level][2](k))

        def place(self):
            return pl.ds(pl.multiple_of(self.at + s * self.sizes[0] + self.offsets[1], 16), self.sizes[1])

        def result(self, device, send):
            src = r.gat.at[self.b, self.rows(self.offsets[1], self.sizes[1])]
            target = {"section": self.b, **device}
            return remote(src, r.grads.at[self.place()], send, r.ag_recv.at[self.n, 0], target)

        def results_whole(self, parts):
            rows = r.grads.at[pl.ds(0, parts * self.sizes[1])]
            return remote(rows, rows, r.ag_send.at[self.n, 0], r.ag_recv.at[self.n, 0], sibling)

        def own(self):
            src = r.gat.at[self.b, self.rows(self.offsets[1], self.sizes[1])]
            return pltpu.make_async_copy(src, r.grads.at[self.place()], r.own.at[self.n])

        def across(self):
            return self.result({}, r.own.at[self.n])

        def each(self, level, body):
            over(1, self.axes[level][0], body)

        def first(self):
            size = self.sizes[0]
            arrive((self.n, "core"))
            mine = r.dw[self.b, pl.ds(pl.multiple_of(self.at + s * size, 16), size), :].astype(F32)
            there = r.sec[self.b, self.base : self.base + size, :].astype(F32)
            r.half[self.b, self.base : self.base + size, :] = (mine + there).astype(BF16)

        def collect(self, level):
            arrive((self.n, "scatter", level))
            count, index, _ = self.axes[level]
            last = level == len(self.axes) - 1
            if self.spread and last:
                total = sum(r.slots[self.slot(level, j), :].astype(F32) for j in range(count))
                r.gat[self.b, self.rows(self.offsets[level], self.sizes[level]), :] = total.astype(BF16)
                return
            here = self.rows(self.offsets[level + 1], self.sizes[level + 1])
            total = r.half[self.b, here, :].astype(F32)
            for k in range(1, count):
                total = total + r.slots[self.slot(level, lax.rem(index + k, count)), :].astype(F32)
            (r.gat if last else r.half)[self.b, here, :] = total.astype(BF16)

        def send(self, level):
            if self.spread and level == len(self.axes) - 1:
                here = self.rows(self.offsets[level], self.sizes[level])
                r.slots[self.slot(level, self.axes[level][1]), :] = r.half[self.b, here, :]
            start, size = self.slots[level]
            rows = r.slots.at[pl.ds(self.slot_base + start, (self.axes[level][0] - 1) * size)]
            whole = remote(rows, rows, r.rs_send.at[self.n, level], r.rs_recv.at[self.n, level], sibling)
            begin((self.n, "scatter", level), lambda: self.each(level, lambda k: self.scatter(level, k).start()), whole)

        def share(self, level):
            count, _, peer = self.axes[level]
            if level:
                rows = r.gat.at[self.b, pl.ds(self.base, (count - 1) * self.sizes[level + 1])]
                whole = remote(rows, rows, r.ag_send.at[self.n, level], r.ag_recv.at[self.n, level], sibling)
                begin((self.n, "gather", level), lambda: self.each(level, lambda k: self.gather(level, k).start()), whole)
                return
            self.each(0, lambda k: self.result(peer(k), r.ag_send.at[self.n, 0]).start())

            @pl.when(s == self.b)
            def _():
                self.own().start()

            @pl.when(s != self.b)
            def _():
                self.across().start()

            results.append(self)

        def finish(self):
            count = self.axes[0][0]

            @pl.when(s == self.b)
            def _():
                self.own().wait()
                self.results_whole(2 * count - 1).wait_recv()

            @pl.when(s != self.b)
            def _():
                self.across().wait_send()

            if count > 1:
                self.results_whole(count - 1).wait_send()

        def plan(self):
            depth = len(self.axes)
            top = depth - 2 if self.spread else depth - 1
            yield alone((self.n, "core"), self.to_core())
            self.first()
            yield self.send(0)
            for level in range(1, depth):
                self.collect(level - 1)
                yield self.send(level)
            self.collect(depth - 1)
            yield self.share(top)
            for level in range(top, 0, -1):
                arrive((self.n, "gather", level))
                yield self.share(level - 1)

        def step(self):
            return next(self.steps, True)

    sums_of = [Reduced(n) for n in range(len(FLAT))]

    factors = ((r.active, (r.gg, r.gg)), (r.readout, (r.gm, r.gm)), (r.scaled, projected_grads))

    def go(gap):
        for n in PLAN[gap]:
            if n < 100:
                sums_of[n].step()
                continue
            if n >= 200:
                vec_steps[n - 200]()
                continue
            b, which = (n - 100) // 3, (n - 100) % 3
            left, right = factors[which]
            weight_grad(b, which, left[b], right[b])
            for one, part in zip(sums_of, FLAT):
                if part[0] == n - 100:
                    one.step()

    def vec_seq(b, k):
        block = r.vec_a.at[b, q]
        return remote(block, block, r.va_send.at[b], r.va_recv.at[b], seq_peer(k))

    def vec_dp(b, k):
        block = r.vec_b.at[b, d]
        return remote(block, block, r.vb_send.at[b], r.vb_recv.at[b], dp_peer(k))

    def vec_one(b, by_skip, by_bias, by_decay):
        zero = jnp.zeros((1, D), F32)
        r.vec_a[b, q, 0:1, :] = zero
        r.vec_a[b, q, 1:2, :] = zero
        r.vec_a[b, q, 2:3, :] = by_skip
        r.vec_a[b, q, 3:4, :] = by_bias[:, :D]
        r.vec_a[b, q, 4:5, :] = by_bias[:, D:]
        r.vec_a[b, q, 5:6, :] = jnp.concatenate([by_decay[0], by_decay[1]], axis=1)
        r.vec_a[b, q, 6:7, :] = jnp.concatenate([by_decay[2], by_decay[2]], axis=1)
        r.vec_a[b, q, 7:8, :] = zero
        rows = r.vec_a.at[b, pl.ds(0, ns - 1)]
        whole = remote(rows, rows, r.va_send.at[b], r.va_recv.at[b], sibling)
        begin(("vec_seq", b), lambda: over(1, ns, lambda k: vec_seq(b, k).start()), whole)

    def vec_two(b):
        arrive(("vec_seq", b))
        r.vec_b[b, d] = jnp.sum(r.vec_a[b], axis=0)
        rows = r.vec_b.at[b, pl.ds(0, nd - 1)]
        whole = remote(rows, rows, r.vb_send.at[b], r.vb_recv.at[b], sibling)
        begin(("vec_dp", b), lambda: over(1, nd, lambda k: vec_dp(b, k).start()), whole)

    def vec_three(b):
        arrive(("vec_dp", b))
        total = jnp.sum(r.vec_b[b], axis=0)
        r.vec_tot[b, 2:8, :] = total[2:8]

    def vec_last():
        vec_three(1)
        vec_three(0)
        alone("vec", remote(r.vec_tot.at[other], r.vec_far, r.far_send.at[6], r.far_recv.at[6], sibling))

    vec_steps = (lambda: vec_two(1), lambda: vec_two(0), vec_last)

    arrive("prm")
    for i in range(3):
        load_w[i].wait()
        arrive(("w", i))
    load_cot.wait()

    def order_cot(rows, carry):
        r.cotv[rows, :] = mm(r.order[...], r.cotv[rows, :]).astype(BF16)
        return carry

    row_tiles(order_cot, 0)

    def in_time(src, dst):
        def tile(rows, carry):
            dst[rows, :] = t_mm(r.order[...], src[rows, :]).astype(BF16)
            return carry

        row_tiles(tile, 0)

    zero_row = jnp.zeros((1, D), F32)

    def nothing():
        pass

    norm_merge(0)
    forward_in(0)
    ahead0, ahead1 = decay(0, 1.0), decay(1, 1.0)
    starts = carry(0, r.u.at[0], ahead0, False, nothing)
    fill_states(0, starts, ahead0, False)

    def finish_one(rows, live, gate, steep, result, sums):
        r.gate[rows, :] = gate
        r.steep[rows, :] = steep
        sums[0] = sums[0] + column_sum(result.astype(F32))
        yield

    norm_sums(1, forward_out(0, finish_one, [zero_row])[0])
    send_all(1)
    in_time(r.act.at[1], r.leave.at[0])
    norm_merge(1)
    forward_in(1)
    starts = carry(1, r.u.at[1], ahead1, True, nothing)
    fill_states(1, starts, ahead1, True)

    def finish_two(rows, live, gate, steep, result, sums):
        return back_tile(1, rows, live * r.cotv[rows, :].astype(F32), gate, steep, sums)

    wide_zero = jnp.zeros((1, 2 * D), F32)
    by_skip, by_bias = forward_out(1, finish_two, [zero_row, wide_zero])

    keep_act = pltpu.make_async_copy(r.leave.at[s], r.act_out.at[s], r.local.at[5])
    give_act = remote(r.leave.at[other], r.act_out.at[s], r.far_send.at[4], r.far_recv.at[4], sibling)

    back0, back1 = decay(0, -1.0), decay(1, -1.0)

    def first_pieces():
        go("carry two")
        in_time(r.act.at[2], r.leave.at[1])
        keep_act.start()
        alone("act", give_act)

    starts = carry(2, r.adj, back1, False, first_pieces)
    by_decay = fill_adjoint(1, starts, back1, False)
    round_adjoint(1)
    go("filled two")
    put_rows(2, *back_in(1))
    send_all(2)
    vec_one(1, by_skip, by_bias, by_decay)
    go("norm two")
    slope, by_bias_total, by_gain_total = back_norm(2, 1)

    def through(rows, sums):
        live = wide(r.live[rows, :])
        upstream = r.cotv[rows, :].astype(F32)
        grad = source_grad(1, rows, upstream, live, slope, by_bias_total, by_gain_total).astype(BF16)
        r.ig[rows, :] = grad
        yield from back_tile(0, rows, live * grad.astype(F32), r.gate[rows, :], r.steep[rows, :], sums)

    by_skip, by_bias = skewed(through, [zero_row, wide_zero])
    go("through")

    def next_pieces():
        go("carry one")

    starts = carry(3, r.adj, back0, True, next_pieces)
    by_decay = fill_adjoint(0, starts, back0, True)
    round_adjoint(0)
    go("filled one")
    put_rows(3, *back_in(0))
    send_all(3)
    vec_one(0, by_skip, by_bias, by_decay)
    go("norm one")
    keep_act.wait()
    leave("act")
    in_time(r.ig, r.leave.at[1])
    slope0, by_bias_total0, by_gain_total0 = back_norm(3, 0)

    def last(rows, carry):
        live = wide(r.live[rows, :])
        upstream = r.ig[rows, :].astype(F32)
        grad = source_grad(0, rows, upstream, live, slope0, by_bias_total0, by_gain_total0)
        r.leave[0, rows, :] = t_mm(r.order[...], (live * grad).astype(BF16)).astype(BF16)
        return carry

    row_tiles(last, 0)
    keep_ig = pltpu.make_async_copy(r.leave.at[s], r.ig_out.at[s], r.local.at[6])
    keep_ig.start()
    give_ig = remote(r.leave.at[other], r.ig_out.at[s], r.far_send.at[5], r.far_recv.at[5], sibling)
    alone("ig", give_ig)

    go("last")
    go("end")
    while not all([one.step() is True for one in sums_of]):
        pass
    arrive("vec")
    total = r.vec_tot[s] + r.vec_far[...]
    r.small[0:5, :] = total[0:5]
    grad_re, grad_im = total[5:6, :STATES], total[5:6, STATES:]
    grad_rate = total[6:7, :STATES] * jnp.exp(-double) / scale_sq - (grad_re * decay_re + grad_im * decay_im)
    r.small[5:6, :STATES] = grad_rate * rate
    r.small[5:6, STATES:] = (grad_im * decay_re - grad_re * decay_im) * phase
    r.small[6:8, :] = jnp.zeros((2, D), F32)

    keep_ig.wait()
    for one in results:
        one.finish()
    end_all()


def results_kernel(
    tokens, act, ig, grads, small, o_act, o_ig, o_glu, o_out, o_in, o_gain, o_bias, o_nu, o_theta, o_skip, o_bglu,
    act_v, ig_v, ig_f, grads_v, grads_f, act_sem, ig_sem, grad_sem,
):
    copy = pltpu.make_async_copy
    act_in = [copy(act.at[i], act_v.at[i], act_sem.at[i, 0]) for i in range(MICRO)]
    ig_in = [copy(ig.at[i], ig_v.at[i], ig_sem.at[i, 0]) for i in range(MICRO)]
    parts = [pl.ds(GRAD_AT[i], GRAD_ROWS[i]) for i in (GLU, OUT, IN)]
    grads_in = [copy(grads.at[parts[i]], grads_v.at[parts[i]], grad_sem.at[i, 0]) for i in (GLU, OUT, IN)]
    for one in ig_in + grads_in + act_in:
        one.start()
    o_gain[...] = small[0:1, :]
    o_bias[...] = small[1:2, :]
    o_skip[...] = small[2:3, :]
    o_bglu[:, :D] = small[3:4, :]
    o_bglu[:, D:] = small[4:5, :]
    o_nu[...] = small[5:6, :STATES]
    o_theta[...] = small[5:6, STATES:]
    out = []

    def leave(src, dst, sem):
        out.append(copy(src, dst, sem))
        out[-1].start()

    for i in range(MICRO):
        ig_in[i].wait()

        def tile(j, carry, i=i):
            rows = pl.ds(pl.multiple_of(j * 64, 64), 64)
            ig_f[i, rows, :] = ig_v[i, rows, :].astype(F32)
            return carry

        lax.fori_loop(0, tokens // 64, tile, 0)
        leave(ig_f.at[i], o_ig.at[i], ig_sem.at[i, 1])
    for i, dst in ((GLU, o_glu), (OUT, o_out), (IN, o_in)):
        grads_in[i].wait()
        for c in range(GRAD_ROWS[i] // D):
            at = GRAD_AT[i] + c * D
            cols = slice(GRAD_AT[i] // 4 + c * LANES, GRAD_AT[i] // 4 + (c + 1) * LANES)
            grads_f[:, cols] = grads_v[at : at + D, :].astype(F32)
        leave(grads_f.at[:, GRAD_AT[i] // 4 : (GRAD_AT[i] + GRAD_ROWS[i]) // 4], dst, grad_sem.at[i, 1])
    for i in range(MICRO):
        act_in[i].wait()
        leave(act_v.at[i], o_act.at[i], act_sem.at[i, 1])
    for one in out:
        one.wait()


def body(ns, nd, inputs, mask, gain, bias, nu, theta, w_in, w_out, skip, w_glu, b_glu, cotangent):
    per = inputs.shape[0] // MICRO
    span = inputs.shape[1]
    tokens = per * span
    segs = tokens // SEG
    dma = pltpu.SemaphoreType.DMA
    vmem = pltpu.VMEM
    names_in = ["x", "cot", "mask", "gain", "bias", "nu", "theta", "skip", "bglu", "w_in", "w_out", "w_glu"]
    any_in = {"x", "cot", "w_in", "w_out", "w_glu"}
    outs = {
        "act_out": jax.ShapeDtypeStruct((MICRO, tokens, D), BF16),
        "ig_out": jax.ShapeDtypeStruct((MICRO, tokens, D), BF16),
        "grads": jax.ShapeDtypeStruct((ALL_ROWS, LANES), BF16),
        "small": jax.ShapeDtypeStruct((8, D), F32),
    }
    any_out = {"act_out", "ig_out", "grads"}
    half = ALL_ROWS // 2
    scratch = {
        "act": vmem((3, tokens, D), BF16),
        "cotv": vmem((tokens, D), BF16),
        "live": vmem((tokens, LANES), F32),
        "win": vmem((2, D, D), BF16),
        "wout": vmem((2, D, D), BF16),
        "wglu": vmem((2, D, 2 * D), BF16),
        "prm": vmem((2, 8, D), F32),
        "stat": vmem((2, 8, D), F32),
        "scaled": vmem((2, tokens, D), BF16),
        "u": vmem((2, 4, tokens, LANES), F32),
        "st": vmem((2, 4, tokens, LANES), F32),
        "start": vmem((2, 4, segs, LANES), F32),
        "readout": vmem((2, tokens, D), BF16),
        "active": vmem((2, tokens, D), BF16),
        "slope": vmem((2, tokens, D), F32),
        "gate": vmem((tokens, D), F32),
        "steep": vmem((tokens, D), F32),
        "gg": vmem((tokens, 2 * D), BF16),
        "gm": vmem((tokens, D), BF16),
        "adj": vmem((4, tokens, LANES), F32),
        "ig": vmem((tokens, D), BF16),
        "leave": vmem((2, tokens, D), BF16),
        "order": vmem((ROWS, ROWS), BF16),
        "bnb": vmem((4, ns * nd, 9, LANES), F32),
        "scb": vmem((4, ns, 4 * per, LANES), F32),
        "dw": vmem((2, ALL_ROWS, LANES), BF16),
        "sec": vmem((2, half, LANES), BF16),
        "half": vmem((2, half, LANES), BF16),
        "gat": vmem((2, half, LANES), BF16),
        "slots": vmem((slot_rows(ns, nd)[-1], LANES), BF16),
        "vec_a": vmem((2, ns, 8, D), F32),
        "vec_b": vmem((2, nd, 8, D), F32),
        "vec_tot": vmem((2, 8, D), F32),
        "vec_far": vmem((8, D), F32),
        "local": dma((7,)),
        "own": dma((len(FLAT),)),
        "far_send": dma((7,)),
        "far_recv": dma((7,)),
        "bn_send": dma((4,)),
        "bn_recv": dma((4,)),
        "sc_send": dma((4,)),
        "sc_recv": dma((4,)),
        "core_send": dma((len(FLAT),)),
        "core_recv": dma((len(FLAT),)),
        "rs_send": dma((len(FLAT), DEPTH)),
        "rs_recv": dma((len(FLAT), DEPTH)),
        "ag_send": dma((len(FLAT), DEPTH)),
        "ag_recv": dma((len(FLAT), DEPTH)),
        "va_send": dma((2,)),
        "va_recv": dma((2,)),
        "vb_send": dma((2,)),
        "vb_recv": dma((2,)),
    }
    in_any = pl.BlockSpec(memory_space=pl.ANY)
    in_vmem = pl.BlockSpec(memory_space=pltpu.VMEM)
    names = names_in + list(outs) + list(scratch)
    act, ig, grads, small = pl.pallas_call(
        functools.partial(kernel, ns, nd, per, span, names),
        out_shape=list(outs.values()),
        in_specs=[in_any if name in any_in else in_vmem for name in names_in],
        out_specs=[in_any if name in any_out else in_vmem for name in outs],
        scratch_shapes=list(scratch.values()),
        compiler_params=pltpu.CompilerParams(
            collective_id=0, has_side_effects=True, vmem_limit_bytes=61 * 2**20
        ),
    )(
        inputs.reshape(MICRO, tokens, D),
        cotangent.reshape(MICRO, tokens, D),
        mask,
        gain,
        bias,
        nu,
        theta,
        skip,
        b_glu,
        w_in,
        w_out,
        w_glu,
    )

    wide_out = [(1, D), (1, D), (1, STATES), (1, STATES), (1, D), (1, 2 * D)]
    big_out = [((MICRO, tokens, D), BF16), ((MICRO, tokens, D), F32)]
    big_out += [((D, GRAD_ROWS[which] // 4), F32) for which in (GLU, OUT, IN)]
    act, ig, d_glu, d_out, d_in, d_gain, d_bias, d_nu, d_theta, d_skip, d_bglu = pl.pallas_call(
        functools.partial(results_kernel, tokens),
        out_shape=[jax.ShapeDtypeStruct(*x) for x in big_out] + [jax.ShapeDtypeStruct(x, F32) for x in wide_out],
        in_specs=[in_any] * 3 + [in_vmem],
        out_specs=[in_any] * 5 + [in_vmem] * 6,
        scratch_shapes=[
            vmem((MICRO, tokens, D), BF16),
            vmem((MICRO, tokens, D), BF16),
            vmem((MICRO, tokens, D), F32),
            vmem((ALL_ROWS, LANES), BF16),
            vmem((D, ALL_ROWS // 4), F32),
            dma((2, 2)),
            dma((2, 2)),
            dma((3, 2)),
        ],
        compiler_params=pltpu.CompilerParams(vmem_limit_bytes=60 * 2**20),
    )(act, ig, grads, small)
    whole = (1, MICRO * per, span, D)
    return (
        act.reshape(whole),
        ig.reshape(whole),
        d_gain,
        d_bias,
        d_nu,
        d_theta,
        d_in[None],
        d_out[None],
        d_skip,
        d_glu[None],
        d_bglu,
    )


def solution(mesh):
    rows = P("section", None)
    cube = P("section", None, None)
    tokens = P("dp", "seq", None)
    spread = P("section", "dp", "seq", None)
    in_specs = (tokens, P("dp", "seq"), rows, rows, rows, rows, cube, cube, rows, cube, rows, tokens)
    out_specs = (spread, spread, rows, rows, rows, rows, cube, cube, rows, cube, rows)
    return jax.shard_map(
        functools.partial(body, mesh.shape["seq"], mesh.shape["dp"]),
        mesh=mesh,
        in_specs=in_specs,
        out_specs=out_specs,
        check_vma=False,
    )
```

```python
import functools
import math
import types

import jax
import jax.numpy as jnp
from jax import lax
from jax.experimental import pallas as pl
from jax.experimental.pallas import tpu as pltpu
from jax.sharding import PartitionSpec as P

D = 512
STATES = 256
MICRO = 2
EPS = 1e-05
LANES = 128
ROWS = 256
SEG = 32
EIGHT = 8
GLU, OUT, IN = 0, 1, 2
GRAD_ROWS = (4096, 2048, 2048)
GRAD_AT = (0, 4096, 6144)
ALL_ROWS = 8192
SD = ("seq", "dp")
DS = ("dp", "seq")
PARTS = (
    ((0, 1536, SD), (1536, 1536, SD), (3072, 1024, DS),),
    ((0, 1024, SD), (1024, 1024, DS),),
    ((0, 2048, SD),),
    ((0, 4096, SD),),
    ((0, 2048, SD),),
    ((0, 1536, SD), (1536, 512, DS),),
)
FLAT = tuple((n, *part) for n, parts in enumerate(PARTS) for part in parts)
DEPTH = max(len(part[-1]) for part in FLAT)
PLAN = {
    "carry two": (104, 103, 7),
    "filled two": (),
    "norm two": (105, 6, 7, 8, 9),
    "through": (7,),
    "carry one": (200, 100, 6, 7, 101, 8),
    "filled one": (3, 2, 9),
    "norm one": (0, 102, 1, 8, 3, 2, 6, 5),
    "last": (8, 1, 9, 0, 6, 201),
    "end": (4, 0, 5, 4, 3, 1, 2, 0, 5, 2, 4, 1, 202, 4, 203, 204, 9, 3, 5),
}
ROOT = math.sqrt(2.0 / math.pi)
CUBE = 0.044715

F32 = jnp.float32
BF16 = jnp.bfloat16
MESH = pl.DeviceIdType.MESH


def mm(a, b):
    return lax.dot_general(a, b, (((1,), (0,)), ((), ())), preferred_element_type=F32)


def mm_t(a, b):
    return lax.dot_general(a, b, (((1,), (1,)), ((), ())), preferred_element_type=F32)


def t_mm(a, b):
    return lax.dot_general(a, b, (((0,), (0,)), ((), ())), preferred_element_type=F32)


def complex_mul(ar, ai, br, bi):
    return ar * br - ai * bi, ar * bi + ai * br


def power(re, im, n):
    out = None
    while n:
        if n & 1:
            out = (re, im) if out is None else complex_mul(*out, re, im)
        n >>= 1
        if n:
            re, im = complex_mul(re, im, re, im)
    return out


def as_row(four):
    return jnp.concatenate([four[c : c + 1] for c in range(4)], axis=1)


def wide(tile):
    return jnp.concatenate([tile] * 4, axis=1)


def column_sum(x):
    return jnp.sum(x, axis=0, keepdims=True)


def slots_of(rows, counts, spread):
    out, start = [], 0
    for level, count in enumerate(counts):
        size = rows if spread and level == len(counts) - 1 else rows // count
        out.append((start, size))
        start += count * size
        rows //= count
    return out


def slot_rows(ns, nd):
    inner = next(n for n in range(math.isqrt(ns), 0, -1) if ns % n == 0)
    sizes = {"seq": ns, "dp": nd, "in": inner, "out": ns // inner}
    bases = [0]
    for _, _, rows, order in FLAT:
        counts = [sizes[name] for name in order]
        spread = rows // 2 // math.prod(counts) % 16 != 0
        start, size = slots_of(rows // 2, counts, spread)[-1]
        bases.append(bases[-1] + start + counts[-1] * size)
    return bases


def kernel(ns, nd, per, span, names, *refs):
    r = types.SimpleNamespace(**dict(zip(names, refs)))
    tokens = per * span
    segs = tokens // SEG
    nseg = span // SEG
    tiles = tokens // ROWS
    blocks = segs // EIGHT
    peers = ns * nd
    s = lax.axis_index("section")
    d = lax.axis_index("dp")
    q = lax.axis_index("seq")
    other = 1 - s
    me = d * ns + q
    sibling = {"section": other}

    def seq_peer(k):
        return {"seq": lax.rem(q + k, ns)}

    def dp_peer(k):
        return {"dp": lax.rem(d + k, nd)}

    def any_peer(k):
        at = lax.rem(me + k, peers)
        return {"dp": at // ns, "seq": lax.rem(at, ns)}

    def remote(src, dst, send, recv, device):
        return pltpu.make_async_remote_copy(
            src_ref=src, dst_ref=dst, send_sem=send, recv_sem=recv, device_id=device, device_id_type=MESH
        )

    def over(low, high, body):
        lax.fori_loop(low, high, lambda k, c: (body(k), c)[1], 0)

    arriving = {}
    leaving = {}

    def begin(key, start, whole):
        start()
        arriving[key] = leaving[key] = whole

    def arrive(key):
        arriving.pop(key).wait_recv()

    def leave(key):
        leaving.pop(key).wait_send()

    def end_all():
        for key in list(arriving):
            arrive(key)
        for key in list(leaving):
            leave(key)

    def alone(key, copy):
        begin(key, copy.start, copy)

    def row_tiles(body, init):
        def step(i, carry):
            return body(pl.ds(pl.multiple_of(i * ROWS, ROWS), ROWS), carry)

        return lax.fori_loop(0, tiles, step, init, unroll=4)

    slot_base = slot_rows(ns, nd)

    def skewed(tile, sums):
        waiting, running = [pl.ds(i * ROWS, ROWS) for i in range(tiles)], []
        while waiting or running:
            if waiting:
                running.append(tile(waiting.pop(0), sums))
            running = [one for one in running if next(one, True) is not True]
        return sums

    barrier = pltpu.get_barrier_semaphore()

    def greet(device):
        pl.semaphore_signal(barrier, inc=1, device_id=device, device_id_type=MESH)

    distant = [*range(nd - 1, 0, -2), *range(nd - 2, 0, -2), 0]
    others = [(a, b) for a in distant for b in range(ns - 1, -1, -1) if a or b]

    def each_other(body):
        if len(others) > 15:
            over(1, peers, lambda k: body(any_peer(k)))
            return
        for a, b in others:
            body({"dp": lax.rem(d + a, nd), "seq": lax.rem(q + b, ns)})

    each_other(greet)
    greet(sibling)
    over(1, ns, lambda k: greet({"section": other, **seq_peer(k)}))
    over(1, nd, lambda k: greet({"section": other, **dp_peer(k)}))

    load_x = pltpu.make_async_copy(r.x.at[s], r.act.at[0], r.local.at[0])
    load_x.start()
    load_small = [
        pltpu.make_async_copy(src, dst, r.local.at[8 + i])
        for i, (src, dst) in enumerate(
            (
                (r.mask, r.mask_v),
                (r.nu, r.nu_v),
                (r.theta, r.theta_v),
                (r.gain, r.gain_v),
                (r.bias, r.bias_v),
                (r.skip, r.skip_v),
                (r.bglu, r.bglu_v),
            )
        )
    ]
    for copy in load_small:
        copy.start()
    load_cot = pltpu.make_async_copy(r.cot.at[s], r.cotv, r.local.at[1])
    weights = ((r.w_in, r.win), (r.w_out, r.wout), (r.w_glu, r.wglu))
    load_w = [
        pltpu.make_async_copy(src.at[0], dst.at[s], r.local.at[2 + i]) for i, (src, dst) in enumerate(weights)
    ]
    for copy in load_w:
        copy.start()
    load_cot.start()
    for copy in load_small:
        copy.wait()

    rate = jnp.exp(r.nu_v[...])
    phase = jnp.exp(r.theta_v[...])
    size = jnp.exp(-rate)
    decay_re = size * jnp.cos(phase)
    decay_im = size * jnp.sin(phase)
    double = 2.0 * rate
    scale_sq = double * (
        1.0
        - double / 2.0 * (1.0 - double / 3.0 * (1.0 - double / 4.0 * (1.0 - double / 5.0 * (1.0 - double / 6.0))))
    )
    scale = jnp.sqrt(scale_sq)
    r.prm[s, 0:1, :] = r.gain_v[...]
    r.prm[s, 1:2, :] = r.bias_v[...]
    r.prm[s, 2:3, :] = r.skip_v[...]
    r.prm[s, 3:4, :] = r.bglu_v[:, :D]
    r.prm[s, 4:5, :] = r.bglu_v[:, D:]
    r.prm[s, 5:6, :] = jnp.concatenate([decay_re, decay_im], axis=1)
    r.prm[s, 6:7, :] = jnp.concatenate([scale, scale], axis=1)
    r.prm[s, 7:8, :] = jnp.zeros((1, D), F32)

    count = jnp.zeros((1, 1), F32)
    row = lax.broadcasted_iota(jnp.int32, (tokens, LANES), 0)
    token = (row & -ROWS) + (row & (EIGHT - 1)) * SEG + ((row & (ROWS - 1)) >> (EIGHT.bit_length() - 1))
    live = jnp.zeros((tokens, LANES), F32)
    for i in range(per):
        here = jnp.sum(r.mask_v[pl.ds(s * per + i, 1), :], axis=1, keepdims=True)
        live = jnp.where((token >= i * span) & (token < i * span + here), 1.0, live)
        count = count + here.astype(F32)
    r.live[...] = live
    count_row = jnp.broadcast_to(count, (1, LANES))
    to_row = lax.broadcasted_iota(jnp.int32, (ROWS, ROWS), 0)
    from_row = lax.broadcasted_iota(jnp.int32, (ROWS, ROWS), 1)
    came_from = (to_row & (EIGHT - 1)) * SEG + (to_row >> (EIGHT.bit_length() - 1))
    r.order[...] = jnp.where(from_row == came_from, 1.0, 0.0).astype(BF16)
    load_x.wait()

    def mask_input(rows, total):
        x = mm(r.order[...], r.act[0, rows, :]) * wide(r.live[rows, :])
        r.act[0, rows, :] = x.astype(BF16)
        return total + column_sum(x)

    def centred(b, mean):
        def tile(rows, total):
            off = (r.act[b, rows, :].astype(F32) - mean) * wide(r.live[rows, :])
            return total + column_sum(off * off)

        return row_tiles(tile, jnp.zeros((1, D), F32))

    def put_rows(ph, upper, lower):
        for c in range(4):
            r.bnb[ph, me, c : c + 1, :] = upper[:, c * LANES : (c + 1) * LANES]
            r.bnb[ph, me, 4 + c : 5 + c, :] = lower[:, c * LANES : (c + 1) * LANES]
        r.bnb[ph, me, 8:9, :] = count_row

    def to_all(ph, device):
        block = r.bnb.at[ph, me]
        return remote(block, block, r.bn_send.at[ph], r.bn_recv.at[ph], device)

    def send_all(ph):
        blocks = r.bnb.at[ph, pl.ds(0, peers - 1)]
        whole = remote(blocks, blocks, r.bn_send.at[ph], r.bn_recv.at[ph], sibling)
        begin(("all", ph), lambda: each_other(lambda device: to_all(ph, device).start()), whole)

    def wait_all(ph):
        arrive(("all", ph))

    def norm_sums(b, total):
        mean = total / jnp.maximum(wide(count_row), 1.0)
        put_rows(b, mean, centred(b, mean))

    def norm_merge(b):
        wait_all(b)
        got = r.bnb[b]
        means, spreads, counts = got[:, 0:4, :], got[:, 4:8, :], got[:, 8:9, :]
        valid = jnp.sum(counts, axis=0)
        mean = jnp.sum(counts * means, axis=0) / valid
        apart = means - mean[None]
        spread = jnp.sum(spreads + counts * apart * apart, axis=0)
        r.stat[b, 0:1, :] = as_row(mean)
        r.stat[b, 1:2, :] = as_row(lax.rsqrt(spread / valid + EPS))
        r.stat[b, 2:3, :] = wide(valid)

    norm_sums(0, row_tiles(mask_input, jnp.zeros((1, D), F32)))

    pl.semaphore_wait(barrier, peers + ns - 1 + nd - 1)
    send_all(0)
    send_prm = remote(r.prm.at[s], r.prm.at[s], r.far_send.at[0], r.far_recv.at[0], sibling)
    send_w = [
        remote(src.at[0], dst.at[s], r.far_send.at[1 + i], r.far_recv.at[1 + i], sibling)
        for i, (src, dst) in enumerate(weights)
    ]

    alone("prm", send_prm)
    for i, copy in enumerate(send_w):
        alone(("w", i), copy)

    def decay(b, sign):
        out = []
        for c in range(2):
            re = r.prm[b, 5:6, c * LANES : (c + 1) * LANES]
            im = r.prm[b, 5:6, STATES + c * LANES : STATES + (c + 1) * LANES]
            out.append((re, sign * im))
        return out

    def step_rows(k, l):
        return pl.ds(pl.multiple_of(k * ROWS + l * EIGHT, EIGHT), EIGHT)

    def at_step(ref, l):
        return jnp.concatenate([ref[step_rows(k, l), :] for k in range(blocks)], axis=0)

    def put_step(ref, l, value):
        for k in range(blocks):
            ref[step_rows(k, l), :] = value[k * EIGHT : (k + 1) * EIGHT]

    def advance(a, state, drive):
        return (
            a[0] * state[0] - a[1] * state[1] + drive[0],
            a[1] * state[0] + a[0] * state[1] + drive[1],
        )

    place = lax.rem(lax.broadcasted_iota(jnp.int32, (segs, LANES), 0), nseg)
    owner = lax.broadcasted_iota(jnp.int32, (segs, LANES), 0) // nseg

    def moved(x, k, reverse):
        if reverse:
            return jnp.where(place < nseg - k, pltpu.roll(x, segs - k, 0), 0.0)
        return jnp.where(place >= k, pltpu.roll(x, k, 0), 0.0)

    def seg_scan(re, im, jump, reverse):
        k = 1
        while k < nseg:
            add_re, add_im = complex_mul(*jump, moved(re, k, reverse), moved(im, k, reverse))
            re, im = re + add_re, im + add_im
            jump = complex_mul(*jump, *jump)
            k *= 2
        return re, im

    def to_seq(ph, k):
        block = r.scb.at[ph, q]
        return remote(block, block, r.sc_send.at[ph], r.sc_recv.at[ph], seq_peer(k))

    def carry(ph, drive, a, reverse, between):
        def step(i, states):
            l = SEG - 1 - i if reverse else i
            return tuple(
                advance(a[c], states[c], (at_step(drive.at[c], l), at_step(drive.at[2 + c], l))) for c in range(2)
            )

        zero = jnp.zeros((segs, LANES), F32)
        ends = lax.fori_loop(0, SEG, step, ((zero, zero), (zero, zero)), unroll=4)
        jumps = [power(*a[c], SEG) for c in range(2)]
        sums = [seg_scan(*ends[c], jumps[c], reverse) for c in range(2)]
        for i in range(per):
            last = i * nseg if reverse else (i + 1) * nseg - 1
            for c in range(2):
                r.scb[ph, q, 4 * i + c : 4 * i + c + 1, :] = sums[c][0][last : last + 1]
                r.scb[ph, q, 4 * i + 2 + c : 4 * i + 3 + c, :] = sums[c][1][last : last + 1]
        ends_of = r.scb.at[ph, pl.ds(0, ns - 1)]
        whole = remote(ends_of, ends_of, r.sc_send.at[ph], r.sc_recv.at[ph], sibling)
        begin(("seq", ph), lambda: over(1, ns, lambda k: to_seq(ph, k).start()), whole)
        first = jnp.where(place == (nseg - 1 if reverse else 0), 1.0, 0.0)
        reach = [seg_scan(first, zero, jumps[c], reverse) for c in range(2)]
        between()
        arrive(("seq", ph))
        starts = []
        for c in range(2):
            far = power(*a[c], span)
            entering = []
            for i in range(per):
                re = jnp.zeros((1, LANES), F32)
                im = jnp.zeros((1, LANES), F32)
                for lap in range(ns):
                    j = ns - 1 - lap if reverse else lap
                    before = j > q if reverse else j < q
                    new_re, new_im = advance(
                        far,
                        (re, im),
                        (r.scb[ph, j, 4 * i + c : 4 * i + c + 1, :], r.scb[ph, j, 4 * i + 2 + c : 4 * i + 3 + c, :]),
                    )
                    re = jnp.where(before, new_re, re)
                    im = jnp.where(before, new_im, im)
                entering.append((re, im))
            in_re = jnp.broadcast_to(entering[0][0], (segs, LANES))
            in_im = jnp.broadcast_to(entering[0][1], (segs, LANES))
            for i in range(1, per):
                in_re = jnp.where(owner == i, entering[i][0], in_re)
                in_im = jnp.where(owner == i, entering[i][1], in_im)
            add_re, add_im = complex_mul(*reach[c], in_re, in_im)
            starts.append((moved(sums[c][0], 1, reverse) + add_re, moved(sums[c][1], 1, reverse) + add_im))
        return starts

    def fill_states(b, starts, a, reverse):
        for c in range(2):
            r.start[b, c] = starts[c][0]
            r.start[b, 2 + c] = starts[c][1]

        def step(i, states):
            l = SEG - 1 - i if reverse else i
            out = []
            for c in range(2):
                new = advance(a[c], states[c], (at_step(r.u.at[b, c], l), at_step(r.u.at[b, 2 + c], l)))
                put_step(r.st.at[b, c], l, new[0])
                put_step(r.st.at[b, 2 + c], l, new[1])
                out.append(new)
            return tuple(out)

        lax.fori_loop(0, SEG, step, tuple(starts), unroll=4)

    def fill_adjoint(b, starts, a, reverse):
        back = 1 if not reverse else -1
        zero = jnp.zeros((segs, LANES), F32)
        sums = []
        for c in range(2):
            scale_c = r.prm[b, 6:7, c * LANES : (c + 1) * LANES]

            def one(l, prior, carry, c=c, scale_c=scale_c):
                state, by_re, by_im, by_scale = carry
                re, im = advance(a[c], state, (at_step(r.adj.at[c], l), at_step(r.adj.at[2 + c], l)))
                put_step(r.adj.at[c], l, scale_c * re)
                put_step(r.adj.at[2 + c], l, scale_c * im)
                by_re = by_re + (re * prior[0] + im * prior[1])
                by_im = by_im + (im * prior[0] - re * prior[1])
                by_scale = by_scale + (re * at_step(r.u.at[b, c], l) + im * at_step(r.u.at[b, 2 + c], l))
                return (re, im), by_re, by_im, by_scale

            def step(i, carry, c=c, one=one):
                l = SEG - 1 - i if reverse else i
                prior = (at_step(r.st.at[b, c], l + back), at_step(r.st.at[b, 2 + c], l + back))
                return one(l, prior, carry)

            carry_c = lax.fori_loop(0, SEG - 1, step, (starts[c], zero, zero, zero), unroll=4)
            final = one(0 if reverse else SEG - 1, (r.start[b, c], r.start[b, 2 + c]), carry_c)
            sums.append([column_sum(x) for x in final[1:]])
        return [jnp.concatenate([sums[0][i], sums[1][i]], axis=1) for i in range(3)]

    def forward_in(b):
        gain, bias, scale_row = r.prm[b, 0:1, :], r.prm[b, 1:2, :], r.prm[b, 6:7, :]
        average = r.stat[b, 0:1, :]
        slope = r.stat[b, 1:2, :] * gain

        def tile(rows, _):
            x = r.act[b, rows, :].astype(F32)
            scaled = (wide(r.live[rows, :]) * ((x - average) * slope + bias)).astype(BF16)
            r.scaled[b, rows, :] = scaled
            yield
            u = mm(scaled, r.win[b])
            yield
            u = u * scale_row
            for c in range(4):
                r.u[b, c, rows, :] = u[:, c * LANES : (c + 1) * LANES]

        skewed(tile, [])

    def forward_out(b, finish, sums):
        skip = r.prm[b, 2:3, :]
        value_bias, half_gate_bias = r.prm[b, 3:4, :], 0.5 * r.prm[b, 4:5, :]

        def tile(rows, sums):
            readout = jnp.concatenate([r.st[b, c, rows, :] for c in range(4)], axis=1).astype(BF16)
            r.readout[b, rows, :] = readout
            through = mm(readout, r.wout[b])
            yield
            mixed = through + skip * r.scaled[b, rows, :].astype(F32)
            square = mixed * mixed
            t = jnp.tanh(mixed * (ROOT + (ROOT * CUBE) * square))
            half = 0.5 + 0.5 * t
            wide_active = mixed * half
            active = wide_active.astype(BF16)
            r.active[b, rows, :] = active
            r.slope[b, rows, :] = half + wide_active * ((1.0 - t) * (ROOT + (3.0 * ROOT * CUBE) * square))
            yield
            gated = mm(active, r.wglu[b])
            yield
            gate = 0.5 + 0.5 * jnp.tanh(0.5 * gated[:, D:] + half_gate_bias)
            product = (gated[:, :D] + value_bias) * gate
            live = wide(r.live[rows, :])
            result = (r.act[b, rows, :].astype(F32) + live * product).astype(BF16)
            r.act[b + 1, rows, :] = result
            yield from finish(rows, live, gate, product * (1.0 - gate), result, sums)

        return skewed(tile, sums)

    def back_tile(b, rows, outer, gate, steep, sums):
        grad_gated = jnp.concatenate([outer * gate, outer * steep], axis=1).astype(BF16)
        r.gg[rows, :] = grad_gated
        sums[1] = sums[1] + column_sum(grad_gated.astype(F32))
        yield
        grad_active = mm_t(grad_gated, r.wglu[b])
        yield
        grad_mixed = (r.slope[b, rows, :] * grad_active).astype(BF16)
        r.gm[rows, :] = grad_mixed
        sums[0] = sums[0] + column_sum(grad_mixed.astype(F32) * r.scaled[b, rows, :].astype(F32))
        yield
        grad_readout = mm_t(grad_mixed, r.wout[b])
        yield
        for c in range(4):
            r.adj[c, rows, :] = grad_readout[:, c * LANES : (c + 1) * LANES]

    def normed(b, rows):
        return (r.act[b, rows, :].astype(F32) - r.stat[b, 0:1, :]) * r.stat[b, 1:2, :]

    projected_grads = (r.cotv, r.ig)

    def round_adjoint(b):
        def tile(rows, carry):
            adjoint = jnp.concatenate([r.adj[c, rows, :] for c in range(4)], axis=1)
            projected_grads[b][rows, :] = adjoint.astype(BF16)
            return carry

        row_tiles(tile, 0)

    def back_in(b):
        skip = r.prm[b, 2:3, :]

        def tile(rows, sums):
            into = mm_t(projected_grads[b][rows, :], r.win[b])
            yield
            masked = wide(r.live[rows, :]) * (skip * r.gm[rows, :].astype(F32) + into)
            r.slope[b, rows, :] = masked
            sums[0] = sums[0] + column_sum(masked * normed(b, rows))
            sums[1] = sums[1] + column_sum(masked)

        zero = jnp.zeros((1, D), F32)
        return skewed(tile, [zero, zero])

    def back_norm(ph, b):
        wait_all(ph)
        got = jnp.sum(r.bnb[ph], axis=0)
        gain_total, bias_total = as_row(got[0:4]), as_row(got[4:8])
        r.vec_tot[b, 0:1, :] = gain_total
        r.vec_tot[b, 1:2, :] = bias_total
        slope = r.stat[b, 1:2, :] * r.prm[b, 0:1, :]
        per_token = slope / r.stat[b, 2:3, :]
        return slope, per_token * bias_total, per_token * gain_total

    def source_grad(b, rows, upstream, live, slope, by_bias, by_gain):
        return upstream + live * (slope * r.slope[b, rows, :] - by_bias - normed(b, rows) * by_gain)

    def weight_grad(b, which, left, right):
        columns = GRAD_ROWS[which] // 4

        def tile(j, carry):
            cols = pl.ds(pl.multiple_of(j * 256, 256), 256)
            grad = t_mm(left, right[:, cols]).astype(BF16)
            at = pl.multiple_of(GRAD_AT[which] + j * 1024, 1024)
            r.dw[b, pl.ds(at, 512), :] = grad[:, :LANES]
            r.dw[b, pl.ds(at + 512, 512), :] = grad[:, LANES:]
            return carry

        lax.fori_loop(0, columns // 256, tile, 0, unroll=2)

    inner = next(n for n in range(math.isqrt(ns), 0, -1) if ns % n == 0)
    outer = ns // inner
    q_out, q_in = q // inner, lax.rem(q, inner)
    axes = {
        "seq": (ns, q, seq_peer),
        "dp": (nd, d, dp_peer),
        "in": (inner, q_in, lambda k: {"seq": q_out * inner + lax.rem(q_in + k, inner)}),
        "out": (outer, q_out, lambda k: {"seq": lax.rem(q_out + k, outer) * inner + q_in}),
    }

    results = []

    class Reduced:
        def __init__(self, n):
            which, start, rows, order = FLAT[n]
            self.b, self.n, self.at = which // 3, n, GRAD_AT[which % 3] + start
            self.base = self.at // 2
            self.axes = [axes[name] for name in order]
            self.sizes, self.offsets = [rows // 2], [0]
            for count, index, _ in self.axes:
                self.sizes.append(self.sizes[-1] // count)
                self.offsets.append(self.offsets[-1] + index * self.sizes[-1])
            self.spread = self.sizes[-1] % 16 != 0
            self.slots = slots_of(rows // 2, [count for count, _, _ in self.axes], self.spread)
            self.slot_base = slot_base[self.n]
            self.steps = self.plan()

        def rows(self, offset, size):
            return pl.ds(pl.multiple_of(self.base + offset, 16), size)

        def to_core(self):
            size = self.sizes[0]
            src = r.dw.at[self.b, pl.ds(pl.multiple_of(self.at + other * size, 16), size)]
            return remote(src, r.sec.at[self.b, self.rows(0, size)], r.core_send.at[self.n], r.core_recv.at[self.n], sibling)

        def slot(self, level, index):
            start, size = self.slots[level]
            return pl.ds(pl.multiple_of(self.slot_base + start + index * size, 16), size)

        def scatter(self, level, k):
            count, index, peer = self.axes[level]
            if self.spread and level == len(self.axes) - 1:
                src = r.slots.at[self.slot(level, index)]
            else:
                size = self.sizes[level + 1]
                src = r.half.at[self.b, self.rows(self.offsets[level] + lax.rem(index + k, count) * size, size)]
            dst = r.slots.at[self.slot(level, index)]
            return remote(src, dst, r.rs_send.at[self.n, level], r.rs_recv.at[self.n, level], peer(k))

        def gather(self, level, k):
            block = r.gat.at[self.b, self.rows(self.offsets[level + 1], self.sizes[level + 1])]
            return remote(block, block, r.ag_send.at[self.n, level], r.ag_recv.at[self.n, level], self.axes[level][2](k))

        def place(self):
            return pl.ds(pl.multiple_of(self.at + s * self.sizes[0] + self.offsets[1], 16), self.sizes[1])

        def result(self, device, send):
            src = r.gat.at[self.b, self.rows(self.offsets[1], self.sizes[1])]
            target = {"section": self.b, **device}
            return remote(src, r.grads.at[self.place()], send, r.ag_recv.at[self.n, 0], target)

        def results_whole(self, parts):
            rows = r.grads.at[pl.ds(0, parts * self.sizes[1])]
            return remote(rows, rows, r.ag_send.at[self.n, 0], r.ag_recv.at[self.n, 0], sibling)

        def own(self):
            src = r.gat.at[self.b, self.rows(self.offsets[1], self.sizes[1])]
            return pltpu.make_async_copy(src, r.grads.at[self.place()], r.own.at[self.n])

        def across(self):
            return self.result({}, r.own.at[self.n])

        def each(self, level, body):
            over(1, self.axes[level][0], body)

        def first(self):
            size = self.sizes[0]
            arrive((self.n, "core"))
            mine = r.dw[self.b, pl.ds(pl.multiple_of(self.at + s * size, 16), size), :].astype(F32)
            there = r.sec[self.b, self.base : self.base + size, :].astype(F32)
            r.half[self.b, self.base : self.base + size, :] = (mine + there).astype(BF16)

        def collect(self, level):
            arrive((self.n, "scatter", level))
            count, index, _ = self.axes[level]
            last = level == len(self.axes) - 1
            if self.spread and last:
                total = sum(r.slots[self.slot(level, j), :].astype(F32) for j in range(count))
                r.gat[self.b, self.rows(self.offsets[level], self.sizes[level]), :] = total.astype(BF16)
                return
            here = self.rows(self.offsets[level + 1], self.sizes[level + 1])
            total = r.half[self.b, here, :].astype(F32)
            for k in range(1, count):
                total = total + r.slots[self.slot(level, lax.rem(index + k, count)), :].astype(F32)
            (r.gat if last else r.half)[self.b, here, :] = total.astype(BF16)

        def send(self, level):
            if self.spread and level == len(self.axes) - 1:
                here = self.rows(self.offsets[level], self.sizes[level])
                r.slots[self.slot(level, self.axes[level][1]), :] = r.half[self.b, here, :]
            start, size = self.slots[level]
            rows = r.slots.at[pl.ds(self.slot_base + start, (self.axes[level][0] - 1) * size)]
            whole = remote(rows, rows, r.rs_send.at[self.n, level], r.rs_recv.at[self.n, level], sibling)
            begin((self.n, "scatter", level), lambda: self.each(level, lambda k: self.scatter(level, k).start()), whole)

        def share(self, level):
            count, _, peer = self.axes[level]
            if level:
                rows = r.gat.at[self.b, pl.ds(self.base, (count - 1) * self.sizes[level + 1])]
                whole = remote(rows, rows, r.ag_send.at[self.n, level], r.ag_recv.at[self.n, level], sibling)
                begin((self.n, "gather", level), lambda: self.each(level, lambda k: self.gather(level, k).start()), whole)
                return
            self.each(0, lambda k: self.result(peer(k), r.ag_send.at[self.n, 0]).start())

            @pl.when(s == self.b)
            def _():
                self.own().start()

            @pl.when(s != self.b)
            def _():
                self.across().start()

            results.append(self)

        def finish(self):
            count = self.axes[0][0]

            @pl.when(s == self.b)
            def _():
                self.own().wait()
                self.results_whole(2 * count - 1).wait_recv()

            @pl.when(s != self.b)
            def _():
                self.across().wait_send()

            if count > 1:
                self.results_whole(count - 1).wait_send()

        def plan(self):
            depth = len(self.axes)
            top = depth - 2 if self.spread else depth - 1
            yield alone((self.n, "core"), self.to_core())
            self.first()
            yield self.send(0)
            for level in range(1, depth):
                self.collect(level - 1)
                yield self.send(level)
            self.collect(depth - 1)
            yield self.share(top)
            for level in range(top, 0, -1):
                arrive((self.n, "gather", level))
                yield self.share(level - 1)

        def step(self):
            return next(self.steps, True)

    sums_of = [Reduced(n) for n in range(len(FLAT))]

    factors = ((r.active, (r.gg, r.gg)), (r.readout, (r.gm, r.gm)), (r.scaled, projected_grads))

    def go(gap):
        for n in PLAN[gap]:
            if n < 100:
                sums_of[n].step()
                continue
            if n >= 200:
                vec_steps[n - 200]()
                continue
            b, which = (n - 100) // 3, (n - 100) % 3
            left, right = factors[which]
            weight_grad(b, which, left[b], right[b])
            for one, part in zip(sums_of, FLAT):
                if part[0] == n - 100:
                    one.step()

    def vec_seq(b, k):
        block = r.vec_a.at[b, q]
        return remote(block, block, r.va_send.at[b], r.va_recv.at[b], seq_peer(k))

    def vec_dp(b, k):
        block = r.vec_b.at[b, d]
        return remote(block, block, r.vb_send.at[b], r.vb_recv.at[b], dp_peer(k))

    def vec_one(b, by_skip, by_bias, by_decay):
        zero = jnp.zeros((1, D), F32)
        r.vec_a[b, q, 0:1, :] = zero
        r.vec_a[b, q, 1:2, :] = zero
        r.vec_a[b, q, 2:3, :] = by_skip
        r.vec_a[b, q, 3:4, :] = by_bias[:, :D]
        r.vec_a[b, q, 4:5, :] = by_bias[:, D:]
        r.vec_a[b, q, 5:6, :] = jnp.concatenate([by_decay[0], by_decay[1]], axis=1)
        r.vec_a[b, q, 6:7, :] = jnp.concatenate([by_decay[2], by_decay[2]], axis=1)
        r.vec_a[b, q, 7:8, :] = zero
        rows = r.vec_a.at[b, pl.ds(0, ns - 1)]
        whole = remote(rows, rows, r.va_send.at[b], r.va_recv.at[b], sibling)
        begin(("vec_seq", b), lambda: over(1, ns, lambda k: vec_seq(b, k).start()), whole)

    def vec_two(b):
        arrive(("vec_seq", b))
        r.vec_b[b, d] = jnp.sum(r.vec_a[b], axis=0)
        rows = r.vec_b.at[b, pl.ds(0, nd - 1)]
        whole = remote(rows, rows, r.vb_send.at[b], r.vb_recv.at[b], sibling)
        begin(("vec_dp", b), lambda: over(1, nd, lambda k: vec_dp(b, k).start()), whole)

    def vec_three(b):
        arrive(("vec_dp", b))
        total = jnp.sum(r.vec_b[b], axis=0)
        r.vec_tot[b, 2:8, :] = total[2:8]

    def vec_last():
        vec_three(1)
        vec_three(0)
        alone("vec", remote(r.vec_tot.at[other], r.vec_far, r.far_send.at[6], r.far_recv.at[6], sibling))

    keep_small = pltpu.make_async_copy(r.small_v, r.small, r.local.at[7])

    def small_out():
        arrive("vec")
        total = r.vec_tot[s] + r.vec_far[...]
        r.small_v[0:5, :] = total[0:5]
        grad_re, grad_im = total[5:6, :STATES], total[5:6, STATES:]
        grad_rate = total[6:7, :STATES] * jnp.exp(-double) / scale_sq - (grad_re * decay_re + grad_im * decay_im)
        r.small_v[5:6, :STATES] = grad_rate * rate
        r.small_v[5:6, STATES:] = (grad_im * decay_re - grad_re * decay_im) * phase
        r.small_v[6:8, :] = jnp.zeros((2, D), F32)
        keep_small.start()

    def let_go():
        for key in [key for key in leaving if key not in arriving]:
            leave(key)

    vec_steps = (lambda: vec_two(1), lambda: vec_two(0), vec_last, small_out, let_go)

    arrive("prm")
    for i in range(3):
        load_w[i].wait()
        arrive(("w", i))
    load_cot.wait()

    def order_cot(rows, carry):
        r.cotv[rows, :] = mm(r.order[...], r.cotv[rows, :]).astype(BF16)
        return carry

    row_tiles(order_cot, 0)

    def in_time(src, dst):
        def tile(rows, carry):
            dst[rows, :] = t_mm(r.order[...], src[rows, :]).astype(BF16)
            return carry

        row_tiles(tile, 0)

    zero_row = jnp.zeros((1, D), F32)

    def nothing():
        pass

    norm_merge(0)
    forward_in(0)
    ahead0, ahead1 = decay(0, 1.0), decay(1, 1.0)
    starts = carry(0, r.u.at[0], ahead0, False, nothing)
    fill_states(0, starts, ahead0, False)

    def finish_one(rows, live, gate, steep, result, sums):
        r.gate[rows, :] = gate
        r.steep[rows, :] = steep
        sums[0] = sums[0] + column_sum(result.astype(F32))
        yield

    norm_sums(1, forward_out(0, finish_one, [zero_row])[0])
    send_all(1)
    in_time(r.act.at[1], r.leave.at[0])
    norm_merge(1)
    forward_in(1)
    starts = carry(1, r.u.at[1], ahead1, True, nothing)
    fill_states(1, starts, ahead1, True)

    def finish_two(rows, live, gate, steep, result, sums):
        return back_tile(1, rows, live * r.cotv[rows, :].astype(F32), gate, steep, sums)

    wide_zero = jnp.zeros((1, 2 * D), F32)
    by_skip, by_bias = forward_out(1, finish_two, [zero_row, wide_zero])

    keep_act = pltpu.make_async_copy(r.leave.at[s], r.act_out.at[s], r.local.at[5])
    give_act = remote(r.leave.at[other], r.act_out.at[s], r.far_send.at[4], r.far_recv.at[4], sibling)

    back0, back1 = decay(0, -1.0), decay(1, -1.0)

    def first_pieces():
        go("carry two")
        in_time(r.act.at[2], r.leave.at[1])
        keep_act.start()
        alone("act", give_act)

    starts = carry(2, r.adj, back1, False, first_pieces)
    by_decay = fill_adjoint(1, starts, back1, False)
    round_adjoint(1)
    go("filled two")
    put_rows(2, *back_in(1))
    send_all(2)
    vec_one(1, by_skip, by_bias, by_decay)
    go("norm two")
    slope, by_bias_total, by_gain_total = back_norm(2, 1)

    def through(rows, sums):
        live = wide(r.live[rows, :])
        upstream = r.cotv[rows, :].astype(F32)
        grad = source_grad(1, rows, upstream, live, slope, by_bias_total, by_gain_total).astype(BF16)
        r.ig[rows, :] = grad
        yield from back_tile(0, rows, live * grad.astype(F32), r.gate[rows, :], r.steep[rows, :], sums)

    by_skip, by_bias = skewed(through, [zero_row, wide_zero])
    go("through")

    def next_pieces():
        go("carry one")

    starts = carry(3, r.adj, back0, True, next_pieces)
    by_decay = fill_adjoint(0, starts, back0, True)
    round_adjoint(0)
    go("filled one")
    put_rows(3, *back_in(0))
    send_all(3)
    vec_one(0, by_skip, by_bias, by_decay)
    go("norm one")
    keep_act.wait()
    leave("act")
    in_time(r.ig, r.leave.at[1])
    slope0, by_bias_total0, by_gain_total0 = back_norm(3, 0)

    def last(rows, carry):
        live = wide(r.live[rows, :])
        upstream = r.ig[rows, :].astype(F32)
        grad = source_grad(0, rows, upstream, live, slope0, by_bias_total0, by_gain_total0)
        r.leave[0, rows, :] = t_mm(r.order[...], (live * grad).astype(BF16)).astype(BF16)
        return carry

    row_tiles(last, 0)
    keep_ig = pltpu.make_async_copy(r.leave.at[s], r.ig_out.at[s], r.local.at[6])
    keep_ig.start()
    give_ig = remote(r.leave.at[other], r.ig_out.at[s], r.far_send.at[5], r.far_recv.at[5], sibling)
    alone("ig", give_ig)

    go("last")
    go("end")
    while not all([one.step() is True for one in sums_of]):
        pass
    keep_ig.wait()
    keep_small.wait()
    for one in results:
        one.finish()
    end_all()


def results_kernel(
    tokens, act, ig, grads, small, o_act, o_ig, o_glu, o_out, o_in, o_gain, o_bias, o_nu, o_theta, o_skip, o_bglu,
    act_v, ig_v, ig_f, grads_v, grads_f, small_v, gain_v, bias_v, nu_v, theta_v, skip_v, bglu_v,
    act_sem, ig_sem, grad_sem, small_sem,
):
    copy = pltpu.make_async_copy
    act_in = [copy(act.at[i], act_v.at[i], act_sem.at[i, 0]) for i in range(MICRO)]
    ig_in = [copy(ig.at[i], ig_v.at[i], ig_sem.at[i, 0]) for i in range(MICRO)]
    parts = [pl.ds(GRAD_AT[i], GRAD_ROWS[i]) for i in (GLU, OUT, IN)]
    grads_in = [copy(grads.at[parts[i]], grads_v.at[parts[i]], grad_sem.at[i, 0]) for i in (GLU, OUT, IN)]
    small_in = copy(small, small_v, small_sem.at[0])
    for one in [small_in] + ig_in + grads_in + act_in:
        one.start()
    out = []

    def leave(src, dst, sem):
        out.append(copy(src, dst, sem))
        out[-1].start()

    for i in range(MICRO):
        ig_in[i].wait()

        def tile(j, carry, i=i):
            rows = pl.ds(pl.multiple_of(j * 64, 64), 64)
            ig_f[i, rows, :] = ig_v[i, rows, :].astype(F32)
            return carry

        lax.fori_loop(0, tokens // 64, tile, 0)
        leave(ig_f.at[i], o_ig.at[i], ig_sem.at[i, 1])
    small_in.wait()
    gain_v[...] = small_v[0:1, :]
    bias_v[...] = small_v[1:2, :]
    skip_v[...] = small_v[2:3, :]
    bglu_v[:, :D] = small_v[3:4, :]
    bglu_v[:, D:] = small_v[4:5, :]
    nu_v[...] = small_v[5:6, :STATES]
    theta_v[...] = small_v[5:6, STATES:]
    small_out = ((gain_v, o_gain), (bias_v, o_bias), (nu_v, o_nu), (theta_v, o_theta), (skip_v, o_skip), (bglu_v, o_bglu))
    for i, (src, dst) in enumerate(small_out):
        leave(src, dst, small_sem.at[1 + i])
    for i, dst in ((GLU, o_glu), (OUT, o_out), (IN, o_in)):
        grads_in[i].wait()
        for c in range(GRAD_ROWS[i] // D):
            at = GRAD_AT[i] + c * D
            cols = slice(GRAD_AT[i] // 4 + c * LANES, GRAD_AT[i] // 4 + (c + 1) * LANES)
            grads_f[:, cols] = grads_v[at : at + D, :].astype(F32)
        leave(grads_f.at[:, GRAD_AT[i] // 4 : (GRAD_AT[i] + GRAD_ROWS[i]) // 4], dst, grad_sem.at[i, 1])
    for i in range(MICRO):
        act_in[i].wait()
        leave(act_v.at[i], o_act.at[i], act_sem.at[i, 1])
    for one in out:
        one.wait()


def body(ns, nd, inputs, mask, gain, bias, nu, theta, w_in, w_out, skip, w_glu, b_glu, cotangent):
    per = inputs.shape[0] // MICRO
    span = inputs.shape[1]
    tokens = per * span
    segs = tokens // SEG
    dma = pltpu.SemaphoreType.DMA
    vmem = pltpu.VMEM
    names_in = ["x", "cot", "mask", "gain", "bias", "nu", "theta", "skip", "bglu", "w_in", "w_out", "w_glu"]
    outs = {
        "act_out": jax.ShapeDtypeStruct((MICRO, tokens, D), BF16),
        "ig_out": jax.ShapeDtypeStruct((MICRO, tokens, D), BF16),
        "grads": jax.ShapeDtypeStruct((ALL_ROWS, LANES), BF16),
        "small": jax.ShapeDtypeStruct((8, D), F32),
    }
    half = ALL_ROWS // 2
    scratch = {
        "act": vmem((3, tokens, D), BF16),
        "cotv": vmem((tokens, D), BF16),
        "live": vmem((tokens, LANES), F32),
        "win": vmem((2, D, D), BF16),
        "wout": vmem((2, D, D), BF16),
        "wglu": vmem((2, D, 2 * D), BF16),
        "prm": vmem((2, 8, D), F32),
        "stat": vmem((2, 8, D), F32),
        "scaled": vmem((2, tokens, D), BF16),
        "u": vmem((2, 4, tokens, LANES), F32),
        "st": vmem((2, 4, tokens, LANES), F32),
        "start": vmem((2, 4, segs, LANES), F32),
        "readout": vmem((2, tokens, D), BF16),
        "active": vmem((2, tokens, D), BF16),
        "slope": vmem((2, tokens, D), F32),
        "gate": vmem((tokens, D), F32),
        "steep": vmem((tokens, D), F32),
        "gg": vmem((tokens, 2 * D), BF16),
        "gm": vmem((tokens, D), BF16),
        "adj": vmem((4, tokens, LANES), F32),
        "ig": vmem((tokens, D), BF16),
        "leave": vmem((2, tokens, D), BF16),
        "order": vmem((ROWS, ROWS), BF16),
        "bnb": vmem((4, ns * nd, 9, LANES), F32),
        "scb": vmem((4, ns, 4 * per, LANES), F32),
        "dw": vmem((2, ALL_ROWS, LANES), BF16),
        "sec": vmem((2, half, LANES), BF16),
        "half": vmem((2, half, LANES), BF16),
        "gat": vmem((2, half, LANES), BF16),
        "slots": vmem((slot_rows(ns, nd)[-1], LANES), BF16),
        "vec_a": vmem((2, ns, 8, D), F32),
        "vec_b": vmem((2, nd, 8, D), F32),
        "vec_tot": vmem((2, 8, D), F32),
        "vec_far": vmem((8, D), F32),
        "mask_v": vmem(mask.shape, jnp.int32),
        "nu_v": vmem((1, STATES), F32),
        "theta_v": vmem((1, STATES), F32),
        "gain_v": vmem((1, D), F32),
        "bias_v": vmem((1, D), F32),
        "skip_v": vmem((1, D), F32),
        "bglu_v": vmem((1, 2 * D), F32),
        "small_v": vmem((8, D), F32),
        "local": dma((15,)),
        "own": dma((len(FLAT),)),
        "far_send": dma((7,)),
        "far_recv": dma((7,)),
        "bn_send": dma((4,)),
        "bn_recv": dma((4,)),
        "sc_send": dma((4,)),
        "sc_recv": dma((4,)),
        "core_send": dma((len(FLAT),)),
        "core_recv": dma((len(FLAT),)),
        "rs_send": dma((len(FLAT), DEPTH)),
        "rs_recv": dma((len(FLAT), DEPTH)),
        "ag_send": dma((len(FLAT), DEPTH)),
        "ag_recv": dma((len(FLAT), DEPTH)),
        "va_send": dma((2,)),
        "va_recv": dma((2,)),
        "vb_send": dma((2,)),
        "vb_recv": dma((2,)),
    }
    in_any = pl.BlockSpec(memory_space=pl.ANY)
    names = names_in + list(outs) + list(scratch)
    act, ig, grads, small = pl.pallas_call(
        functools.partial(kernel, ns, nd, per, span, names),
        out_shape=list(outs.values()),
        in_specs=[in_any] * len(names_in),
        out_specs=[in_any] * len(outs),
        scratch_shapes=list(scratch.values()),
        compiler_params=pltpu.CompilerParams(
            collective_id=0, has_side_effects=True, vmem_limit_bytes=61 * 2**20
        ),
    )(
        inputs.reshape(MICRO, tokens, D),
        cotangent.reshape(MICRO, tokens, D),
        mask,
        gain,
        bias,
        nu,
        theta,
        skip,
        b_glu,
        w_in,
        w_out,
        w_glu,
    )

    wide_out = [(1, D), (1, D), (1, STATES), (1, STATES), (1, D), (1, 2 * D)]
    big_out = [((MICRO, tokens, D), BF16), ((MICRO, tokens, D), F32)]
    big_out += [((D, GRAD_ROWS[which] // 4), F32) for which in (GLU, OUT, IN)]
    act, ig, d_glu, d_out, d_in, d_gain, d_bias, d_nu, d_theta, d_skip, d_bglu = pl.pallas_call(
        functools.partial(results_kernel, tokens),
        out_shape=[jax.ShapeDtypeStruct(*x) for x in big_out] + [jax.ShapeDtypeStruct(x, F32) for x in wide_out],
        in_specs=[in_any] * 4,
        out_specs=[in_any] * 11,
        scratch_shapes=[
            vmem((MICRO, tokens, D), BF16),
            vmem((MICRO, tokens, D), BF16),
            vmem((MICRO, tokens, D), F32),
            vmem((ALL_ROWS, LANES), BF16),
            vmem((D, ALL_ROWS // 4), F32),
            vmem((8, D), F32),
            *[vmem(x, F32) for x in wide_out],
            dma((2, 2)),
            dma((2, 2)),
            dma((3, 2)),
            dma((7,)),
        ],
        compiler_params=pltpu.CompilerParams(vmem_limit_bytes=60 * 2**20),
    )(act, ig, grads, small)
    whole = (1, MICRO * per, span, D)
    return (
        act.reshape(whole),
        ig.reshape(whole),
        d_gain,
        d_bias,
        d_nu,
        d_theta,
        d_in[None],
        d_out[None],
        d_skip,
        d_glu[None],
        d_bglu,
    )


def solution(mesh):
    rows = P("section", None)
    cube = P("section", None, None)
    tokens = P("dp", "seq", None)
    spread = P("section", "dp", "seq", None)
    in_specs = (tokens, P("dp", "seq"), rows, rows, rows, rows, cube, cube, rows, cube, rows, tokens)
    out_specs = (spread, spread, rows, rows, rows, rows, cube, cube, rows, cube, rows)
    return jax.shard_map(
        functools.partial(body, mesh.shape["seq"], mesh.shape["dp"]),
        mesh=mesh,
        in_specs=in_specs,
        out_specs=out_specs,
        check_vma=False,
    )
```

```python
import functools
import math
import types

import jax
import jax.numpy as jnp
from jax import lax
from jax.experimental import pallas as pl
from jax.experimental.pallas import tpu as pltpu
from jax.sharding import PartitionSpec as P

D = 512
STATES = 256
MICRO = 2
EPS = 1e-05
LANES = 128
ROWS = 256
SEG = 32
EIGHT = 8
GLU, OUT, IN = 0, 1, 2
GRAD_ROWS = (4096, 2048, 2048)
GRAD_AT = (0, 4096, 6144)
ALL_ROWS = 8192
SD = ("seq", "dp")
DS = ("dp", "seq")
PARTS = (
    ((0, 2560, SD), (2560, 1536, DS),),
    ((0, 2048, SD),),
    ((0, 1536, SD), (1536, 512, DS),),
    ((0, 2048, SD), (2048, 2048, SD),),
    ((0, 2048, SD),),
    ((0, 2048, SD),),
)
FLAT = tuple((n, *part) for n, parts in enumerate(PARTS) for part in parts)
DEPTH = max(len(part[-1]) for part in FLAT)
PLAN = {
    "carry two": (104, 103, 7),
    "filled two": (),
    "norm two": (5, 105, 7, 6, 8),
    "through": (7,),
    "carry one": (200, 101, 5, 7, 6, 8, 2, 100, 5),
    "filled one": (0, 1, 8, 5),
    "norm one": (2, 102, 4, 6, 1, 3, 0, 1, 8),
    "last": (201,),
    "end": (4, 2, 6, 3, 4, 0, 2, 202, 3, 1, 203, 204, 0, 3, 4),
}
ROOT = math.sqrt(2.0 / math.pi)
CUBE = 0.044715

F32 = jnp.float32
BF16 = jnp.bfloat16
MESH = pl.DeviceIdType.MESH


def mm(a, b):
    return lax.dot_general(a, b, (((1,), (0,)), ((), ())), preferred_element_type=F32)


def mm_t(a, b):
    return lax.dot_general(a, b, (((1,), (1,)), ((), ())), preferred_element_type=F32)


def t_mm(a, b):
    return lax.dot_general(a, b, (((0,), (0,)), ((), ())), preferred_element_type=F32)


def complex_mul(ar, ai, br, bi):
    return ar * br - ai * bi, ar * bi + ai * br


def power(re, im, n):
    out = None
    while n:
        if n & 1:
            out = (re, im) if out is None else complex_mul(*out, re, im)
        n >>= 1
        if n:
            re, im = complex_mul(re, im, re, im)
    return out


def as_row(four):
    return jnp.concatenate([four[c : c + 1] for c in range(4)], axis=1)


def wide(tile):
    return jnp.concatenate([tile] * 4, axis=1)


def column_sum(x):
    return jnp.sum(x, axis=0, keepdims=True)


def slots_of(rows, counts, spread):
    out, start = [], 0
    for level, count in enumerate(counts):
        size = rows if spread and level == len(counts) - 1 else rows // count
        out.append((start, size))
        start += count * size
        rows //= count
    return out


def slot_rows(ns, nd):
    inner = next(n for n in range(math.isqrt(ns), 0, -1) if ns % n == 0)
    sizes = {"seq": ns, "dp": nd, "in": inner, "out": ns // inner}
    bases = [0]
    for _, _, rows, order in FLAT:
        counts = [sizes[name] for name in order]
        spread = rows // 2 // math.prod(counts) % 16 != 0
        start, size = slots_of(rows // 2, counts, spread)[-1]
        bases.append(bases[-1] + start + counts[-1] * size)
    return bases


def kernel(ns, nd, per, span, names, *refs):
    r = types.SimpleNamespace(**dict(zip(names, refs)))
    tokens = per * span
    segs = tokens // SEG
    nseg = span // SEG
    tiles = tokens // ROWS
    blocks = segs // EIGHT
    peers = ns * nd
    s = lax.axis_index("section")
    d = lax.axis_index("dp")
    q = lax.axis_index("seq")
    other = 1 - s
    me = d * ns + q
    sibling = {"section": other}

    def seq_peer(k):
        return {"seq": lax.rem(q + k, ns)}

    def dp_peer(k):
        return {"dp": lax.rem(d + k, nd)}

    def any_peer(k):
        at = lax.rem(me + k, peers)
        return {"dp": at // ns, "seq": lax.rem(at, ns)}

    def remote(src, dst, send, recv, device):
        return pltpu.make_async_remote_copy(
            src_ref=src, dst_ref=dst, send_sem=send, recv_sem=recv, device_id=device, device_id_type=MESH
        )

    def over(low, high, body):
        lax.fori_loop(low, high, lambda k, c: (body(k), c)[1], 0)

    arriving = {}
    leaving = {}

    def begin(key, start, whole, later=False):
        start()
        arriving[key] = whole
        if not later:
            leaving[key] = whole

    def arrive(key):
        arriving.pop(key).wait_recv()

    def leave(key):
        leaving.pop(key).wait_send()

    def end_all():
        for key in list(arriving):
            arrive(key)
        for key in list(leaving):
            leave(key)

    def alone(key, copy, later=False):
        begin(key, copy.start, copy, later)

    def row_tiles(body, init):
        def step(i, carry):
            return body(pl.ds(pl.multiple_of(i * ROWS, ROWS), ROWS), carry)

        return lax.fori_loop(0, tiles, step, init, unroll=4)

    slot_base = slot_rows(ns, nd)

    def skewed(tile, sums):
        waiting, running = [pl.ds(i * ROWS, ROWS) for i in range(tiles)], []
        while waiting or running:
            if waiting:
                running.append(tile(waiting.pop(0), sums))
            running = [one for one in running if next(one, True) is not True]
        return sums

    barrier = pltpu.get_barrier_semaphore()

    def greet(device):
        pl.semaphore_signal(barrier, inc=1, device_id=device, device_id_type=MESH)

    distant = [*range(nd - 1, 0, -2), *range(nd - 2, 0, -2), 0]
    others = [(a, b) for a in distant for b in range(ns - 1, -1, -1) if a or b]

    def each_other(body):
        if len(others) > 15:
            over(1, peers, lambda k: body(any_peer(k)))
            return
        for a, b in others:
            body({"dp": lax.rem(d + a, nd), "seq": lax.rem(q + b, ns)})

    each_other(greet)
    greet(sibling)
    over(1, ns, lambda k: greet({"section": other, **seq_peer(k)}))
    over(1, nd, lambda k: greet({"section": other, **dp_peer(k)}))

    load_x = pltpu.make_async_copy(r.x.at[s], r.act.at[0], r.local.at[0])
    load_x.start()
    load_small = [
        pltpu.make_async_copy(src, dst, r.local.at[8 + i])
        for i, (src, dst) in enumerate(
            (
                (r.mask, r.mask_v),
                (r.nu, r.nu_v),
                (r.theta, r.theta_v),
                (r.gain, r.gain_v),
                (r.bias, r.bias_v),
                (r.skip, r.skip_v),
                (r.bglu, r.bglu_v),
            )
        )
    ]
    for copy in load_small:
        copy.start()
    load_cot = pltpu.make_async_copy(r.cot.at[s], r.cotv, r.local.at[1])
    weights = ((r.w_in, r.win), (r.w_out, r.wout), (r.w_glu, r.wglu))
    load_w = [
        pltpu.make_async_copy(src.at[0], dst.at[s], r.local.at[2 + i]) for i, (src, dst) in enumerate(weights)
    ]
    for copy in load_w:
        copy.start()
    load_cot.start()
    for copy in load_small:
        copy.wait()

    rate = jnp.exp(r.nu_v[...])
    phase = jnp.exp(r.theta_v[...])
    size = jnp.exp(-rate)
    decay_re = size * jnp.cos(phase)
    decay_im = size * jnp.sin(phase)
    double = 2.0 * rate
    scale_sq = double * (
        1.0
        - double / 2.0 * (1.0 - double / 3.0 * (1.0 - double / 4.0 * (1.0 - double / 5.0 * (1.0 - double / 6.0))))
    )
    scale = jnp.sqrt(scale_sq)
    r.prm[s, 0:1, :] = r.gain_v[...]
    r.prm[s, 1:2, :] = r.bias_v[...]
    r.prm[s, 2:3, :] = r.skip_v[...]
    r.prm[s, 3:4, :] = r.bglu_v[:, :D]
    r.prm[s, 4:5, :] = r.bglu_v[:, D:]
    r.prm[s, 5:6, :] = jnp.concatenate([decay_re, decay_im], axis=1)
    r.prm[s, 6:7, :] = jnp.concatenate([scale, scale], axis=1)
    r.prm[s, 7:8, :] = jnp.zeros((1, D), F32)

    count = jnp.zeros((1, 1), F32)
    row = lax.broadcasted_iota(jnp.int32, (tokens, LANES), 0)
    token = (row & -ROWS) + (row & (EIGHT - 1)) * SEG + ((row & (ROWS - 1)) >> (EIGHT.bit_length() - 1))
    live = jnp.zeros((tokens, LANES), F32)
    for i in range(per):
        here = jnp.sum(r.mask_v[pl.ds(s * per + i, 1), :], axis=1, keepdims=True)
        live = jnp.where((token >= i * span) & (token < i * span + here), 1.0, live)
        count = count + here.astype(F32)
    r.live[...] = live
    count_row = jnp.broadcast_to(count, (1, LANES))
    to_row = lax.broadcasted_iota(jnp.int32, (ROWS, ROWS), 0)
    from_row = lax.broadcasted_iota(jnp.int32, (ROWS, ROWS), 1)
    came_from = (to_row & (EIGHT - 1)) * SEG + (to_row >> (EIGHT.bit_length() - 1))
    r.order[...] = jnp.where(from_row == came_from, 1.0, 0.0).astype(BF16)
    load_x.wait()

    def mask_input(rows, total):
        x = mm(r.order[...], r.act[0, rows, :]) * wide(r.live[rows, :])
        r.act[0, rows, :] = x.astype(BF16)
        return total + column_sum(x)

    def centred(b, mean):
        def tile(rows, total):
            off = (r.act[b, rows, :].astype(F32) - mean) * wide(r.live[rows, :])
            return total + column_sum(off * off)

        return row_tiles(tile, jnp.zeros((1, D), F32))

    def put_rows(ph, upper, lower):
        for c in range(4):
            r.bnb[ph, me, c : c + 1, :] = upper[:, c * LANES : (c + 1) * LANES]
            r.bnb[ph, me, 4 + c : 5 + c, :] = lower[:, c * LANES : (c + 1) * LANES]
        r.bnb[ph, me, 8:9, :] = count_row

    def to_all(ph, device):
        block = r.bnb.at[ph, me]
        return remote(block, block, r.bn_send.at[ph], r.bn_recv.at[ph], device)

    def send_all(ph):
        blocks = r.bnb.at[ph, pl.ds(0, peers - 1)]
        whole = remote(blocks, blocks, r.bn_send.at[ph], r.bn_recv.at[ph], sibling)
        begin(("all", ph), lambda: each_other(lambda device: to_all(ph, device).start()), whole)

    def wait_all(ph):
        arrive(("all", ph))

    def norm_sums(b, total):
        mean = total / jnp.maximum(wide(count_row), 1.0)
        put_rows(b, mean, centred(b, mean))

    def norm_merge(b):
        wait_all(b)
        got = r.bnb[b]
        means, spreads, counts = got[:, 0:4, :], got[:, 4:8, :], got[:, 8:9, :]
        valid = jnp.sum(counts, axis=0)
        mean = jnp.sum(counts * means, axis=0) / valid
        apart = means - mean[None]
        spread = jnp.sum(spreads + counts * apart * apart, axis=0)
        r.stat[b, 0:1, :] = as_row(mean)
        r.stat[b, 1:2, :] = as_row(lax.rsqrt(spread / valid + EPS))
        r.stat[b, 2:3, :] = wide(valid)

    norm_sums(0, row_tiles(mask_input, jnp.zeros((1, D), F32)))

    pl.semaphore_wait(barrier, peers + ns - 1 + nd - 1)
    send_all(0)
    send_prm = remote(r.prm.at[s], r.prm.at[s], r.far_send.at[0], r.far_recv.at[0], sibling)
    send_w = [
        remote(src.at[0], dst.at[s], r.far_send.at[1 + i], r.far_recv.at[1 + i], sibling)
        for i, (src, dst) in enumerate(weights)
    ]

    alone("prm", send_prm)
    for i, copy in enumerate(send_w):
        alone(("w", i), copy)

    def decay(b, sign):
        out = []
        for c in range(2):
            re = r.prm[b, 5:6, c * LANES : (c + 1) * LANES]
            im = r.prm[b, 5:6, STATES + c * LANES : STATES + (c + 1) * LANES]
            out.append((re, sign * im))
        return out

    def step_rows(k, l):
        return pl.ds(pl.multiple_of(k * ROWS + l * EIGHT, EIGHT), EIGHT)

    def at_step(ref, l):
        return jnp.concatenate([ref[step_rows(k, l), :] for k in range(blocks)], axis=0)

    def put_step(ref, l, value):
        for k in range(blocks):
            ref[step_rows(k, l), :] = value[k * EIGHT : (k + 1) * EIGHT]

    def advance(a, state, drive):
        return (
            a[0] * state[0] - a[1] * state[1] + drive[0],
            a[1] * state[0] + a[0] * state[1] + drive[1],
        )

    place = lax.rem(lax.broadcasted_iota(jnp.int32, (segs, LANES), 0), nseg)
    owner = lax.broadcasted_iota(jnp.int32, (segs, LANES), 0) // nseg

    def moved(x, k, reverse):
        if reverse:
            return jnp.where(place < nseg - k, pltpu.roll(x, segs - k, 0), 0.0)
        return jnp.where(place >= k, pltpu.roll(x, k, 0), 0.0)

    def seg_scan(re, im, jump, reverse):
        k = 1
        while k < nseg:
            add_re, add_im = complex_mul(*jump, moved(re, k, reverse), moved(im, k, reverse))
            re, im = re + add_re, im + add_im
            jump = complex_mul(*jump, *jump)
            k *= 2
        return re, im

    def to_seq(ph, k):
        block = r.scb.at[ph, q]
        return remote(block, block, r.sc_send.at[ph], r.sc_recv.at[ph], seq_peer(k))

    def carry(ph, drive, a, reverse, between):
        def step(i, states):
            l = SEG - 1 - i if reverse else i
            return tuple(
                advance(a[c], states[c], (at_step(drive.at[c], l), at_step(drive.at[2 + c], l))) for c in range(2)
            )

        zero = jnp.zeros((segs, LANES), F32)
        ends = lax.fori_loop(0, SEG, step, ((zero, zero), (zero, zero)), unroll=4)
        jumps = [power(*a[c], SEG) for c in range(2)]
        sums = [seg_scan(*ends[c], jumps[c], reverse) for c in range(2)]
        for i in range(per):
            last = i * nseg if reverse else (i + 1) * nseg - 1
            for c in range(2):
                r.scb[ph, q, 4 * i + c : 4 * i + c + 1, :] = sums[c][0][last : last + 1]
                r.scb[ph, q, 4 * i + 2 + c : 4 * i + 3 + c, :] = sums[c][1][last : last + 1]
        ends_of = r.scb.at[ph, pl.ds(0, ns - 1)]
        whole = remote(ends_of, ends_of, r.sc_send.at[ph], r.sc_recv.at[ph], sibling)
        begin(("seq", ph), lambda: over(1, ns, lambda k: to_seq(ph, k).start()), whole)
        first = jnp.where(place == (nseg - 1 if reverse else 0), 1.0, 0.0)
        reach = [seg_scan(first, zero, jumps[c], reverse) for c in range(2)]
        between()
        arrive(("seq", ph))
        starts = []
        for c in range(2):
            far = power(*a[c], span)
            entering = []
            for i in range(per):
                re = jnp.zeros((1, LANES), F32)
                im = jnp.zeros((1, LANES), F32)
                for lap in range(ns):
                    j = ns - 1 - lap if reverse else lap
                    before = j > q if reverse else j < q
                    new_re, new_im = advance(
                        far,
                        (re, im),
                        (r.scb[ph, j, 4 * i + c : 4 * i + c + 1, :], r.scb[ph, j, 4 * i + 2 + c : 4 * i + 3 + c, :]),
                    )
                    re = jnp.where(before, new_re, re)
                    im = jnp.where(before, new_im, im)
                entering.append((re, im))
            in_re = jnp.broadcast_to(entering[0][0], (segs, LANES))
            in_im = jnp.broadcast_to(entering[0][1], (segs, LANES))
            for i in range(1, per):
                in_re = jnp.where(owner == i, entering[i][0], in_re)
                in_im = jnp.where(owner == i, entering[i][1], in_im)
            add_re, add_im = complex_mul(*reach[c], in_re, in_im)
            starts.append((moved(sums[c][0], 1, reverse) + add_re, moved(sums[c][1], 1, reverse) + add_im))
        return starts

    def fill_states(b, starts, a, reverse):
        for c in range(2):
            r.start[b, c] = starts[c][0]
            r.start[b, 2 + c] = starts[c][1]

        def step(i, states):
            l = SEG - 1 - i if reverse else i
            out = []
            for c in range(2):
                new = advance(a[c], states[c], (at_step(r.u.at[b, c], l), at_step(r.u.at[b, 2 + c], l)))
                put_step(r.st.at[b, c], l, new[0])
                put_step(r.st.at[b, 2 + c], l, new[1])
                out.append(new)
            return tuple(out)

        lax.fori_loop(0, SEG, step, tuple(starts), unroll=4)

    def fill_adjoint(b, starts, a, reverse):
        back = 1 if not reverse else -1
        zero = jnp.zeros((segs, LANES), F32)
        sums = []
        for c in range(2):
            scale_c = r.prm[b, 6:7, c * LANES : (c + 1) * LANES]

            def one(l, prior, carry, c=c, scale_c=scale_c):
                state, by_re, by_im, by_scale = carry
                re, im = advance(a[c], state, (at_step(r.adj.at[c], l), at_step(r.adj.at[2 + c], l)))
                put_step(r.adj.at[c], l, scale_c * re)
                put_step(r.adj.at[2 + c], l, scale_c * im)
                by_re = by_re + (re * prior[0] + im * prior[1])
                by_im = by_im + (im * prior[0] - re * prior[1])
                by_scale = by_scale + (re * at_step(r.u.at[b, c], l) + im * at_step(r.u.at[b, 2 + c], l))
                return (re, im), by_re, by_im, by_scale

            def step(i, carry, c=c, one=one):
                l = SEG - 1 - i if reverse else i
                prior = (at_step(r.st.at[b, c], l + back), at_step(r.st.at[b, 2 + c], l + back))
                return one(l, prior, carry)

            carry_c = lax.fori_loop(0, SEG - 1, step, (starts[c], zero, zero, zero), unroll=4)
            final = one(0 if reverse else SEG - 1, (r.start[b, c], r.start[b, 2 + c]), carry_c)
            sums.append([column_sum(x) for x in final[1:]])
        return [jnp.concatenate([sums[0][i], sums[1][i]], axis=1) for i in range(3)]

    def forward_in(b):
        gain, bias, scale_row = r.prm[b, 0:1, :], r.prm[b, 1:2, :], r.prm[b, 6:7, :]
        average = r.stat[b, 0:1, :]
        slope = r.stat[b, 1:2, :] * gain

        def tile(rows, _):
            x = r.act[b, rows, :].astype(F32)
            scaled = (wide(r.live[rows, :]) * ((x - average) * slope + bias)).astype(BF16)
            r.scaled[b, rows, :] = scaled
            yield
            u = mm(scaled, r.win[b])
            yield
            u = u * scale_row
            for c in range(4):
                r.u[b, c, rows, :] = u[:, c * LANES : (c + 1) * LANES]

        skewed(tile, [])

    def forward_out(b, finish, sums):
        skip = r.prm[b, 2:3, :]
        value_bias, half_gate_bias = r.prm[b, 3:4, :], 0.5 * r.prm[b, 4:5, :]

        def tile(rows, sums):
            readout = jnp.concatenate([r.st[b, c, rows, :] for c in range(4)], axis=1).astype(BF16)
            r.readout[b, rows, :] = readout
            through = mm(readout, r.wout[b])
            yield
            mixed = through + skip * r.scaled[b, rows, :].astype(F32)
            square = mixed * mixed
            t = jnp.tanh(mixed * (ROOT + (ROOT * CUBE) * square))
            half = 0.5 + 0.5 * t
            wide_active = mixed * half
            active = wide_active.astype(BF16)
            r.active[b, rows, :] = active
            r.slope[b, rows, :] = half + wide_active * ((1.0 - t) * (ROOT + (3.0 * ROOT * CUBE) * square))
            yield
            gated = mm(active, r.wglu[b])
            yield
            gate = 0.5 + 0.5 * jnp.tanh(0.5 * gated[:, D:] + half_gate_bias)
            product = (gated[:, :D] + value_bias) * gate
            live = wide(r.live[rows, :])
            result = (r.act[b, rows, :].astype(F32) + live * product).astype(BF16)
            r.act[b + 1, rows, :] = result
            yield from finish(rows, live, gate, product * (1.0 - gate), result, sums)

        return skewed(tile, sums)

    def back_tile(b, rows, outer, gate, steep, sums):
        grad_gated = jnp.concatenate([outer * gate, outer * steep], axis=1).astype(BF16)
        r.gg[rows, :] = grad_gated
        sums[1] = sums[1] + column_sum(grad_gated.astype(F32))
        yield
        grad_active = mm_t(grad_gated, r.wglu[b])
        yield
        grad_mixed = (r.slope[b, rows, :] * grad_active).astype(BF16)
        r.gm[rows, :] = grad_mixed
        sums[0] = sums[0] + column_sum(grad_mixed.astype(F32) * r.scaled[b, rows, :].astype(F32))
        yield
        grad_readout = mm_t(grad_mixed, r.wout[b])
        yield
        for c in range(4):
            r.adj[c, rows, :] = grad_readout[:, c * LANES : (c + 1) * LANES]

    def normed(b, rows):
        return (r.act[b, rows, :].astype(F32) - r.stat[b, 0:1, :]) * r.stat[b, 1:2, :]

    projected_grads = (r.cotv, r.ig)

    def round_adjoint(b):
        def tile(rows, carry):
            adjoint = jnp.concatenate([r.adj[c, rows, :] for c in range(4)], axis=1)
            projected_grads[b][rows, :] = adjoint.astype(BF16)
            return carry

        row_tiles(tile, 0)

    def back_in(b):
        skip = r.prm[b, 2:3, :]

        def tile(rows, sums):
            into = mm_t(projected_grads[b][rows, :], r.win[b])
            yield
            masked = wide(r.live[rows, :]) * (skip * r.gm[rows, :].astype(F32) + into)
            r.slope[b, rows, :] = masked
            sums[0] = sums[0] + column_sum(masked * normed(b, rows))
            sums[1] = sums[1] + column_sum(masked)

        zero = jnp.zeros((1, D), F32)
        return skewed(tile, [zero, zero])

    def back_norm(ph, b):
        wait_all(ph)
        got = jnp.sum(r.bnb[ph], axis=0)
        gain_total, bias_total = as_row(got[0:4]), as_row(got[4:8])
        r.vec_tot[b, 0:1, :] = gain_total
        r.vec_tot[b, 1:2, :] = bias_total
        slope = r.stat[b, 1:2, :] * r.prm[b, 0:1, :]
        per_token = slope / r.stat[b, 2:3, :]
        return slope, per_token * bias_total, per_token * gain_total

    def source_grad(b, rows, upstream, live, slope, by_bias, by_gain):
        return upstream + live * (slope * r.slope[b, rows, :] - by_bias - normed(b, rows) * by_gain)

    def weight_grad(b, which, left, right):
        columns = GRAD_ROWS[which] // 4

        def tile(j, carry):
            cols = pl.ds(pl.multiple_of(j * 256, 256), 256)
            grad = t_mm(left, right[:, cols]).astype(BF16)
            at = pl.multiple_of(GRAD_AT[which] + j * 1024, 1024)
            r.dw[b, pl.ds(at, 512), :] = grad[:, :LANES]
            r.dw[b, pl.ds(at + 512, 512), :] = grad[:, LANES:]
            return carry

        lax.fori_loop(0, columns // 256, tile, 0, unroll=2)

    inner = next(n for n in range(math.isqrt(ns), 0, -1) if ns % n == 0)
    outer = ns // inner
    q_out, q_in = q // inner, lax.rem(q, inner)
    axes = {
        "seq": (ns, q, seq_peer),
        "dp": (nd, d, dp_peer),
        "in": (inner, q_in, lambda k: {"seq": q_out * inner + lax.rem(q_in + k, inner)}),
        "out": (outer, q_out, lambda k: {"seq": lax.rem(q_out + k, outer) * inner + q_in}),
    }

    results = []

    class Reduced:
        def __init__(self, n):
            which, start, rows, order = FLAT[n]
            self.b, self.n, self.at = which // 3, n, GRAD_AT[which % 3] + start
            self.base = self.at // 2
            self.axes = [axes[name] for name in order]
            self.sizes, self.offsets = [rows // 2], [0]
            for count, index, _ in self.axes:
                self.sizes.append(self.sizes[-1] // count)
                self.offsets.append(self.offsets[-1] + index * self.sizes[-1])
            self.spread = self.sizes[-1] % 16 != 0
            self.slots = slots_of(rows // 2, [count for count, _, _ in self.axes], self.spread)
            self.slot_base = slot_base[self.n]
            self.steps = self.plan()

        def rows(self, offset, size):
            return pl.ds(pl.multiple_of(self.base + offset, 16), size)

        def to_core(self):
            size = self.sizes[0]
            src = r.dw.at[self.b, pl.ds(pl.multiple_of(self.at + other * size, 16), size)]
            return remote(src, r.sec.at[self.b, self.rows(0, size)], r.send.at[self.n], r.core_recv.at[self.n], sibling)

        def slot(self, level, index):
            start, size = self.slots[level]
            return pl.ds(pl.multiple_of(self.slot_base + start + index * size, 16), size)

        def scatter(self, level, k):
            count, index, peer = self.axes[level]
            if self.spread and level == len(self.axes) - 1:
                src = r.slots.at[self.slot(level, index)]
            else:
                size = self.sizes[level + 1]
                src = r.half.at[self.b, self.rows(self.offsets[level] + lax.rem(index + k, count) * size, size)]
            dst = r.slots.at[self.slot(level, index)]
            return remote(src, dst, r.send.at[self.n], r.rs_recv.at[self.n, level], peer(k))

        def gather(self, level, k):
            block = r.gat.at[self.b, self.rows(self.offsets[level + 1], self.sizes[level + 1])]
            return remote(block, block, r.send.at[self.n], r.ag_recv.at[self.n, level], self.axes[level][2](k))

        def place(self):
            return pl.ds(pl.multiple_of(self.at + s * self.sizes[0] + self.offsets[1], 16), self.sizes[1])

        def result(self, device, send):
            src = r.gat.at[self.b, self.rows(self.offsets[1], self.sizes[1])]
            target = {"section": self.b, **device}
            return remote(src, r.grads.at[self.place()], send, r.ag_recv.at[self.n, 0], target)

        def results_whole(self, parts):
            rows = r.grads.at[pl.ds(0, parts * self.sizes[1])]
            return remote(rows, rows, r.send.at[self.n], r.ag_recv.at[self.n, 0], sibling)

        def own(self):
            src = r.gat.at[self.b, self.rows(self.offsets[1], self.sizes[1])]
            return pltpu.make_async_copy(src, r.grads.at[self.place()], r.own.at[self.n])

        def across(self):
            return self.result({}, r.own.at[self.n])

        def each(self, level, body):
            over(1, self.axes[level][0], body)

        def first(self):
            size = self.sizes[0]
            arrive((self.n, "core"))
            mine = r.dw[self.b, pl.ds(pl.multiple_of(self.at + s * size, 16), size), :].astype(F32)
            there = r.sec[self.b, self.base : self.base + size, :].astype(F32)
            r.half[self.b, self.base : self.base + size, :] = (mine + there).astype(BF16)

        def collect(self, level):
            arrive((self.n, "scatter", level))
            count, index, _ = self.axes[level]
            last = level == len(self.axes) - 1
            if self.spread and last:
                total = sum(r.slots[self.slot(level, j), :].astype(F32) for j in range(count))
                r.gat[self.b, self.rows(self.offsets[level], self.sizes[level]), :] = total.astype(BF16)
                return
            here = self.rows(self.offsets[level + 1], self.sizes[level + 1])
            total = r.half[self.b, here, :].astype(F32)
            for k in range(1, count):
                total = total + r.slots[self.slot(level, lax.rem(index + k, count)), :].astype(F32)
            (r.gat if last else r.half)[self.b, here, :] = total.astype(BF16)

        def send(self, level):
            if self.spread and level == len(self.axes) - 1:
                here = self.rows(self.offsets[level], self.sizes[level])
                r.slots[self.slot(level, self.axes[level][1]), :] = r.half[self.b, here, :]
            start, size = self.slots[level]
            rows = r.slots.at[pl.ds(self.slot_base + start, (self.axes[level][0] - 1) * size)]
            whole = remote(rows, rows, r.send.at[self.n], r.rs_recv.at[self.n, level], sibling)
            begin((self.n, "scatter", level), lambda: self.each(level, lambda k: self.scatter(level, k).start()), whole, True)

        def share(self, level):
            count, _, peer = self.axes[level]
            if level:
                rows = r.gat.at[self.b, pl.ds(self.base, (count - 1) * self.sizes[level + 1])]
                whole = remote(rows, rows, r.send.at[self.n], r.ag_recv.at[self.n, level], sibling)
                begin((self.n, "gather", level), lambda: self.each(level, lambda k: self.gather(level, k).start()), whole, True)
                return
            self.each(0, lambda k: self.result(peer(k), r.send.at[self.n]).start())

            @pl.when(s == self.b)
            def _():
                self.own().start()

            @pl.when(s != self.b)
            def _():
                self.across().start()

            results.append(self)

        def finish(self):
            count = self.axes[0][0]

            @pl.when(s == self.b)
            def _():
                self.own().wait()
                self.results_whole(2 * count - 1).wait_recv()

            @pl.when(s != self.b)
            def _():
                self.across().wait_send()

            sent = self.sizes[0] + (count - 1) * self.sizes[1]
            top = len(self.axes) - (2 if self.spread else 1)
            for level, (n, _, _) in enumerate(self.axes):
                sent += (n - 1) * self.slots[level][1]
                if 0 < level <= top:
                    sent += (n - 1) * self.sizes[level + 1]
            rows = r.dw.at[self.b, pl.ds(0, sent)]
            remote(rows, rows, r.send.at[self.n], r.core_recv.at[self.n], sibling).wait_send()

        def plan(self):
            depth = len(self.axes)
            top = depth - 2 if self.spread else depth - 1
            yield alone((self.n, "core"), self.to_core(), True)
            self.first()
            yield self.send(0)
            for level in range(1, depth):
                self.collect(level - 1)
                yield self.send(level)
            self.collect(depth - 1)
            yield self.share(top)
            for level in range(top, 0, -1):
                arrive((self.n, "gather", level))
                yield self.share(level - 1)

        def step(self):
            return next(self.steps, True)

    sums_of = [Reduced(n) for n in range(len(FLAT))]

    factors = ((r.active, (r.gg, r.gg)), (r.readout, (r.gm, r.gm)), (r.scaled, projected_grads))

    def go(gap):
        for n in PLAN[gap]:
            if n < 100:
                sums_of[n].step()
                continue
            if n >= 200:
                vec_steps[n - 200]()
                continue
            b, which = (n - 100) // 3, (n - 100) % 3
            left, right = factors[which]
            weight_grad(b, which, left[b], right[b])
            for one, part in zip(sums_of, FLAT):
                if part[0] == n - 100:
                    one.step()

    def vec_seq(b, k):
        block = r.vec_a.at[b, q]
        return remote(block, block, r.va_send.at[b], r.va_recv.at[b], seq_peer(k))

    def vec_dp(b, k):
        block = r.vec_b.at[b, d]
        return remote(block, block, r.vb_send.at[b], r.vb_recv.at[b], dp_peer(k))

    def vec_one(b, by_skip, by_bias, by_decay):
        zero = jnp.zeros((1, D), F32)
        r.vec_a[b, q, 0:1, :] = zero
        r.vec_a[b, q, 1:2, :] = zero
        r.vec_a[b, q, 2:3, :] = by_skip
        r.vec_a[b, q, 3:4, :] = by_bias[:, :D]
        r.vec_a[b, q, 4:5, :] = by_bias[:, D:]
        r.vec_a[b, q, 5:6, :] = jnp.concatenate([by_decay[0], by_decay[1]], axis=1)
        r.vec_a[b, q, 6:7, :] = jnp.concatenate([by_decay[2], by_decay[2]], axis=1)
        r.vec_a[b, q, 7:8, :] = zero
        rows = r.vec_a.at[b, pl.ds(0, ns - 1)]
        whole = remote(rows, rows, r.va_send.at[b], r.va_recv.at[b], sibling)
        begin(("vec_seq", b), lambda: over(1, ns, lambda k: vec_seq(b, k).start()), whole)

    def vec_two(b):
        arrive(("vec_seq", b))
        r.vec_b[b, d] = jnp.sum(r.vec_a[b], axis=0)
        rows = r.vec_b.at[b, pl.ds(0, nd - 1)]
        whole = remote(rows, rows, r.vb_send.at[b], r.vb_recv.at[b], sibling)
        begin(("vec_dp", b), lambda: over(1, nd, lambda k: vec_dp(b, k).start()), whole)

    def vec_three(b):
        arrive(("vec_dp", b))
        total = jnp.sum(r.vec_b[b], axis=0)
        r.vec_tot[b, 2:8, :] = total[2:8]

    def vec_last():
        vec_three(1)
        vec_three(0)
        alone("vec", remote(r.vec_tot.at[other], r.vec_far, r.far_send.at[6], r.far_recv.at[6], sibling))

    keep_small = pltpu.make_async_copy(r.small_v, r.small, r.local.at[7])

    def small_out():
        arrive("vec")
        total = r.vec_tot[s] + r.vec_far[...]
        r.small_v[0:5, :] = total[0:5]
        grad_re, grad_im = total[5:6, :STATES], total[5:6, STATES:]
        grad_rate = total[6:7, :STATES] * jnp.exp(-double) / scale_sq - (grad_re * decay_re + grad_im * decay_im)
        r.small_v[5:6, :STATES] = grad_rate * rate
        r.small_v[5:6, STATES:] = (grad_im * decay_re - grad_re * decay_im) * phase
        r.small_v[6:8, :] = jnp.zeros((2, D), F32)
        keep_small.start()

    def let_go():
        for key in [key for key in leaving if key not in arriving]:
            leave(key)

    vec_steps = (lambda: vec_two(1), lambda: vec_two(0), vec_last, small_out, let_go)

    arrive("prm")
    for i in range(3):
        load_w[i].wait()
        arrive(("w", i))
    load_cot.wait()

    def order_cot(rows, carry):
        r.cotv[rows, :] = mm(r.order[...], r.cotv[rows, :]).astype(BF16)
        return carry

    row_tiles(order_cot, 0)

    def in_time(src, dst):
        def tile(rows, carry):
            dst[rows, :] = t_mm(r.order[...], src[rows, :]).astype(BF16)
            return carry

        row_tiles(tile, 0)

    zero_row = jnp.zeros((1, D), F32)

    def nothing():
        pass

    norm_merge(0)
    forward_in(0)
    ahead0, ahead1 = decay(0, 1.0), decay(1, 1.0)
    starts = carry(0, r.u.at[0], ahead0, False, nothing)
    fill_states(0, starts, ahead0, False)

    def finish_one(rows, live, gate, steep, result, sums):
        r.gate[rows, :] = gate
        r.steep[rows, :] = steep
        sums[0] = sums[0] + column_sum(result.astype(F32))
        yield

    norm_sums(1, forward_out(0, finish_one, [zero_row])[0])
    send_all(1)
    in_time(r.act.at[1], r.leave.at[0])
    norm_merge(1)
    forward_in(1)
    starts = carry(1, r.u.at[1], ahead1, True, nothing)
    fill_states(1, starts, ahead1, True)

    def finish_two(rows, live, gate, steep, result, sums):
        return back_tile(1, rows, live * r.cotv[rows, :].astype(F32), gate, steep, sums)

    wide_zero = jnp.zeros((1, 2 * D), F32)
    by_skip, by_bias = forward_out(1, finish_two, [zero_row, wide_zero])

    keep_act = pltpu.make_async_copy(r.leave.at[s], r.act_out.at[s], r.local.at[5])
    give_act = remote(r.leave.at[other], r.act_out.at[s], r.far_send.at[4], r.far_recv.at[4], sibling)

    back0, back1 = decay(0, -1.0), decay(1, -1.0)

    def first_pieces():
        go("carry two")
        in_time(r.act.at[2], r.leave.at[1])
        keep_act.start()
        alone("act", give_act)

    starts = carry(2, r.adj, back1, False, first_pieces)
    by_decay = fill_adjoint(1, starts, back1, False)
    round_adjoint(1)
    go("filled two")
    put_rows(2, *back_in(1))
    send_all(2)
    vec_one(1, by_skip, by_bias, by_decay)
    go("norm two")
    slope, by_bias_total, by_gain_total = back_norm(2, 1)

    def through(rows, sums):
        live = wide(r.live[rows, :])
        upstream = r.cotv[rows, :].astype(F32)
        grad = source_grad(1, rows, upstream, live, slope, by_bias_total, by_gain_total).astype(BF16)
        r.ig[rows, :] = grad
        yield from back_tile(0, rows, live * grad.astype(F32), r.gate[rows, :], r.steep[rows, :], sums)

    by_skip, by_bias = skewed(through, [zero_row, wide_zero])
    go("through")

    def next_pieces():
        go("carry one")

    starts = carry(3, r.adj, back0, True, next_pieces)
    by_decay = fill_adjoint(0, starts, back0, True)
    round_adjoint(0)
    go("filled one")
    put_rows(3, *back_in(0))
    send_all(3)
    vec_one(0, by_skip, by_bias, by_decay)
    go("norm one")
    keep_act.wait()
    leave("act")
    in_time(r.ig, r.leave.at[1])
    slope0, by_bias_total0, by_gain_total0 = back_norm(3, 0)

    def last(rows, carry):
        live = wide(r.live[rows, :])
        upstream = r.ig[rows, :].astype(F32)
        grad = source_grad(0, rows, upstream, live, slope0, by_bias_total0, by_gain_total0)
        r.leave[0, rows, :] = t_mm(r.order[...], (live * grad).astype(BF16)).astype(BF16)
        return carry

    row_tiles(last, 0)
    keep_ig = pltpu.make_async_copy(r.leave.at[s], r.ig_out.at[s], r.local.at[6])
    keep_ig.start()
    give_ig = remote(r.leave.at[other], r.ig_out.at[s], r.far_send.at[5], r.far_recv.at[5], sibling)
    alone("ig", give_ig)

    go("last")
    go("end")
    while not all([one.step() is True for one in sums_of]):
        pass
    keep_ig.wait()
    keep_small.wait()
    for one in results:
        one.finish()
    end_all()


def results_kernel(
    tokens, act, ig, grads, small, o_act, o_ig, o_glu, o_out, o_in, o_gain, o_bias, o_nu, o_theta, o_skip, o_bglu,
    act_v, ig_v, ig_f, grads_v, grads_f, small_v, gain_v, bias_v, nu_v, theta_v, skip_v, bglu_v,
    act_sem, ig_sem, grad_sem, small_sem,
):
    copy = pltpu.make_async_copy
    act_in = [copy(act.at[i], act_v.at[i], act_sem.at[i, 0]) for i in range(MICRO)]
    ig_in = [copy(ig.at[i], ig_v.at[i], ig_sem.at[i, 0]) for i in range(MICRO)]
    parts = [pl.ds(GRAD_AT[i], GRAD_ROWS[i]) for i in (GLU, OUT, IN)]
    grads_in = [copy(grads.at[parts[i]], grads_v.at[parts[i]], grad_sem.at[i, 0]) for i in (GLU, OUT, IN)]
    small_in = copy(small, small_v, small_sem.at[0])
    for one in [small_in] + ig_in + grads_in + act_in:
        one.start()
    out = []

    def leave(src, dst, sem):
        out.append(copy(src, dst, sem))
        out[-1].start()

    for i in range(MICRO):
        ig_in[i].wait()

        def tile(j, carry, i=i):
            rows = pl.ds(pl.multiple_of(j * 64, 64), 64)
            ig_f[i, rows, :] = ig_v[i, rows, :].astype(F32)
            return carry

        lax.fori_loop(0, tokens // 64, tile, 0)
        leave(ig_f.at[i], o_ig.at[i], ig_sem.at[i, 1])
    small_in.wait()
    gain_v[...] = small_v[0:1, :]
    bias_v[...] = small_v[1:2, :]
    skip_v[...] = small_v[2:3, :]
    bglu_v[:, :D] = small_v[3:4, :]
    bglu_v[:, D:] = small_v[4:5, :]
    nu_v[...] = small_v[5:6, :STATES]
    theta_v[...] = small_v[5:6, STATES:]
    small_out = ((gain_v, o_gain), (bias_v, o_bias), (nu_v, o_nu), (theta_v, o_theta), (skip_v, o_skip), (bglu_v, o_bglu))
    for i, (src, dst) in enumerate(small_out):
        leave(src, dst, small_sem.at[1 + i])
    for i, dst in ((GLU, o_glu), (OUT, o_out), (IN, o_in)):
        grads_in[i].wait()
        for c in range(GRAD_ROWS[i] // D):
            at = GRAD_AT[i] + c * D
            cols = slice(GRAD_AT[i] // 4 + c * LANES, GRAD_AT[i] // 4 + (c + 1) * LANES)
            grads_f[:, cols] = grads_v[at : at + D, :].astype(F32)
        leave(grads_f.at[:, GRAD_AT[i] // 4 : (GRAD_AT[i] + GRAD_ROWS[i]) // 4], dst, grad_sem.at[i, 1])
    for i in range(MICRO):
        act_in[i].wait()
        leave(act_v.at[i], o_act.at[i], act_sem.at[i, 1])
    for one in out:
        one.wait()


def body(ns, nd, inputs, mask, gain, bias, nu, theta, w_in, w_out, skip, w_glu, b_glu, cotangent):
    per = inputs.shape[0] // MICRO
    span = inputs.shape[1]
    tokens = per * span
    segs = tokens // SEG
    dma = pltpu.SemaphoreType.DMA
    vmem = pltpu.VMEM
    names_in = ["x", "cot", "mask", "gain", "bias", "nu", "theta", "skip", "bglu", "w_in", "w_out", "w_glu"]
    outs = {
        "act_out": jax.ShapeDtypeStruct((MICRO, tokens, D), BF16),
        "ig_out": jax.ShapeDtypeStruct((MICRO, tokens, D), BF16),
        "grads": jax.ShapeDtypeStruct((ALL_ROWS, LANES), BF16),
        "small": jax.ShapeDtypeStruct((8, D), F32),
    }
    half = ALL_ROWS // 2
    scratch = {
        "act": vmem((3, tokens, D), BF16),
        "cotv": vmem((tokens, D), BF16),
        "live": vmem((tokens, LANES), F32),
        "win": vmem((2, D, D), BF16),
        "wout": vmem((2, D, D), BF16),
        "wglu": vmem((2, D, 2 * D), BF16),
        "prm": vmem((2, 8, D), F32),
        "stat": vmem((2, 8, D), F32),
        "scaled": vmem((2, tokens, D), BF16),
        "u": vmem((2, 4, tokens, LANES), F32),
        "st": vmem((2, 4, tokens, LANES), F32),
        "start": vmem((2, 4, segs, LANES), F32),
        "readout": vmem((2, tokens, D), BF16),
        "active": vmem((2, tokens, D), BF16),
        "slope": vmem((2, tokens, D), F32),
        "gate": vmem((tokens, D), F32),
        "steep": vmem((tokens, D), F32),
        "gg": vmem((tokens, 2 * D), BF16),
        "gm": vmem((tokens, D), BF16),
        "adj": vmem((4, tokens, LANES), F32),
        "ig": vmem((tokens, D), BF16),
        "leave": vmem((2, tokens, D), BF16),
        "order": vmem((ROWS, ROWS), BF16),
        "bnb": vmem((4, ns * nd, 9, LANES), F32),
        "scb": vmem((4, ns, 4 * per, LANES), F32),
        "dw": vmem((2, ALL_ROWS, LANES), BF16),
        "sec": vmem((2, half, LANES), BF16),
        "half": vmem((2, half, LANES), BF16),
        "gat": vmem((2, half, LANES), BF16),
        "slots": vmem((slot_rows(ns, nd)[-1], LANES), BF16),
        "vec_a": vmem((2, ns, 8, D), F32),
        "vec_b": vmem((2, nd, 8, D), F32),
        "vec_tot": vmem((2, 8, D), F32),
        "vec_far": vmem((8, D), F32),
        "mask_v": vmem(mask.shape, jnp.int32),
        "nu_v": vmem((1, STATES), F32),
        "theta_v": vmem((1, STATES), F32),
        "gain_v": vmem((1, D), F32),
        "bias_v": vmem((1, D), F32),
        "skip_v": vmem((1, D), F32),
        "bglu_v": vmem((1, 2 * D), F32),
        "small_v": vmem((8, D), F32),
        "local": dma((15,)),
        "own": dma((len(FLAT),)),
        "far_send": dma((7,)),
        "far_recv": dma((7,)),
        "bn_send": dma((4,)),
        "bn_recv": dma((4,)),
        "sc_send": dma((4,)),
        "sc_recv": dma((4,)),
        "send": dma((len(FLAT),)),
        "core_recv": dma((len(FLAT),)),
        "rs_recv": dma((len(FLAT), DEPTH)),
        "ag_recv": dma((len(FLAT), DEPTH)),
        "va_send": dma((2,)),
        "va_recv": dma((2,)),
        "vb_send": dma((2,)),
        "vb_recv": dma((2,)),
    }
    in_any = pl.BlockSpec(memory_space=pl.ANY)
    names = names_in + list(outs) + list(scratch)
    act, ig, grads, small = pl.pallas_call(
        functools.partial(kernel, ns, nd, per, span, names),
        out_shape=list(outs.values()),
        in_specs=[in_any] * len(names_in),
        out_specs=[in_any] * len(outs),
        scratch_shapes=list(scratch.values()),
        compiler_params=pltpu.CompilerParams(
            collective_id=0, has_side_effects=True, vmem_limit_bytes=61 * 2**20
        ),
    )(
        inputs.reshape(MICRO, tokens, D),
        cotangent.reshape(MICRO, tokens, D),
        mask,
        gain,
        bias,
        nu,
        theta,
        skip,
        b_glu,
        w_in,
        w_out,
        w_glu,
    )

    wide_out = [(1, D), (1, D), (1, STATES), (1, STATES), (1, D), (1, 2 * D)]
    big_out = [((MICRO, tokens, D), BF16), ((MICRO, tokens, D), F32)]
    big_out += [((D, GRAD_ROWS[which] // 4), F32) for which in (GLU, OUT, IN)]
    act, ig, d_glu, d_out, d_in, d_gain, d_bias, d_nu, d_theta, d_skip, d_bglu = pl.pallas_call(
        functools.partial(results_kernel, tokens),
        out_shape=[jax.ShapeDtypeStruct(*x) for x in big_out] + [jax.ShapeDtypeStruct(x, F32) for x in wide_out],
        in_specs=[in_any] * 4,
        out_specs=[in_any] * 11,
        scratch_shapes=[
            vmem((MICRO, tokens, D), BF16),
            vmem((MICRO, tokens, D), BF16),
            vmem((MICRO, tokens, D), F32),
            vmem((ALL_ROWS, LANES), BF16),
            vmem((D, ALL_ROWS // 4), F32),
            vmem((8, D), F32),
            *[vmem(x, F32) for x in wide_out],
            dma((2, 2)),
            dma((2, 2)),
            dma((3, 2)),
            dma((7,)),
        ],
        compiler_params=pltpu.CompilerParams(vmem_limit_bytes=60 * 2**20),
    )(act, ig, grads, small)
    whole = (1, MICRO * per, span, D)
    return (
        act.reshape(whole),
        ig.reshape(whole),
        d_gain,
        d_bias,
        d_nu,
        d_theta,
        d_in[None],
        d_out[None],
        d_skip,
        d_glu[None],
        d_bglu,
    )


def solution(mesh):
    rows = P("section", None)
    cube = P("section", None, None)
    tokens = P("dp", "seq", None)
    spread = P("section", "dp", "seq", None)
    in_specs = (tokens, P("dp", "seq"), rows, rows, rows, rows, cube, cube, rows, cube, rows, tokens)
    out_specs = (spread, spread, rows, rows, rows, rows, cube, cube, rows, cube, rows)
    return jax.shard_map(
        functools.partial(body, mesh.shape["seq"], mesh.shape["dp"]),
        mesh=mesh,
        in_specs=in_specs,
        out_specs=out_specs,
        check_vma=False,
    )
```

```python
import functools
import math
import types

import jax
import jax.numpy as jnp
from jax import lax
from jax.experimental import pallas as pl
from jax.experimental.pallas import tpu as pltpu
from jax.sharding import PartitionSpec as P

D = 512
STATES = 256
MICRO = 2
EPS = 1e-05
LANES = 128
ROWS = 256
SEG = 32
EIGHT = 8
GLU, OUT, IN = 0, 1, 2
GRAD_ROWS = (4096, 2048, 2048)
GRAD_AT = (0, 4096, 6144)
ALL_ROWS = 8192
SD = ("seq", "dp")
DS = ("dp", "seq")
PARTS = (
    ((0, 2560, SD), (2560, 1536, DS),),
    ((0, 2048, SD),),
    ((0, 1536, SD), (1536, 512, DS),),
    ((0, 2048, SD), (2048, 2048, SD),),
    ((0, 2048, SD),),
    ((0, 2048, SD),),
)
FLAT = tuple((n, *part) for n, parts in enumerate(PARTS) for part in parts)
DEPTH = max(len(part[-1]) for part in FLAT)
PLAN = {
    "carry two": (104, 103, 7),
    "filled two": (),
    "norm two": (5, 105, 7, 6, 8),
    "through": (7,),
    "carry one": (200, 101, 5, 7, 6, 8, 2, 100, 5),
    "filled one": (0, 1, 8, 5),
    "norm one": (2, 102, 4, 6, 1, 3, 0, 1, 8),
    "last": (201,),
    "end": (4, 2, 6, 3, 4, 0, 2, 202, 3, 1, 203, 204, 0, 3, 4),
}
ROOT = math.sqrt(2.0 / math.pi)
CUBE = 0.044715

F32 = jnp.float32
BF16 = jnp.bfloat16
MESH = pl.DeviceIdType.MESH


def mm(a, b):
    return lax.dot_general(a, b, (((1,), (0,)), ((), ())), preferred_element_type=F32)


def mm_t(a, b):
    return lax.dot_general(a, b, (((1,), (1,)), ((), ())), preferred_element_type=F32)


def t_mm(a, b):
    return lax.dot_general(a, b, (((0,), (0,)), ((), ())), preferred_element_type=F32)


def complex_mul(ar, ai, br, bi):
    return ar * br - ai * bi, ar * bi + ai * br


def power(re, im, n):
    out = None
    while n:
        if n & 1:
            out = (re, im) if out is None else complex_mul(*out, re, im)
        n >>= 1
        if n:
            re, im = complex_mul(re, im, re, im)
    return out


def as_row(four):
    return jnp.concatenate([four[c : c + 1] for c in range(4)], axis=1)


def wide(tile):
    return jnp.concatenate([tile] * 4, axis=1)


def column_sum(x):
    return jnp.sum(x, axis=0, keepdims=True)


def slots_of(rows, counts, spread):
    out, start = [], 0
    for level, count in enumerate(counts):
        size = rows if spread and level == len(counts) - 1 else rows // count
        out.append((start, size))
        start += count * size
        rows //= count
    return out


def slot_rows(ns, nd):
    inner = next(n for n in range(math.isqrt(ns), 0, -1) if ns % n == 0)
    sizes = {"seq": ns, "dp": nd, "in": inner, "out": ns // inner}
    bases = [0]
    for _, _, rows, order in FLAT:
        counts = [sizes[name] for name in order]
        spread = rows // 2 // math.prod(counts) % 16 != 0
        start, size = slots_of(rows // 2, counts, spread)[-1]
        bases.append(bases[-1] + start + counts[-1] * size)
    return bases


def kernel(ns, nd, per, span, names, *refs):
    r = types.SimpleNamespace(**dict(zip(names, refs)))
    tokens = per * span
    segs = tokens // SEG
    nseg = span // SEG
    tiles = tokens // ROWS
    blocks = segs // EIGHT
    peers = ns * nd
    s = lax.axis_index("section")
    d = lax.axis_index("dp")
    q = lax.axis_index("seq")
    other = 1 - s
    me = d * ns + q
    sibling = {"section": other}

    def seq_peer(k):
        return {"seq": lax.rem(q + k, ns)}

    def dp_peer(k):
        return {"dp": lax.rem(d + k, nd)}

    def any_peer(k):
        at = lax.rem(me + k, peers)
        return {"dp": at // ns, "seq": lax.rem(at, ns)}

    def remote(src, dst, send, recv, device):
        return pltpu.make_async_remote_copy(
            src_ref=src, dst_ref=dst, send_sem=send, recv_sem=recv, device_id=device, device_id_type=MESH
        )

    def over(low, high, body):
        lax.fori_loop(low, high, lambda k, c: (body(k), c)[1], 0)

    arriving = {}
    leaving = {}

    def begin(key, start, whole, later=False):
        start()
        arriving[key] = whole
        if not later:
            leaving[key] = whole

    def arrive(key):
        arriving.pop(key).wait_recv()

    def leave(key):
        leaving.pop(key).wait_send()

    def end_all():
        for key in list(arriving):
            arrive(key)
        for key in list(leaving):
            leave(key)

    def alone(key, copy, later=False):
        begin(key, copy.start, copy, later)

    def row_tiles(body, init):
        def step(i, carry):
            return body(pl.ds(pl.multiple_of(i * ROWS, ROWS), ROWS), carry)

        return lax.fori_loop(0, tiles, step, init, unroll=4)

    slot_base = slot_rows(ns, nd)

    def skewed(tile, sums):
        waiting, running = [pl.ds(i * ROWS, ROWS) for i in range(tiles)], []
        while waiting or running:
            if waiting:
                running.append(tile(waiting.pop(0), sums))
            running = [one for one in running if next(one, True) is not True]
        return sums

    barrier = pltpu.get_barrier_semaphore()

    def greet(device):
        pl.semaphore_signal(barrier, inc=1, device_id=device, device_id_type=MESH)

    distant = [*range(nd - 1, 0, -2), *range(nd - 2, 0, -2), 0]
    others = [(a, b) for a in distant for b in range(ns - 1, -1, -1) if a or b]

    def each_other(body):
        if len(others) > 15:
            over(1, peers, lambda k: body(any_peer(k)))
            return
        for a, b in others:
            body({"dp": lax.rem(d + a, nd), "seq": lax.rem(q + b, ns)})

    each_other(greet)
    greet(sibling)
    over(1, ns, lambda k: greet({"section": other, **seq_peer(k)}))
    over(1, nd, lambda k: greet({"section": other, **dp_peer(k)}))

    load_x = pltpu.make_async_copy(r.x.at[s], r.act.at[0], r.local.at[0])
    load_x.start()
    load_small = [
        pltpu.make_async_copy(src, dst, r.local.at[8 + i])
        for i, (src, dst) in enumerate(
            (
                (r.mask, r.mask_v),
                (r.nu, r.nu_v),
                (r.theta, r.theta_v),
                (r.gain, r.gain_v),
                (r.bias, r.bias_v),
                (r.skip, r.skip_v),
                (r.bglu, r.bglu_v),
            )
        )
    ]
    for copy in load_small:
        copy.start()
    load_cot = pltpu.make_async_copy(r.cot.at[s], r.cotv, r.local.at[1])
    weights = ((r.w_in, r.win), (r.w_out, r.wout), (r.w_glu, r.wglu))
    load_w = [
        pltpu.make_async_copy(src.at[0], dst.at[s], r.local.at[2 + i]) for i, (src, dst) in enumerate(weights)
    ]
    for copy in load_w:
        copy.start()
    load_cot.start()
    for copy in load_small:
        copy.wait()

    rate = jnp.exp(r.nu_v[...])
    phase = jnp.exp(r.theta_v[...])
    size = jnp.exp(-rate)
    decay_re = size * jnp.cos(phase)
    decay_im = size * jnp.sin(phase)
    double = 2.0 * rate
    scale_sq = double * (
        1.0
        - double / 2.0 * (1.0 - double / 3.0 * (1.0 - double / 4.0 * (1.0 - double / 5.0 * (1.0 - double / 6.0))))
    )
    scale = jnp.sqrt(scale_sq)
    r.prm[s, 0:1, :] = r.gain_v[...]
    r.prm[s, 1:2, :] = r.bias_v[...]
    r.prm[s, 2:3, :] = r.skip_v[...]
    r.prm[s, 3:4, :] = r.bglu_v[:, :D]
    r.prm[s, 4:5, :] = r.bglu_v[:, D:]
    r.prm[s, 5:6, :] = jnp.concatenate([decay_re, decay_im], axis=1)
    r.prm[s, 6:7, :] = jnp.concatenate([scale, scale], axis=1)
    r.prm[s, 7:8, :] = jnp.zeros((1, D), F32)

    count = jnp.zeros((1, 1), F32)
    row = lax.broadcasted_iota(jnp.int32, (tokens, LANES), 0)
    token = (row & -ROWS) + (row & (EIGHT - 1)) * SEG + ((row & (ROWS - 1)) >> (EIGHT.bit_length() - 1))
    live = jnp.zeros((tokens, LANES), F32)
    for i in range(per):
        here = jnp.sum(r.mask_v[pl.ds(s * per + i, 1), :], axis=1, keepdims=True)
        live = jnp.where((token >= i * span) & (token < i * span + here), 1.0, live)
        count = count + here.astype(F32)
    r.live[...] = live
    count_row = jnp.broadcast_to(count, (1, LANES))
    to_row = lax.broadcasted_iota(jnp.int32, (ROWS, ROWS), 0)
    from_row = lax.broadcasted_iota(jnp.int32, (ROWS, ROWS), 1)
    came_from = (to_row & (EIGHT - 1)) * SEG + (to_row >> (EIGHT.bit_length() - 1))
    r.order[...] = jnp.where(from_row == came_from, 1.0, 0.0).astype(BF16)
    load_x.wait()

    def mask_input(rows, total):
        x = mm(r.order[...], r.act[0, rows, :]) * wide(r.live[rows, :])
        r.act[0, rows, :] = x.astype(BF16)
        return total + column_sum(x)

    def centred(b, mean):
        def tile(rows, total):
            off = (r.act[b, rows, :].astype(F32) - mean) * wide(r.live[rows, :])
            return total + column_sum(off * off)

        return row_tiles(tile, jnp.zeros((1, D), F32))

    def put_rows(ph, upper, lower):
        for c in range(4):
            r.bnb[ph, me, c : c + 1, :] = upper[:, c * LANES : (c + 1) * LANES]
            r.bnb[ph, me, 4 + c : 5 + c, :] = lower[:, c * LANES : (c + 1) * LANES]
        if ph == 0:
            r.bnb[ph, me, 8:9, :] = count_row

    def to_all(ph, device):
        block = r.bnb.at[ph, me] if ph == 0 else r.bnb.at[ph, me, pl.ds(0, 8)]
        return remote(block, block, r.bn_send.at[ph], r.bn_recv.at[ph], device)

    def send_all(ph):
        blocks = r.bnb.at[ph, pl.ds(0, peers - 1)]
        if ph > 0:
            blocks = r.bnb.at[ph, pl.ds(0, peers - 1), pl.ds(0, 8)]
        whole = remote(blocks, blocks, r.bn_send.at[ph], r.bn_recv.at[ph], sibling)
        begin(("all", ph), lambda: each_other(lambda device: to_all(ph, device).start()), whole)

    def wait_all(ph):
        arrive(("all", ph))

    def norm_sums(b, total):
        mean = total / jnp.maximum(wide(count_row), 1.0)
        put_rows(b, mean, centred(b, mean))

    def norm_merge(b):
        wait_all(b)
        got, counts = r.bnb[b, :, 0:8, :], r.bnb[0, :, 8:9, :]
        means, spreads = got[:, 0:4, :], got[:, 4:8, :]
        valid = jnp.sum(counts, axis=0)
        mean = jnp.sum(counts * means, axis=0) / valid
        apart = means - mean[None]
        spread = jnp.sum(spreads + counts * apart * apart, axis=0)
        r.stat[b, 0:1, :] = as_row(mean)
        r.stat[b, 1:2, :] = as_row(lax.rsqrt(spread / valid + EPS))
        r.stat[b, 2:3, :] = wide(valid)

    norm_sums(0, row_tiles(mask_input, jnp.zeros((1, D), F32)))

    pl.semaphore_wait(barrier, peers + ns - 1 + nd - 1)
    send_all(0)
    send_prm = remote(r.prm.at[s], r.prm.at[s], r.far_send.at[0], r.far_recv.at[0], sibling)
    send_w = [
        remote(src.at[0], dst.at[s], r.far_send.at[1 + i], r.far_recv.at[1 + i], sibling)
        for i, (src, dst) in enumerate(weights)
    ]

    alone("prm", send_prm)
    for i, copy in enumerate(send_w):
        alone(("w", i), copy)

    def decay(b, sign):
        out = []
        for c in range(2):
            re = r.prm[b, 5:6, c * LANES : (c + 1) * LANES]
            im = r.prm[b, 5:6, STATES + c * LANES : STATES + (c + 1) * LANES]
            out.append((re, sign * im))
        return out

    def step_rows(k, l):
        return pl.ds(pl.multiple_of(k * ROWS + l * EIGHT, EIGHT), EIGHT)

    def at_step(ref, l):
        return jnp.concatenate([ref[step_rows(k, l), :] for k in range(blocks)], axis=0)

    def put_step(ref, l, value):
        for k in range(blocks):
            ref[step_rows(k, l), :] = value[k * EIGHT : (k + 1) * EIGHT]

    def advance(a, state, drive):
        return (
            a[0] * state[0] - a[1] * state[1] + drive[0],
            a[1] * state[0] + a[0] * state[1] + drive[1],
        )

    place = lax.rem(lax.broadcasted_iota(jnp.int32, (segs, LANES), 0), nseg)
    owner = lax.broadcasted_iota(jnp.int32, (segs, LANES), 0) // nseg

    def moved(x, k, reverse):
        if reverse:
            return jnp.where(place < nseg - k, pltpu.roll(x, segs - k, 0), 0.0)
        return jnp.where(place >= k, pltpu.roll(x, k, 0), 0.0)

    def seg_scan(re, im, jump, reverse):
        k = 1
        while k < nseg:
            add_re, add_im = complex_mul(*jump, moved(re, k, reverse), moved(im, k, reverse))
            re, im = re + add_re, im + add_im
            jump = complex_mul(*jump, *jump)
            k *= 2
        return re, im

    def to_seq(ph, k):
        block = r.scb.at[ph, q]
        return remote(block, block, r.sc_send.at[ph], r.sc_recv.at[ph], seq_peer(k))

    def carry(ph, drive, a, reverse, between):
        def step(i, states):
            l = SEG - 1 - i if reverse else i
            return tuple(
                advance(a[c], states[c], (at_step(drive.at[c], l), at_step(drive.at[2 + c], l))) for c in range(2)
            )

        zero = jnp.zeros((segs, LANES), F32)
        ends = lax.fori_loop(0, SEG, step, ((zero, zero), (zero, zero)), unroll=4)
        jumps = [power(*a[c], SEG) for c in range(2)]
        sums = [seg_scan(*ends[c], jumps[c], reverse) for c in range(2)]
        for i in range(per):
            last = i * nseg if reverse else (i + 1) * nseg - 1
            for c in range(2):
                r.scb[ph, q, 4 * i + c : 4 * i + c + 1, :] = sums[c][0][last : last + 1]
                r.scb[ph, q, 4 * i + 2 + c : 4 * i + 3 + c, :] = sums[c][1][last : last + 1]
        ends_of = r.scb.at[ph, pl.ds(0, ns - 1)]
        whole = remote(ends_of, ends_of, r.sc_send.at[ph], r.sc_recv.at[ph], sibling)
        begin(("seq", ph), lambda: over(1, ns, lambda k: to_seq(ph, k).start()), whole)
        first = jnp.where(place == (nseg - 1 if reverse else 0), 1.0, 0.0)
        reach = [seg_scan(first, zero, jumps[c], reverse) for c in range(2)]
        between()
        arrive(("seq", ph))
        starts = []
        for c in range(2):
            far = power(*a[c], span)
            entering = []
            for i in range(per):
                re = jnp.zeros((1, LANES), F32)
                im = jnp.zeros((1, LANES), F32)
                for lap in range(ns):
                    j = ns - 1 - lap if reverse else lap
                    before = j > q if reverse else j < q
                    new_re, new_im = advance(
                        far,
                        (re, im),
                        (r.scb[ph, j, 4 * i + c : 4 * i + c + 1, :], r.scb[ph, j, 4 * i + 2 + c : 4 * i + 3 + c, :]),
                    )
                    re = jnp.where(before, new_re, re)
                    im = jnp.where(before, new_im, im)
                entering.append((re, im))
            in_re = jnp.broadcast_to(entering[0][0], (segs, LANES))
            in_im = jnp.broadcast_to(entering[0][1], (segs, LANES))
            for i in range(1, per):
                in_re = jnp.where(owner == i, entering[i][0], in_re)
                in_im = jnp.where(owner == i, entering[i][1], in_im)
            add_re, add_im = complex_mul(*reach[c], in_re, in_im)
            starts.append((moved(sums[c][0], 1, reverse) + add_re, moved(sums[c][1], 1, reverse) + add_im))
        return starts

    def fill_states(b, starts, a, reverse):
        for c in range(2):
            r.start[b, c] = starts[c][0]
            r.start[b, 2 + c] = starts[c][1]

        def step(i, states):
            l = SEG - 1 - i if reverse else i
            out = []
            for c in range(2):
                new = advance(a[c], states[c], (at_step(r.u.at[b, c], l), at_step(r.u.at[b, 2 + c], l)))
                put_step(r.st.at[b, c], l, new[0])
                put_step(r.st.at[b, 2 + c], l, new[1])
                out.append(new)
            return tuple(out)

        lax.fori_loop(0, SEG, step, tuple(starts), unroll=4)

    def fill_adjoint(b, starts, a, reverse):
        back = 1 if not reverse else -1
        zero = jnp.zeros((segs, LANES), F32)
        sums = []
        for c in range(2):
            scale_c = r.prm[b, 6:7, c * LANES : (c + 1) * LANES]

            def one(l, prior, carry, c=c, scale_c=scale_c):
                state, by_re, by_im, by_scale = carry
                re, im = advance(a[c], state, (at_step(r.adj.at[c], l), at_step(r.adj.at[2 + c], l)))
                put_step(r.adj.at[c], l, scale_c * re)
                put_step(r.adj.at[2 + c], l, scale_c * im)
                by_re = by_re + (re * prior[0] + im * prior[1])
                by_im = by_im + (im * prior[0] - re * prior[1])
                by_scale = by_scale + (re * at_step(r.u.at[b, c], l) + im * at_step(r.u.at[b, 2 + c], l))
                return (re, im), by_re, by_im, by_scale

            def step(i, carry, c=c, one=one):
                l = SEG - 1 - i if reverse else i
                prior = (at_step(r.st.at[b, c], l + back), at_step(r.st.at[b, 2 + c], l + back))
                return one(l, prior, carry)

            carry_c = lax.fori_loop(0, SEG - 1, step, (starts[c], zero, zero, zero), unroll=4)
            final = one(0 if reverse else SEG - 1, (r.start[b, c], r.start[b, 2 + c]), carry_c)
            sums.append([column_sum(x) for x in final[1:]])
        return [jnp.concatenate([sums[0][i], sums[1][i]], axis=1) for i in range(3)]

    def forward_in(b):
        gain, bias, scale_row = r.prm[b, 0:1, :], r.prm[b, 1:2, :], r.prm[b, 6:7, :]
        average = r.stat[b, 0:1, :]
        slope = r.stat[b, 1:2, :] * gain

        def tile(rows, _):
            x = r.act[b, rows, :].astype(F32)
            scaled = (wide(r.live[rows, :]) * ((x - average) * slope + bias)).astype(BF16)
            r.scaled[b, rows, :] = scaled
            yield
            u = mm(scaled, r.win[b])
            yield
            u = u * scale_row
            for c in range(4):
                r.u[b, c, rows, :] = u[:, c * LANES : (c + 1) * LANES]

        skewed(tile, [])

    def forward_out(b, finish, sums):
        skip = r.prm[b, 2:3, :]
        value_bias, half_gate_bias = r.prm[b, 3:4, :], 0.5 * r.prm[b, 4:5, :]

        def tile(rows, sums):
            readout = jnp.concatenate([r.st[b, c, rows, :] for c in range(4)], axis=1).astype(BF16)
            r.readout[b, rows, :] = readout
            through = mm(readout, r.wout[b])
            yield
            mixed = through + skip * r.scaled[b, rows, :].astype(F32)
            square = mixed * mixed
            t = jnp.tanh(mixed * (ROOT + (ROOT * CUBE) * square))
            half = 0.5 + 0.5 * t
            wide_active = mixed * half
            active = wide_active.astype(BF16)
            r.active[b, rows, :] = active
            r.slope[b, rows, :] = half + wide_active * ((1.0 - t) * (ROOT + (3.0 * ROOT * CUBE) * square))
            yield
            gated = mm(active, r.wglu[b])
            yield
            gate = 0.5 + 0.5 * jnp.tanh(0.5 * gated[:, D:] + half_gate_bias)
            product = (gated[:, :D] + value_bias) * gate
            live = wide(r.live[rows, :])
            result = (r.act[b, rows, :].astype(F32) + live * product).astype(BF16)
            r.act[b + 1, rows, :] = result
            yield from finish(rows, live, gate, product * (1.0 - gate), result, sums)

        return skewed(tile, sums)

    def back_tile(b, rows, outer, gate, steep, sums):
        grad_gated = jnp.concatenate([outer * gate, outer * steep], axis=1).astype(BF16)
        r.gg[rows, :] = grad_gated
        sums[1] = sums[1] + column_sum(grad_gated.astype(F32))
        yield
        grad_active = mm_t(grad_gated, r.wglu[b])
        yield
        grad_mixed = (r.slope[b, rows, :] * grad_active).astype(BF16)
        r.gm[rows, :] = grad_mixed
        sums[0] = sums[0] + column_sum(grad_mixed.astype(F32) * r.scaled[b, rows, :].astype(F32))
        yield
        grad_readout = mm_t(grad_mixed, r.wout[b])
        yield
        for c in range(4):
            r.adj[c, rows, :] = grad_readout[:, c * LANES : (c + 1) * LANES]

    def normed(b, rows):
        return (r.act[b, rows, :].astype(F32) - r.stat[b, 0:1, :]) * r.stat[b, 1:2, :]

    projected_grads = (r.cotv, r.ig)

    def round_adjoint(b):
        def tile(rows, carry):
            adjoint = jnp.concatenate([r.adj[c, rows, :] for c in range(4)], axis=1)
            projected_grads[b][rows, :] = adjoint.astype(BF16)
            return carry

        row_tiles(tile, 0)

    def back_in(b):
        skip = r.prm[b, 2:3, :]

        def tile(rows, sums):
            into = mm_t(projected_grads[b][rows, :], r.win[b])
            yield
            masked = wide(r.live[rows, :]) * (skip * r.gm[rows, :].astype(F32) + into)
            r.slope[b, rows, :] = masked
            sums[0] = sums[0] + column_sum(masked * normed(b, rows))
            sums[1] = sums[1] + column_sum(masked)

        zero = jnp.zeros((1, D), F32)
        return skewed(tile, [zero, zero])

    def back_norm(ph, b):
        wait_all(ph)
        got = jnp.sum(r.bnb[ph, :, 0:8, :], axis=0)
        gain_total, bias_total = as_row(got[0:4]), as_row(got[4:8])
        r.vec_tot[b, 0:1, :] = gain_total
        r.vec_tot[b, 1:2, :] = bias_total
        slope = r.stat[b, 1:2, :] * r.prm[b, 0:1, :]
        per_token = slope / r.stat[b, 2:3, :]
        return slope, per_token * bias_total, per_token * gain_total

    def source_grad(b, rows, upstream, live, slope, by_bias, by_gain):
        return upstream + live * (slope * r.slope[b, rows, :] - by_bias - normed(b, rows) * by_gain)

    def weight_grad(b, which, left, right):
        columns = GRAD_ROWS[which] // 4

        def tile(j, carry):
            cols = pl.ds(pl.multiple_of(j * 256, 256), 256)
            grad = t_mm(left, right[:, cols]).astype(BF16)
            at = pl.multiple_of(GRAD_AT[which] + j * 1024, 1024)
            r.dw[b, pl.ds(at, 512), :] = grad[:, :LANES]
            r.dw[b, pl.ds(at + 512, 512), :] = grad[:, LANES:]
            return carry

        lax.fori_loop(0, columns // 256, tile, 0, unroll=2)

    inner = next(n for n in range(math.isqrt(ns), 0, -1) if ns % n == 0)
    outer = ns // inner
    q_out, q_in = q // inner, lax.rem(q, inner)
    axes = {
        "seq": (ns, q, seq_peer),
        "dp": (nd, d, dp_peer),
        "in": (inner, q_in, lambda k: {"seq": q_out * inner + lax.rem(q_in + k, inner)}),
        "out": (outer, q_out, lambda k: {"seq": lax.rem(q_out + k, outer) * inner + q_in}),
    }

    results = []

    class Reduced:
        def __init__(self, n):
            which, start, rows, order = FLAT[n]
            self.b, self.n, self.at = which // 3, n, GRAD_AT[which % 3] + start
            self.base = self.at // 2
            self.axes = [axes[name] for name in order]
            self.sizes, self.offsets = [rows // 2], [0]
            for count, index, _ in self.axes:
                self.sizes.append(self.sizes[-1] // count)
                self.offsets.append(self.offsets[-1] + index * self.sizes[-1])
            self.spread = self.sizes[-1] % 16 != 0
            self.slots = slots_of(rows // 2, [count for count, _, _ in self.axes], self.spread)
            self.slot_base = slot_base[self.n]
            self.steps = self.plan()

        def rows(self, offset, size):
            return pl.ds(pl.multiple_of(self.base + offset, 16), size)

        def to_core(self):
            size = self.sizes[0]
            src = r.dw.at[self.b, pl.ds(pl.multiple_of(self.at + other * size, 16), size)]
            return remote(src, r.sec.at[self.b, self.rows(0, size)], r.send.at[self.n], r.core_recv.at[self.n], sibling)

        def slot(self, level, index):
            start, size = self.slots[level]
            return pl.ds(pl.multiple_of(self.slot_base + start + index * size, 16), size)

        def scatter(self, level, k):
            count, index, peer = self.axes[level]
            if self.spread and level == len(self.axes) - 1:
                src = r.slots.at[self.slot(level, index)]
            else:
                size = self.sizes[level + 1]
                src = r.half.at[self.b, self.rows(self.offsets[level] + lax.rem(index + k, count) * size, size)]
            dst = r.slots.at[self.slot(level, index)]
            return remote(src, dst, r.send.at[self.n], r.rs_recv.at[self.n, level], peer(k))

        def gather(self, level, k):
            block = r.gat.at[self.b, self.rows(self.offsets[level + 1], self.sizes[level + 1])]
            return remote(block, block, r.send.at[self.n], r.ag_recv.at[self.n, level], self.axes[level][2](k))

        def place(self):
            return pl.ds(pl.multiple_of(self.at + s * self.sizes[0] + self.offsets[1], 16), self.sizes[1])

        def result(self, device, send):
            src = r.gat.at[self.b, self.rows(self.offsets[1], self.sizes[1])]
            target = {"section": self.b, **device}
            return remote(src, r.grads.at[self.place()], send, r.ag_recv.at[self.n, 0], target)

        def results_whole(self, parts):
            rows = r.grads.at[pl.ds(0, parts * self.sizes[1])]
            return remote(rows, rows, r.send.at[self.n], r.ag_recv.at[self.n, 0], sibling)

        def own(self):
            src = r.gat.at[self.b, self.rows(self.offsets[1], self.sizes[1])]
            return pltpu.make_async_copy(src, r.grads.at[self.place()], r.own.at[self.n])

        def across(self):
            return self.result({}, r.own.at[self.n])

        def each(self, level, body):
            over(1, self.axes[level][0], body)

        def first(self):
            size = self.sizes[0]
            arrive((self.n, "core"))
            mine = r.dw[self.b, pl.ds(pl.multiple_of(self.at + s * size, 16), size), :].astype(F32)
            there = r.sec[self.b, self.base : self.base + size, :].astype(F32)
            r.half[self.b, self.base : self.base + size, :] = (mine + there).astype(BF16)

        def collect(self, level):
            arrive((self.n, "scatter", level))
            count, index, _ = self.axes[level]
            last = level == len(self.axes) - 1
            if self.spread and last:
                total = sum(r.slots[self.slot(level, j), :].astype(F32) for j in range(count))
                r.gat[self.b, self.rows(self.offsets[level], self.sizes[level]), :] = total.astype(BF16)
                return
            here = self.rows(self.offsets[level + 1], self.sizes[level + 1])
            total = r.half[self.b, here, :].astype(F32)
            for k in range(1, count):
                total = total + r.slots[self.slot(level, lax.rem(index + k, count)), :].astype(F32)
            (r.gat if last else r.half)[self.b, here, :] = total.astype(BF16)

        def send(self, level):
            if self.spread and level == len(self.axes) - 1:
                here = self.rows(self.offsets[level], self.sizes[level])
                r.slots[self.slot(level, self.axes[level][1]), :] = r.half[self.b, here, :]
            start, size = self.slots[level]
            rows = r.slots.at[pl.ds(self.slot_base + start, (self.axes[level][0] - 1) * size)]
            whole = remote(rows, rows, r.send.at[self.n], r.rs_recv.at[self.n, level], sibling)
            begin((self.n, "scatter", level), lambda: self.each(level, lambda k: self.scatter(level, k).start()), whole, True)

        def share(self, level):
            count, _, peer = self.axes[level]
            if level:
                rows = r.gat.at[self.b, pl.ds(self.base, (count - 1) * self.sizes[level + 1])]
                whole = remote(rows, rows, r.send.at[self.n], r.ag_recv.at[self.n, level], sibling)
                begin((self.n, "gather", level), lambda: self.each(level, lambda k: self.gather(level, k).start()), whole, True)
                return
            self.each(0, lambda k: self.result(peer(k), r.send.at[self.n]).start())

            @pl.when(s == self.b)
            def _():
                self.own().start()

            @pl.when(s != self.b)
            def _():
                self.across().start()

            results.append(self)

        def finish(self):
            count = self.axes[0][0]

            @pl.when(s == self.b)
            def _():
                self.own().wait()
                self.results_whole(2 * count - 1).wait_recv()

            @pl.when(s != self.b)
            def _():
                self.across().wait_send()

            sent = self.sizes[0] + (count - 1) * self.sizes[1]
            top = len(self.axes) - (2 if self.spread else 1)
            for level, (n, _, _) in enumerate(self.axes):
                sent += (n - 1) * self.slots[level][1]
                if 0 < level <= top:
                    sent += (n - 1) * self.sizes[level + 1]
            rows = r.dw.at[self.b, pl.ds(0, sent)]
            remote(rows, rows, r.send.at[self.n], r.core_recv.at[self.n], sibling).wait_send()

        def plan(self):
            depth = len(self.axes)
            top = depth - 2 if self.spread else depth - 1
            yield alone((self.n, "core"), self.to_core(), True)
            self.first()
            yield self.send(0)
            for level in range(1, depth):
                self.collect(level - 1)
                yield self.send(level)
            self.collect(depth - 1)
            yield self.share(top)
            for level in range(top, 0, -1):
                arrive((self.n, "gather", level))
                yield self.share(level - 1)

        def step(self):
            return next(self.steps, True)

    sums_of = [Reduced(n) for n in range(len(FLAT))]

    factors = ((r.active, (r.gg, r.gg)), (r.readout, (r.gm, r.gm)), (r.scaled, projected_grads))

    def go(gap):
        for n in PLAN[gap]:
            if n < 100:
                sums_of[n].step()
                continue
            if n >= 200:
                vec_steps[n - 200]()
                continue
            b, which = (n - 100) // 3, (n - 100) % 3
            left, right = factors[which]
            weight_grad(b, which, left[b], right[b])
            for one, part in zip(sums_of, FLAT):
                if part[0] == n - 100:
                    one.step()

    def vec_seq(b, k):
        block = r.vec_a.at[b, q]
        return remote(block, block, r.va_send.at[b], r.va_recv.at[b], seq_peer(k))

    def vec_dp(b, k):
        block = r.vec_b.at[b, d]
        return remote(block, block, r.vb_send.at[b], r.vb_recv.at[b], dp_peer(k))

    def vec_one(b, by_skip, by_bias, by_decay):
        zero = jnp.zeros((1, D), F32)
        r.vec_a[b, q, 0:1, :] = zero
        r.vec_a[b, q, 1:2, :] = zero
        r.vec_a[b, q, 2:3, :] = by_skip
        r.vec_a[b, q, 3:4, :] = by_bias[:, :D]
        r.vec_a[b, q, 4:5, :] = by_bias[:, D:]
        r.vec_a[b, q, 5:6, :] = jnp.concatenate([by_decay[0], by_decay[1]], axis=1)
        r.vec_a[b, q, 6:7, :] = jnp.concatenate([by_decay[2], by_decay[2]], axis=1)
        r.vec_a[b, q, 7:8, :] = zero
        rows = r.vec_a.at[b, pl.ds(0, ns - 1)]
        whole = remote(rows, rows, r.va_send.at[b], r.va_recv.at[b], sibling)
        begin(("vec_seq", b), lambda: over(1, ns, lambda k: vec_seq(b, k).start()), whole)

    def vec_two(b):
        arrive(("vec_seq", b))
        r.vec_b[b, d] = jnp.sum(r.vec_a[b], axis=0)
        rows = r.vec_b.at[b, pl.ds(0, nd - 1)]
        whole = remote(rows, rows, r.vb_send.at[b], r.vb_recv.at[b], sibling)
        begin(("vec_dp", b), lambda: over(1, nd, lambda k: vec_dp(b, k).start()), whole)

    def vec_three(b):
        arrive(("vec_dp", b))
        total = jnp.sum(r.vec_b[b], axis=0)
        r.vec_tot[b, 2:8, :] = total[2:8]

    def vec_last():
        vec_three(1)
        vec_three(0)
        alone("vec", remote(r.vec_tot.at[other], r.vec_far, r.far_send.at[6], r.far_recv.at[6], sibling))

    keep_small = pltpu.make_async_copy(r.small_v, r.small, r.local.at[7])

    def small_out():
        arrive("vec")
        total = r.vec_tot[s] + r.vec_far[...]
        r.small_v[0:5, :] = total[0:5]
        grad_re, grad_im = total[5:6, :STATES], total[5:6, STATES:]
        grad_rate = total[6:7, :STATES] * jnp.exp(-double) / scale_sq - (grad_re * decay_re + grad_im * decay_im)
        r.small_v[5:6, :STATES] = grad_rate * rate
        r.small_v[5:6, STATES:] = (grad_im * decay_re - grad_re * decay_im) * phase
        r.small_v[6:8, :] = jnp.zeros((2, D), F32)
        keep_small.start()

    def let_go():
        for key in [key for key in leaving if key not in arriving]:
            leave(key)

    vec_steps = (lambda: vec_two(1), lambda: vec_two(0), vec_last, small_out, let_go)

    arrive("prm")
    for i in range(3):
        load_w[i].wait()
        arrive(("w", i))
    load_cot.wait()

    def order_cot(rows, carry):
        r.cotv[rows, :] = mm(r.order[...], r.cotv[rows, :]).astype(BF16)
        return carry

    row_tiles(order_cot, 0)

    def in_time(src, dst):
        def tile(rows, carry):
            dst[rows, :] = t_mm(r.order[...], src[rows, :]).astype(BF16)
            return carry

        row_tiles(tile, 0)

    zero_row = jnp.zeros((1, D), F32)

    def nothing():
        pass

    norm_merge(0)
    forward_in(0)
    ahead0, ahead1 = decay(0, 1.0), decay(1, 1.0)
    starts = carry(0, r.u.at[0], ahead0, False, nothing)
    fill_states(0, starts, ahead0, False)

    def finish_one(rows, live, gate, steep, result, sums):
        r.gate[rows, :] = gate
        r.steep[rows, :] = steep
        sums[0] = sums[0] + column_sum(result.astype(F32))
        yield

    norm_sums(1, forward_out(0, finish_one, [zero_row])[0])
    send_all(1)
    in_time(r.act.at[1], r.leave.at[0])
    norm_merge(1)
    forward_in(1)
    starts = carry(1, r.u.at[1], ahead1, True, nothing)
    fill_states(1, starts, ahead1, True)

    def finish_two(rows, live, gate, steep, result, sums):
        return back_tile(1, rows, live * r.cotv[rows, :].astype(F32), gate, steep, sums)

    wide_zero = jnp.zeros((1, 2 * D), F32)
    by_skip, by_bias = forward_out(1, finish_two, [zero_row, wide_zero])

    keep_act = pltpu.make_async_copy(r.leave.at[s], r.act_out.at[s], r.local.at[5])
    give_act = remote(r.leave.at[other], r.act_out.at[s], r.far_send.at[4], r.far_recv.at[4], sibling)

    back0, back1 = decay(0, -1.0), decay(1, -1.0)

    def first_pieces():
        go("carry two")
        in_time(r.act.at[2], r.leave.at[1])
        keep_act.start()
        alone("act", give_act)

    starts = carry(2, r.adj, back1, False, first_pieces)
    by_decay = fill_adjoint(1, starts, back1, False)
    round_adjoint(1)
    go("filled two")
    put_rows(2, *back_in(1))
    send_all(2)
    vec_one(1, by_skip, by_bias, by_decay)
    go("norm two")
    slope, by_bias_total, by_gain_total = back_norm(2, 1)

    def through(rows, sums):
        live = wide(r.live[rows, :])
        upstream = r.cotv[rows, :].astype(F32)
        grad = source_grad(1, rows, upstream, live, slope, by_bias_total, by_gain_total).astype(BF16)
        r.ig[rows, :] = grad
        yield from back_tile(0, rows, live * grad.astype(F32), r.gate[rows, :], r.steep[rows, :], sums)

    by_skip, by_bias = skewed(through, [zero_row, wide_zero])
    go("through")

    def next_pieces():
        go("carry one")

    starts = carry(3, r.adj, back0, True, next_pieces)
    by_decay = fill_adjoint(0, starts, back0, True)
    round_adjoint(0)
    go("filled one")
    put_rows(3, *back_in(0))
    send_all(3)
    vec_one(0, by_skip, by_bias, by_decay)
    go("norm one")
    keep_act.wait()
    leave("act")
    in_time(r.ig, r.leave.at[1])
    slope0, by_bias_total0, by_gain_total0 = back_norm(3, 0)

    def last(rows, carry):
        live = wide(r.live[rows, :])
        upstream = r.ig[rows, :].astype(F32)
        grad = source_grad(0, rows, upstream, live, slope0, by_bias_total0, by_gain_total0)
        r.leave[0, rows, :] = t_mm(r.order[...], (live * grad).astype(BF16)).astype(BF16)
        return carry

    row_tiles(last, 0)
    keep_ig = pltpu.make_async_copy(r.leave.at[s], r.ig_out.at[s], r.local.at[6])
    keep_ig.start()
    give_ig = remote(r.leave.at[other], r.ig_out.at[s], r.far_send.at[5], r.far_recv.at[5], sibling)
    alone("ig", give_ig)

    go("last")
    go("end")
    while not all([one.step() is True for one in sums_of]):
        pass
    keep_ig.wait()
    keep_small.wait()
    for one in results:
        one.finish()
    end_all()


def results_kernel(
    tokens, act, ig, grads, small, o_act, o_ig, o_glu, o_out, o_in, o_gain, o_bias, o_nu, o_theta, o_skip, o_bglu,
    act_v, ig_v, ig_f, grads_v, grads_f, small_v, gain_v, bias_v, nu_v, theta_v, skip_v, bglu_v,
    act_sem, ig_sem, grad_sem, small_sem,
):
    copy = pltpu.make_async_copy
    act_in = [copy(act.at[i], act_v.at[i], act_sem.at[i, 0]) for i in range(MICRO)]
    ig_in = [copy(ig.at[i], ig_v.at[i], ig_sem.at[i, 0]) for i in range(MICRO)]
    parts = [pl.ds(GRAD_AT[i], GRAD_ROWS[i]) for i in (GLU, OUT, IN)]
    grads_in = [copy(grads.at[parts[i]], grads_v.at[parts[i]], grad_sem.at[i, 0]) for i in (GLU, OUT, IN)]
    small_in = copy(small, small_v, small_sem.at[0])
    for one in [small_in] + ig_in + grads_in + act_in:
        one.start()
    out = []

    def leave(src, dst, sem):
        out.append(copy(src, dst, sem))
        out[-1].start()

    for i in range(MICRO):
        ig_in[i].wait()

        def tile(j, carry, i=i):
            rows = pl.ds(pl.multiple_of(j * 64, 64), 64)
            ig_f[i, rows, :] = ig_v[i, rows, :].astype(F32)
            return carry

        lax.fori_loop(0, tokens // 64, tile, 0)
        leave(ig_f.at[i], o_ig.at[i], ig_sem.at[i, 1])
    small_in.wait()
    gain_v[...] = small_v[0:1, :]
    bias_v[...] = small_v[1:2, :]
    skip_v[...] = small_v[2:3, :]
    bglu_v[:, :D] = small_v[3:4, :]
    bglu_v[:, D:] = small_v[4:5, :]
    nu_v[...] = small_v[5:6, :STATES]
    theta_v[...] = small_v[5:6, STATES:]
    small_out = ((gain_v, o_gain), (bias_v, o_bias), (nu_v, o_nu), (theta_v, o_theta), (skip_v, o_skip), (bglu_v, o_bglu))
    for i, (src, dst) in enumerate(small_out):
        leave(src, dst, small_sem.at[1 + i])
    for i, dst in ((GLU, o_glu), (OUT, o_out), (IN, o_in)):
        grads_in[i].wait()
        for c in range(GRAD_ROWS[i] // D):
            at = GRAD_AT[i] + c * D
            cols = slice(GRAD_AT[i] // 4 + c * LANES, GRAD_AT[i] // 4 + (c + 1) * LANES)
            grads_f[:, cols] = grads_v[at : at + D, :].astype(F32)
        leave(grads_f.at[:, GRAD_AT[i] // 4 : (GRAD_AT[i] + GRAD_ROWS[i]) // 4], dst, grad_sem.at[i, 1])
    for i in range(MICRO):
        act_in[i].wait()
        leave(act_v.at[i], o_act.at[i], act_sem.at[i, 1])
    for one in out:
        one.wait()


def body(ns, nd, inputs, mask, gain, bias, nu, theta, w_in, w_out, skip, w_glu, b_glu, cotangent):
    per = inputs.shape[0] // MICRO
    span = inputs.shape[1]
    tokens = per * span
    segs = tokens // SEG
    dma = pltpu.SemaphoreType.DMA
    vmem = pltpu.VMEM
    names_in = ["x", "cot", "mask", "gain", "bias", "nu", "theta", "skip", "bglu", "w_in", "w_out", "w_glu"]
    outs = {
        "act_out": jax.ShapeDtypeStruct((MICRO, tokens, D), BF16),
        "ig_out": jax.ShapeDtypeStruct((MICRO, tokens, D), BF16),
        "grads": jax.ShapeDtypeStruct((ALL_ROWS, LANES), BF16),
        "small": jax.ShapeDtypeStruct((8, D), F32),
    }
    half = ALL_ROWS // 2
    scratch = {
        "act": vmem((3, tokens, D), BF16),
        "cotv": vmem((tokens, D), BF16),
        "live": vmem((tokens, LANES), F32),
        "win": vmem((2, D, D), BF16),
        "wout": vmem((2, D, D), BF16),
        "wglu": vmem((2, D, 2 * D), BF16),
        "prm": vmem((2, 8, D), F32),
        "stat": vmem((2, 8, D), F32),
        "scaled": vmem((2, tokens, D), BF16),
        "u": vmem((2, 4, tokens, LANES), F32),
        "st": vmem((2, 4, tokens, LANES), F32),
        "start": vmem((2, 4, segs, LANES), F32),
        "readout": vmem((2, tokens, D), BF16),
        "active": vmem((2, tokens, D), BF16),
        "slope": vmem((2, tokens, D), F32),
        "gate": vmem((tokens, D), F32),
        "steep": vmem((tokens, D), F32),
        "gg": vmem((tokens, 2 * D), BF16),
        "gm": vmem((tokens, D), BF16),
        "adj": vmem((4, tokens, LANES), F32),
        "ig": vmem((tokens, D), BF16),
        "leave": vmem((2, tokens, D), BF16),
        "order": vmem((ROWS, ROWS), BF16),
        "bnb": vmem((4, ns * nd, 9, LANES), F32),
        "scb": vmem((4, ns, 4 * per, LANES), F32),
        "dw": vmem((2, ALL_ROWS, LANES), BF16),
        "sec": vmem((2, half, LANES), BF16),
        "half": vmem((2, half, LANES), BF16),
        "gat": vmem((2, half, LANES), BF16),
        "slots": vmem((slot_rows(ns, nd)[-1], LANES), BF16),
        "vec_a": vmem((2, ns, 8, D), F32),
        "vec_b": vmem((2, nd, 8, D), F32),
        "vec_tot": vmem((2, 8, D), F32),
        "vec_far": vmem((8, D), F32),
        "mask_v": vmem(mask.shape, jnp.int32),
        "nu_v": vmem((1, STATES), F32),
        "theta_v": vmem((1, STATES), F32),
        "gain_v": vmem((1, D), F32),
        "bias_v": vmem((1, D), F32),
        "skip_v": vmem((1, D), F32),
        "bglu_v": vmem((1, 2 * D), F32),
        "small_v": vmem((8, D), F32),
        "local": dma((15,)),
        "own": dma((len(FLAT),)),
        "far_send": dma((7,)),
        "far_recv": dma((7,)),
        "bn_send": dma((4,)),
        "bn_recv": dma((4,)),
        "sc_send": dma((4,)),
        "sc_recv": dma((4,)),
        "send": dma((len(FLAT),)),
        "core_recv": dma((len(FLAT),)),
        "rs_recv": dma((len(FLAT), DEPTH)),
        "ag_recv": dma((len(FLAT), DEPTH)),
        "va_send": dma((2,)),
        "va_recv": dma((2,)),
        "vb_send": dma((2,)),
        "vb_recv": dma((2,)),
    }
    in_any = pl.BlockSpec(memory_space=pl.ANY)
    names = names_in + list(outs) + list(scratch)
    act, ig, grads, small = pl.pallas_call(
        functools.partial(kernel, ns, nd, per, span, names),
        out_shape=list(outs.values()),
        in_specs=[in_any] * len(names_in),
        out_specs=[in_any] * len(outs),
        scratch_shapes=list(scratch.values()),
        compiler_params=pltpu.CompilerParams(
            collective_id=0, has_side_effects=True, vmem_limit_bytes=61 * 2**20
        ),
    )(
        inputs.reshape(MICRO, tokens, D),
        cotangent.reshape(MICRO, tokens, D),
        mask,
        gain,
        bias,
        nu,
        theta,
        skip,
        b_glu,
        w_in,
        w_out,
        w_glu,
    )

    wide_out = [(1, D), (1, D), (1, STATES), (1, STATES), (1, D), (1, 2 * D)]
    big_out = [((MICRO, tokens, D), BF16), ((MICRO, tokens, D), F32)]
    big_out += [((D, GRAD_ROWS[which] // 4), F32) for which in (GLU, OUT, IN)]
    act, ig, d_glu, d_out, d_in, d_gain, d_bias, d_nu, d_theta, d_skip, d_bglu = pl.pallas_call(
        functools.partial(results_kernel, tokens),
        out_shape=[jax.ShapeDtypeStruct(*x) for x in big_out] + [jax.ShapeDtypeStruct(x, F32) for x in wide_out],
        in_specs=[in_any] * 4,
        out_specs=[in_any] * 11,
        scratch_shapes=[
            vmem((MICRO, tokens, D), BF16),
            vmem((MICRO, tokens, D), BF16),
            vmem((MICRO, tokens, D), F32),
            vmem((ALL_ROWS, LANES), BF16),
            vmem((D, ALL_ROWS // 4), F32),
            vmem((8, D), F32),
            *[vmem(x, F32) for x in wide_out],
            dma((2, 2)),
            dma((2, 2)),
            dma((3, 2)),
            dma((7,)),
        ],
        compiler_params=pltpu.CompilerParams(vmem_limit_bytes=60 * 2**20),
    )(act, ig, grads, small)
    whole = (1, MICRO * per, span, D)
    return (
        act.reshape(whole),
        ig.reshape(whole),
        d_gain,
        d_bias,
        d_nu,
        d_theta,
        d_in[None],
        d_out[None],
        d_skip,
        d_glu[None],
        d_bglu,
    )


def solution(mesh):
    rows = P("section", None)
    cube = P("section", None, None)
    tokens = P("dp", "seq", None)
    spread = P("section", "dp", "seq", None)
    in_specs = (tokens, P("dp", "seq"), rows, rows, rows, rows, cube, cube, rows, cube, rows, tokens)
    out_specs = (spread, spread, rows, rows, rows, rows, cube, cube, rows, cube, rows)
    return jax.shard_map(
        functools.partial(body, mesh.shape["seq"], mesh.shape["dp"]),
        mesh=mesh,
        in_specs=in_specs,
        out_specs=out_specs,
        check_vma=False,
    )
```
